256 devices in a mesh: frame: 64 (over z, y, x_lo), row: 4 (over x_hi, core).
Axes of the slice: x: 4 (x_hi: 2, x_lo: 2; x = x_hi * 2 + x_lo), y: 4, z: 8, core: 2. Of those that a mesh axis runs over, the one named last changes fastest.
Arguments:
- video: bfloat16 [64, 512, 1152], P('frame', 'row'), may hold values from -6 to 6
- modulation: float32 [2, 6, 1152], replicated, may hold values from -3 to 3
- query_key_value_weight: bfloat16 [2, 1152, 3, 1152], P(None, 'frame', None, 'row'), may hold values from -8 to 8
- attention_output_weight: bfloat16 [2, 1152, 1152], P(None, 'row', 'frame'), may hold values from -0.1875 to 0.1875
- feed_forward_up_weight: bfloat16 [2, 1152, 4608], P(None, 'frame', 'row'), may hold values from -0.1875 to 0.1875
- feed_forward_down_weight: bfloat16 [2, 4608, 1152], P(None, 'row', 'frame'), may hold values from -0.09375 to 0.09375
Outputs:
- denoised: bfloat16 [64, 512, 1152], P('frame', 'row')
The draws below stay inside these ranges and needn't reach their ends.
All inputs are finite; a program needn't handle non-finite values.
Results may differ from the reference program's by a relative error of at most 0.013.
Values may be sent and summed in bfloat16 or wider, within the bound.
No kernel may reach another device: no remote copies, remote signals or barrier semaphores. Data moves between devices by JAX's collectives and lax.ppermute only.
A program may use at most 64 MiB of HBM per device.

```python
import math
import jax
import jax.numpy as jnp
from jax import lax

D = 1152
HEADS = 16
FF = 4608
PATCHES = 512
FRAMES = 64


def draw_query_key_value_weight(key, part):
    key = jax.random.fold_in(key, 7)
    base = jax.random.normal(key, (2, D, 3, D), jnp.float32) / math.sqrt(D)
    query_cols = base[:, :, 0, :]
    key_cols = base[:, :, 1, :]
    value_cols = base[:, :, 2, :]
    full = jnp.stack([query_cols, key_cols, value_cols], axis=2)
    return jnp.clip(full, -8.0, 8.0).astype(jnp.bfloat16)


def block_scale(rng, shape, shards, smallest, largest):
    gain = 1.0
    for dim, blocks in shards:
        heights = jax.random.uniform(jax.random.fold_in(jax.random.fold_in(rng, 6), dim), (blocks,), jnp.float32, smallest / len(shards), largest / len(shards))
        gain = gain * jnp.repeat(jnp.exp(heights), shape[dim] // blocks).reshape((-1,) + (1,) * (len(shape) - 1 - dim))
    return gain


def centred(key, shape, scale, most, shards=(), held_as=jnp.bfloat16):
    level = block_scale(key, shape, shards, -0.22, 0.18) if shards else 1.0
    values = jax.random.normal(key, shape, jnp.float32) * scale * level
    return jnp.minimum(jnp.maximum(values, -most), most).astype(held_as)


def setup_inputs(seed: int = 0) -> dict:
    keys = jax.random.split(jax.random.key(seed), 7)
    video = centred(keys[0], (FRAMES, PATCHES, D), 1.0, 6.0, ((0, 64), (1, 4)))
    modulation = centred(keys[1], (2, 6, D), 0.5, 3.0, (), jnp.float32)
    query_key_value_weight = draw_query_key_value_weight(jax.random.fold_in(keys[6], 71), 0)
    attention_output_weight = centred(keys[3], (2, D, D), D ** -0.5, 0.1875, ((1, 4), (2, 64)))
    feed_forward_up_weight = centred(keys[4], (2, D, FF), D ** -0.5, 0.1875, ((1, 64), (2, 4)))
    feed_forward_down_weight = centred(keys[5], (2, FF, D), FF ** -0.5, 0.09375, ((1, 4), (2, 64)))
    return {"video": video, "modulation": modulation, "query_key_value_weight": query_key_value_weight, "attention_output_weight": attention_output_weight, "feed_forward_up_weight": feed_forward_up_weight, "feed_forward_down_weight": feed_forward_down_weight}


epsilon = 1e-06

def normalize(token_sequence, shift, scale):
    values = token_sequence.astype(jnp.float32)
    center = values - lax.optimization_barrier(jnp.mean(values, axis=-1, keepdims=True))
    spread = lax.optimization_barrier(jnp.mean(center * center, axis=-1, keepdims=True))
    return (center * lax.rsqrt(spread + epsilon) * (1.0 + scale) + shift).astype(jnp.bfloat16)

def attend(query_part, key_part, value_part):
    head_size = query_part.shape[-1]
    scores = jnp.einsum('blhd,bmhd->bhlm', query_part.astype(jnp.float32), key_part.astype(jnp.float32)) * head_size ** (-0.5)
    scores = scores - lax.optimization_barrier(jnp.max(scores, axis=-1, keepdims=True))
    raised = jnp.exp(scores)
    probs = (raised / lax.optimization_barrier(jnp.sum(raised, axis=-1, keepdims=True))).astype(jnp.bfloat16)
    return jnp.einsum('bhlm,bmhd->blhd', probs.astype(jnp.float32), value_part.astype(jnp.float32)).astype(jnp.bfloat16)

def diffusion_transformer_block(token_sequence, modulation, query_key_value_matrix, output_projection_matrix, leading_block, trailing_block):
    batch, length, width = token_sequence.shape
    head_size = width // HEADS
    normed = normalize(token_sequence, modulation[0], modulation[1]).reshape(-1, width)
    packed = jnp.dot(normed, query_key_value_matrix.reshape(width, 3 * width), preferred_element_type=jnp.float32).astype(jnp.bfloat16)
    triple = packed.reshape(batch, length, 3, HEADS, head_size)
    mixed = attend(triple[:, :, 0], triple[:, :, 1], triple[:, :, 2]).reshape(-1, width)
    update = jnp.dot(mixed, output_projection_matrix, preferred_element_type=jnp.float32)
    flat = token_sequence.reshape(-1, width)
    attended = (flat.astype(jnp.float32) + modulation[2] * update).astype(jnp.bfloat16)
    normed_two = normalize(attended, modulation[3], modulation[4])
    hidden = jnp.dot(normed_two, leading_block, preferred_element_type=jnp.float32)
    activated = jax.nn.gelu(hidden, approximate=True).astype(jnp.bfloat16)
    update_two = jnp.dot(activated, trailing_block, preferred_element_type=jnp.float32)
    result = (attended.astype(jnp.float32) + modulation[5] * update_two).astype(jnp.bfloat16)
    return result.reshape(batch, length, width)

def reference(video, modulation, query_key_value_weight, attention_output_weight, feed_forward_up_weight, feed_forward_down_weight):

    def spatial(per_frame_tokens):
        return diffusion_transformer_block(per_frame_tokens[None], modulation[0], query_key_value_weight[0], attention_output_weight[0], feed_forward_up_weight[0], feed_forward_down_weight[0])[0]
    token_sequence = lax.map(spatial, video)
    frames, patches, width = token_sequence.shape
    across = jnp.swapaxes(token_sequence, 0, 1).reshape(patches // 16, 16, frames, width)

    def temporal(token_grouping):
        return diffusion_transformer_block(token_grouping, modulation[1], query_key_value_weight[1], attention_output_weight[1], feed_forward_up_weight[1], feed_forward_down_weight[1])
    done = lax.map(temporal, across).reshape(patches, frames, width)
    return jnp.swapaxes(done, 0, 1)
```

```python
import jax
import jax.numpy as jnp
from jax import lax
from jax.sharding import Mesh, PartitionSpec as P

HEADS = 16
EPSILON = 1e-06
LINE = ("xl", "xh", "c")
RING = ("xl", "xh")
PLANE = ("z", "y")
FRAME = ("z", "y", "xl")


def normalize(token_sequence, shift, scale):
    values = token_sequence.astype(jnp.float32)
    center = values - jnp.mean(values, axis=-1, keepdims=True)
    spread = jnp.mean(center * center, axis=-1, keepdims=True)
    return (center * lax.rsqrt(spread + EPSILON) * (1.0 + scale) + shift).astype(jnp.bfloat16)


def attend(query_part, key_part, value_part):
    head_size = query_part.shape[-1]
    scores = jnp.einsum(
        "blhd,bmhd->bhlm", query_part, key_part, preferred_element_type=jnp.float32
    ) * head_size ** (-0.5)
    scores = scores - jnp.max(scores, axis=-1, keepdims=True)
    raised = jnp.exp(scores)
    probs = (raised / jnp.sum(raised, axis=-1, keepdims=True)).astype(jnp.bfloat16)
    return jnp.einsum(
        "bhlm,bmhd->blhd", probs, value_part, preferred_element_type=jnp.float32
    ).astype(jnp.bfloat16)


def exchange(blocks, axes):
    return lax.all_to_all(blocks, axes, split_axis=0, concat_axis=0, tiled=True)


def spread_out(block, axes):
    count = lax.axis_size(axes)
    return exchange(jnp.broadcast_to(block[None], (count,) + block.shape), axes)


def times(tokens, weight):
    return jnp.dot(tokens, weight, preferred_element_type=jnp.float32)


def times_transposed(tokens, weight):
    return lax.dot_general(
        tokens, weight, (((1,), (1,)), ((), ())), preferred_element_type=jnp.float32
    )


def gather_line(normed):
    chips = spread_out(normed, RING)
    cores = spread_out(chips, ("c",))
    own, width = normed.shape
    cores = cores.reshape(2, 2, 2, own, width)
    return jnp.transpose(cores, (1, 2, 0, 3, 4)).reshape(-1, width)


def scatter_line(partial, own):
    width = partial.shape[-1]
    blocks = partial.astype(jnp.bfloat16).reshape(2, 2, 2, own, width)
    blocks = jnp.transpose(blocks, (2, 0, 1, 3, 4)).reshape(2, 4 * own, width)
    half = jnp.sum(exchange(blocks, ("c",)).astype(jnp.float32), axis=0).astype(jnp.bfloat16)
    quarter = exchange(half.reshape(4, own, width), RING)
    return jnp.sum(quarter.astype(jnp.float32), axis=0)


def gather_pair(normed):
    return spread_out(normed, ("c",)).reshape(-1, normed.shape[-1])


def scatter_pair(partial, own):
    width = partial.shape[-1]
    return jnp.sum(exchange(partial.reshape(2, own, width), ("c",)), axis=0)


def on_device(
    video,
    modulation,
    query_key_value_weight,
    attention_output_weight,
    feed_forward_up_weight,
    feed_forward_down_weight,
):
    stream = video[0]
    own, width = stream.shape
    head_size = width // HEADS
    depth, _, quarter = query_key_value_weight.shape[1:]
    hidden = feed_forward_up_weight.shape[2]
    output_rows = jnp.swapaxes(attention_output_weight, 1, 2)
    down_rows = jnp.swapaxes(feed_forward_down_weight, 1, 2)

    def halves(rows):
        return jnp.swapaxes(rows.reshape(depth, 2, -1), 0, 1)

    qkv = query_key_value_weight[0].reshape(depth, 3, 2, quarter // 2)
    qkv = jnp.transpose(qkv, (2, 0, 1, 3)).reshape(2, depth, -1)
    packs = jnp.concatenate(
        [qkv, halves(output_rows[0]), halves(feed_forward_up_weight[0]), halves(down_rows[0])], axis=2
    )
    packs = exchange(packs, ("xl",)).reshape(2 * depth, -1)
    first = 2 * quarter
    attention_pack = spread_out(packs[:, :first], PLANE).reshape(width, first)
    feed_pack = lax.all_gather(packs[:, first:], PLANE, axis=0, tiled=True)

    pack = jnp.concatenate(
        [
            query_key_value_weight[1].reshape(depth, -1),
            output_rows[1],
            feed_forward_up_weight[1],
            down_rows[1],
        ],
        axis=1,
    )
    pack = spread_out(pack, RING).reshape(2, 2, depth, -1)
    pack = jnp.swapaxes(pack, 1, 2).reshape(2 * depth, 2, -1)
    own_qkv = pack[:, :, : 3 * quarter].reshape(-1, 2, 3, quarter)
    rest = pack[:, :, 3 * quarter :]
    pack = jnp.concatenate(
        [
            jnp.swapaxes(own_qkv, 1, 2).reshape(2 * depth, -1),
            rest[:, :, :quarter].reshape(2 * depth, -1),
            rest[:, :, quarter : quarter + hidden].reshape(2 * depth, -1),
            rest[:, :, quarter + hidden :].reshape(2 * depth, -1),
        ],
        axis=1,
    )
    temporal_pack = lax.all_gather(pack, PLANE, axis=0, tiled=True)

    mod = modulation[0]
    local = quarter // 2
    normed = gather_line(normalize(stream, mod[0], mod[1]))
    packed = times(normed, attention_pack[:, : 3 * local]).astype(jnp.bfloat16)
    triple = packed.reshape(2, -1, 3, local // head_size, head_size)
    mixed = attend(triple[:, :, 0], triple[:, :, 1], triple[:, :, 2]).reshape(-1, local)
    update = scatter_line(times_transposed(mixed, attention_pack[:, 3 * local :]), own)
    stream = (stream.astype(jnp.float32) + mod[2] * update).astype(jnp.bfloat16)
    normed = gather_line(normalize(stream, mod[3], mod[4]))
    activated = jax.nn.gelu(times(normed, feed_pack[:, : hidden // 2]), approximate=True).astype(
        jnp.bfloat16
    )
    update = scatter_line(times_transposed(activated, feed_pack[:, hidden // 2 :]), own)
    stream = (stream.astype(jnp.float32) + mod[5] * update).astype(jnp.bfloat16)

    frames = lax.axis_size(FRAME)
    stream = exchange(stream.reshape(frames, own // frames, width), FRAME).reshape(own, width)
    mod = modulation[1]
    local = 2 * quarter
    normed = gather_pair(normalize(stream, mod[0], mod[1]))
    packed = times(normed, temporal_pack[:, : 3 * local]).astype(jnp.bfloat16)
    triple = packed.reshape(2, frames, own // frames, 3, local // head_size, head_size)
    triple = jnp.swapaxes(triple, 1, 2).reshape(-1, frames, 3, local // head_size, head_size)
    mixed = attend(triple[:, :, 0], triple[:, :, 1], triple[:, :, 2])
    mixed = jnp.swapaxes(mixed.reshape(2, own // frames, frames, local), 1, 2).reshape(-1, local)
    update = scatter_pair(times_transposed(mixed, temporal_pack[:, 3 * local : 4 * local]), own)
    stream = (stream.astype(jnp.float32) + mod[2] * update).astype(jnp.bfloat16)
    normed = gather_pair(normalize(stream, mod[3], mod[4]))
    start = 4 * local
    activated = jax.nn.gelu(
        times(normed, temporal_pack[:, start : start + 2 * hidden]), approximate=True
    ).astype(jnp.bfloat16)
    update = scatter_pair(times_transposed(activated, temporal_pack[:, start + 2 * hidden :]), own)
    stream = (stream.astype(jnp.float32) + mod[5] * update).astype(jnp.bfloat16)
    stream = exchange(stream.reshape(frames, own // frames, width), FRAME)
    return stream.reshape(1, own, width)


def solution(mesh):
    fine = Mesh(mesh.devices.reshape(8, 4, 2, 2, 2), ("z", "y", "xl", "xh", "c"))
    rows = ("xh", "c")
    in_specs = (
        P(FRAME, rows, None),
        P(),
        P(None, FRAME, None, rows),
        P(None, rows, FRAME),
        P(None, FRAME, rows),
        P(None, rows, FRAME),
    )
    out_specs = P(FRAME, rows, None)
    return jax.shard_map(
        on_device, mesh=fine, in_specs=in_specs, out_specs=out_specs, check_vma=False
    )
```

```python
import jax
import jax.numpy as jnp
import numpy as np
from jax import lax
from jax.sharding import Mesh, PartitionSpec as P

HEADS = 16
EPSILON = 1e-06
LINE = ("xl", "xh", "c")
RING = ("xl", "xh")
PLANE = ("zh", "zl", "y")
FRAME = ("zh", "zl", "y", "xl")


def normalize(token_sequence, shift, scale):
    values = token_sequence.astype(jnp.float32)
    center = values - jnp.mean(values, axis=-1, keepdims=True)
    spread = jnp.mean(center * center, axis=-1, keepdims=True)
    return (center * lax.rsqrt(spread + EPSILON) * (1.0 + scale) + shift).astype(jnp.bfloat16)


def attend(query_part, key_part, value_part):
    head_size = query_part.shape[-1]
    scores = jnp.einsum(
        "blhd,bmhd->bhlm", query_part, key_part, preferred_element_type=jnp.float32
    ) * head_size ** (-0.5)
    scores = scores - jnp.max(scores, axis=-1, keepdims=True)
    raised = jnp.exp(scores)
    probs = (raised / jnp.sum(raised, axis=-1, keepdims=True)).astype(jnp.bfloat16)
    return jnp.einsum(
        "bhlm,bmhd->blhd", probs, value_part, preferred_element_type=jnp.float32
    ).astype(jnp.bfloat16)


def exchange(blocks, axes):
    return lax.all_to_all(blocks, axes, split_axis=0, concat_axis=0, tiled=True)


def spread_out(block, axes):
    count = lax.axis_size(axes)
    return exchange(jnp.broadcast_to(block[None], (count,) + block.shape), axes)


def times(tokens, weight):
    return jnp.dot(tokens, weight, preferred_element_type=jnp.float32)


def times_transposed(tokens, weight):
    return lax.dot_general(
        tokens, weight, (((1,), (1,)), ((), ())), preferred_element_type=jnp.float32
    )


def gather_line(normed):
    chips = spread_out(normed, RING)
    cores = spread_out(chips, ("c",))
    own, width = normed.shape
    cores = cores.reshape(2, 2, 2, own, width)
    return jnp.transpose(cores, (1, 2, 0, 3, 4)).reshape(-1, width)


def scatter_line(partial, own):
    width = partial.shape[-1]
    blocks = partial.astype(jnp.bfloat16).reshape(2, 2, 2, own, width)
    blocks = jnp.transpose(blocks, (2, 0, 1, 3, 4)).reshape(2, 4 * own, width)
    half = jnp.sum(exchange(blocks, ("c",)).astype(jnp.float32), axis=0).astype(jnp.bfloat16)
    quarter = exchange(half.reshape(4, own, width), RING)
    return jnp.sum(quarter.astype(jnp.float32), axis=0)


def gather_pair(normed):
    return spread_out(normed, ("c",)).reshape(-1, normed.shape[-1])


def scatter_pair(partial, own):
    width = partial.shape[-1]
    return jnp.sum(exchange(partial.reshape(2, own, width), ("c",)), axis=0)


def on_device(
    video,
    modulation,
    query_key_value_weight,
    attention_output_weight,
    feed_forward_up_weight,
    feed_forward_down_weight,
):
    stream = video[0]
    own, width = stream.shape
    head_size = width // HEADS
    depth, _, quarter = query_key_value_weight.shape[1:]
    hidden = feed_forward_up_weight.shape[2]
    order = np.arange(width).reshape(2, 16, -1).swapaxes(0, 1).reshape(-1)
    inner = jnp.asarray(np.eye(width)[:, order], jnp.bfloat16)
    stream = times(stream, inner).astype(jnp.bfloat16)
    modulation = jnp.swapaxes(modulation.reshape(2, 6, 2, 16, -1), 2, 3).reshape(2, 6, width)
    output_rows = jnp.swapaxes(attention_output_weight, 1, 2)
    down_rows = jnp.swapaxes(feed_forward_down_weight, 1, 2)

    def halves(rows):
        return jnp.swapaxes(rows.reshape(depth, 2, -1), 0, 1)

    def split_qkv(weight):
        parts = weight.reshape(depth, 3, 2, quarter // 2)
        return jnp.transpose(parts, (2, 0, 1, 3)).reshape(2, depth, -1)

    def spread_plane(packs):
        columns = packs.shape[-1]
        lines = lax.axis_size(("zh", "zl"))
        packs = jnp.broadcast_to(packs[None], (lines,) + packs.shape)
        packs = exchange(packs.reshape(2 * lines, depth, columns), ("zh", "zl", "xl"))
        packs = spread_out(packs.reshape(-1, columns), ("y",))
        packs = packs.reshape(4, 2, 4, 2 * depth, columns)
        return jnp.transpose(packs, (2, 0, 1, 3, 4)).reshape(width, columns)

    attention_pack = spread_plane(
        jnp.concatenate([split_qkv(query_key_value_weight[0]), halves(output_rows[0])], axis=2)
    )

    pack = jnp.concatenate(
        [
            halves(feed_forward_up_weight[1]),
            halves(down_rows[1]),
            split_qkv(query_key_value_weight[1]),
            halves(output_rows[1]),
        ],
        axis=2,
    )
    pack = jnp.broadcast_to(pack[:, None], (2, 4) + pack.shape[1:]).reshape(8, depth, -1)
    pack = exchange(pack, ("zh", "xl", "xh")).reshape(4, 2, depth, -1)
    pack = jnp.transpose(pack, (0, 2, 1, 3)).reshape(4 * depth, 2, -1)
    half_hidden = hidden // 2
    half = quarter // 2
    qkv_start = 2 * half_hidden
    qkv = pack[:, :, qkv_start : qkv_start + 3 * half].reshape(-1, 2, 3, half)
    pack = jnp.concatenate(
        [
            pack[:, :, :half_hidden].reshape(4 * depth, -1),
            pack[:, :, half_hidden:qkv_start].reshape(4 * depth, -1),
            jnp.swapaxes(qkv, 1, 2).reshape(4 * depth, -1),
            pack[:, :, qkv_start + 3 * half :].reshape(4 * depth, -1),
        ],
        axis=1,
    )
    temporal_packs = lax.all_gather(pack, PLANE, axis=0).reshape(2, width, -1)

    feed_pack = spread_plane(
        jnp.concatenate([halves(feed_forward_up_weight[0]), halves(down_rows[0])], axis=2)
    )

    mod = modulation[0]
    local = quarter // 2
    normed = gather_line(normalize(stream, mod[0], mod[1]))
    packed = times(normed, attention_pack[:, : 3 * local]).astype(jnp.bfloat16)
    triple = packed.reshape(2, -1, 3, local // head_size, head_size)
    mixed = attend(triple[:, :, 0], triple[:, :, 1], triple[:, :, 2]).reshape(-1, local)
    update = scatter_line(times_transposed(mixed, attention_pack[:, 3 * local :]), own)
    stream = (stream.astype(jnp.float32) + mod[2] * update).astype(jnp.bfloat16)
    normed = gather_line(normalize(stream, mod[3], mod[4]))
    activated = jax.nn.gelu(times(normed, feed_pack[:, : hidden // 2]), approximate=True).astype(
        jnp.bfloat16
    )
    update = scatter_line(times_transposed(activated, feed_pack[:, hidden // 2 :]), own)
    stream = (stream.astype(jnp.float32) + mod[5] * update).astype(jnp.bfloat16)

    frames = lax.axis_size(FRAME)
    stream = exchange(stream.reshape(frames, own // frames, width), FRAME).reshape(own, width)
    mod = modulation[1]
    local = quarter
    heads = local // head_size
    normed = gather_pair(normalize(stream, mod[0], mod[1]))
    update = 0.0
    for group in range(2):
        weights = temporal_packs[group][:, 2 * hidden :]
        packed = times(normed, weights[:, : 3 * local]).astype(jnp.bfloat16)
        triple = packed.reshape(2, frames, own // frames, 3, heads, head_size)
        triple = jnp.swapaxes(triple, 1, 2).reshape(-1, frames, 3, heads, head_size)
        mixed = attend(triple[:, :, 0], triple[:, :, 1], triple[:, :, 2])
        mixed = jnp.swapaxes(mixed.reshape(2, own // frames, frames, local), 1, 2)
        update += times_transposed(mixed.reshape(-1, local), weights[:, 3 * local :])
    stream = (stream.astype(jnp.float32) + mod[2] * scatter_pair(update, own)).astype(jnp.bfloat16)
    normed = gather_pair(normalize(stream, mod[3], mod[4]))
    update = 0.0
    for group in range(2):
        weights = temporal_packs[group][:, : 2 * hidden]
        activated = jax.nn.gelu(times(normed, weights[:, :hidden]), approximate=True)
        update += times_transposed(activated.astype(jnp.bfloat16), weights[:, hidden:])
    stream = (stream.astype(jnp.float32) + mod[5] * scatter_pair(update, own)).astype(jnp.bfloat16)
    stream = times_transposed(stream, inner).astype(jnp.bfloat16)
    stream = exchange(stream.reshape(frames, own // frames, width), FRAME)
    return stream.reshape(1, own, width)


def solution(mesh):
    fine = Mesh(mesh.devices.reshape(2, 4, 4, 2, 2, 2), ("zh", "zl", "y", "xl", "xh", "c"))
    rows = ("xh", "c")
    in_specs = (
        P(FRAME, rows, None),
        P(),
        P(None, FRAME, None, rows),
        P(None, rows, FRAME),
        P(None, FRAME, rows),
        P(None, rows, FRAME),
    )
    out_specs = P(FRAME, rows, None)
    return jax.shard_map(
        on_device, mesh=fine, in_specs=in_specs, out_specs=out_specs, check_vma=False
    )
```

```python
import jax
import jax.numpy as jnp
from jax import lax
from jax.sharding import Mesh, PartitionSpec as P

HEADS = 16
EPSILON = 1e-06
LINE = ("xl", "xh", "c")
RING = ("xl", "xh")
PLANE = ("z", "y")
FRAME = ("z", "y", "xl")


def normalize(token_sequence, shift, scale):
    values = token_sequence.astype(jnp.float32)
    center = values - jnp.mean(values, axis=-1, keepdims=True)
    spread = jnp.mean(center * center, axis=-1, keepdims=True)
    return (center * lax.rsqrt(spread + EPSILON) * (1.0 + scale) + shift).astype(jnp.bfloat16)


def attend(query_part, key_part, value_part):
    head_size = query_part.shape[-1]
    scores = jnp.einsum(
        "blhd,bmhd->bhlm", query_part, key_part, preferred_element_type=jnp.float32
    ) * head_size ** (-0.5)
    scores = scores - jnp.max(scores, axis=-1, keepdims=True)
    raised = jnp.exp(scores)
    probs = (raised / jnp.sum(raised, axis=-1, keepdims=True)).astype(jnp.bfloat16)
    return jnp.einsum(
        "bhlm,bmhd->blhd", probs, value_part, preferred_element_type=jnp.float32
    ).astype(jnp.bfloat16)


def exchange(blocks, axes):
    return lax.all_to_all(blocks, axes, split_axis=0, concat_axis=0, tiled=True)


def spread_out(block, axes):
    count = lax.axis_size(axes)
    return exchange(jnp.broadcast_to(block[None], (count,) + block.shape), axes)


def times(tokens, weight):
    return jnp.dot(tokens, weight, preferred_element_type=jnp.float32)


def times_transposed(tokens, weight):
    return lax.dot_general(
        tokens, weight, (((1,), (1,)), ((), ())), preferred_element_type=jnp.float32
    )


def shift_ring(block, steps):
    places = [0, 2, 1, 3]
    pairs = [(places[i], places[(i + steps) % 4]) for i in range(4)]
    return lax.ppermute(block, RING, pairs)


def swap_cores(block):
    return lax.ppermute(block, "c", [(0, 1), (1, 0)])


def gather_line(normed):
    before = shift_ring(normed, 1)
    after = shift_ring(normed, -1)
    across = shift_ring(normed, 2)
    near = jnp.concatenate([before, after])
    own_frame = jnp.concatenate([normed, across, swap_cores(normed), swap_cores(across)])
    return own_frame, jnp.concatenate([near, swap_cores(near)])


def join_cores(partial):
    kept, sent = jnp.split(partial, 2)
    return kept + swap_cores(sent.astype(jnp.bfloat16)).astype(jnp.float32)


def scatter_line(own_frame, other_frame):
    before, after = jnp.split(join_cores(other_frame).astype(jnp.bfloat16), 2)
    returned = [shift_ring(before, -1), shift_ring(after, 1)]
    own, across = jnp.split(join_cores(own_frame), 2)
    returned.append(shift_ring(across.astype(jnp.bfloat16), 2))
    return own + sum(part.astype(jnp.float32) for part in returned)


def gather_pair(normed):
    return jnp.concatenate([normed, swap_cores(normed)])


def scatter_pair(partial):
    kept, sent = jnp.split(partial, 2)
    return kept + swap_cores(sent)


def on_device(
    video,
    modulation,
    query_key_value_weight,
    attention_output_weight,
    feed_forward_up_weight,
    feed_forward_down_weight,
):
    stream = video[0]
    own, width = stream.shape
    head_size = width // HEADS
    depth, _, quarter = query_key_value_weight.shape[1:]
    hidden = feed_forward_up_weight.shape[2]
    output_rows = jnp.swapaxes(attention_output_weight, 1, 2)
    down_rows = jnp.swapaxes(feed_forward_down_weight, 1, 2)

    def halves(rows):
        return jnp.swapaxes(rows.reshape(depth, 2, -1), 0, 1)

    def spread_plane(packs):
        columns = packs.shape[-1]
        layers = lax.axis_size("z")
        packs = jnp.broadcast_to(packs[None], (layers,) + packs.shape)
        packs = exchange(packs.reshape(2 * layers, depth, columns), ("z", "xl"))
        packs = spread_out(packs.reshape(-1, columns), ("y",))
        packs = packs.reshape(-1, layers, 2 * depth, columns)
        return jnp.swapaxes(packs, 0, 1).reshape(width, columns)

    qkv = query_key_value_weight[0].reshape(depth, 3, 2, quarter // 2)
    qkv = jnp.transpose(qkv, (2, 0, 1, 3)).reshape(2, depth, -1)
    attention_pack = spread_plane(jnp.concatenate([qkv, halves(output_rows[0])], axis=2))

    pack = jnp.concatenate(
        [
            query_key_value_weight[1].reshape(depth, -1),
            output_rows[1],
            feed_forward_up_weight[1],
            down_rows[1],
        ],
        axis=1,
    )
    packs = jnp.stack([pack] + [shift_ring(pack, -steps) for steps in (1, 2, 3)])
    place = 2 * lax.axis_index("xh") + lax.axis_index("xl")
    packs = lax.dynamic_slice_in_dim(jnp.concatenate([packs, packs]), (4 - place) % 4, 4)
    packs = jnp.transpose(packs.reshape(2, 2, depth, -1), (1, 2, 0, 3)).reshape(2 * depth, 2, -1)
    parts = []
    start = 0
    for count, size in ((3, quarter), (1, quarter), (1, hidden), (1, hidden)):
        part = packs[:, :, start : start + count * size].reshape(-1, 2, count, size)
        parts.append(jnp.swapaxes(part, 1, 2).reshape(2 * depth, -1))
        start += count * size
    gathered = lax.all_gather(jnp.concatenate(parts, axis=1), PLANE, axis=0)

    feed_rows = jnp.concatenate([halves(feed_forward_up_weight[0]), halves(down_rows[0])], axis=2)
    feed_rows, attention_pack = lax.optimization_barrier((feed_rows, attention_pack))
    feed_pack = spread_plane(feed_rows)

    mod = modulation[0]
    local = quarter // 2

    def spatial_attention(normed):
        packed = times(normed, attention_pack[:, : 3 * local]).astype(jnp.bfloat16)
        triple = packed.reshape(1, -1, 3, local // head_size, head_size)
        mixed = attend(triple[:, :, 0], triple[:, :, 1], triple[:, :, 2]).reshape(-1, local)
        return times_transposed(mixed, attention_pack[:, 3 * local :])

    def spatial_feed(normed):
        activated = jax.nn.gelu(times(normed, feed_pack[:, : hidden // 2]), approximate=True)
        return times_transposed(activated.astype(jnp.bfloat16), feed_pack[:, hidden // 2 :])

    own_frame, other_frame = gather_line(normalize(stream, mod[0], mod[1]))
    update = scatter_line(spatial_attention(own_frame), spatial_attention(other_frame))
    stream = (stream.astype(jnp.float32) + mod[2] * update).astype(jnp.bfloat16)
    own_frame, other_frame = gather_line(normalize(stream, mod[3], mod[4]))
    update = scatter_line(spatial_feed(own_frame), spatial_feed(other_frame))
    stream = (stream.astype(jnp.float32) + mod[5] * update).astype(jnp.bfloat16)

    frames = lax.axis_size(FRAME)
    stream = exchange(stream.reshape(frames, own // frames, width), FRAME).reshape(own, width)
    mod = modulation[1]
    local = 2 * quarter
    ends = (4 * local, 4 * local + 2 * hidden)
    attention_pack, up, down = (
        part.reshape(width, -1) for part in jnp.split(gathered, ends, axis=2)
    )
    normed = gather_pair(normalize(stream, mod[0], mod[1]))
    packed = times(normed, attention_pack[:, : 3 * local]).astype(jnp.bfloat16)
    triple = packed.reshape(2, frames, own // frames, 3, local // head_size, head_size)
    triple = jnp.swapaxes(triple, 1, 2).reshape(-1, frames, 3, local // head_size, head_size)
    mixed = attend(triple[:, :, 0], triple[:, :, 1], triple[:, :, 2])
    mixed = jnp.swapaxes(mixed.reshape(2, own // frames, frames, local), 1, 2).reshape(-1, local)
    update = scatter_pair(times_transposed(mixed, attention_pack[:, 3 * local :]))
    stream = (stream.astype(jnp.float32) + mod[2] * update).astype(jnp.bfloat16)
    normed = gather_pair(normalize(stream, mod[3], mod[4]))
    activated = jax.nn.gelu(times(normed, up), approximate=True).astype(jnp.bfloat16)
    update = scatter_pair(times_transposed(activated, down))
    stream = (stream.astype(jnp.float32) + mod[5] * update).astype(jnp.bfloat16)
    stream = exchange(stream.reshape(frames, own // frames, width), FRAME)
    return stream.reshape(1, own, width)


def solution(mesh):
    fine = Mesh(mesh.devices.reshape(8, 4, 2, 2, 2), ("z", "y", "xl", "xh", "c"))
    rows = ("xh", "c")
    in_specs = (
        P(FRAME, rows, None),
        P(),
        P(None, FRAME, None, rows),
        P(None, rows, FRAME),
        P(None, FRAME, rows),
        P(None, rows, FRAME),
    )
    out_specs = P(FRAME, rows, None)
    return jax.shard_map(
        on_device, mesh=fine, in_specs=in_specs, out_specs=out_specs, check_vma=False
    )
```

```python
import jax
import jax.numpy as jnp
import numpy as np
from jax import lax
from jax.sharding import Mesh, PartitionSpec as P

HEADS = 16
EPSILON = 1e-06
LINE = ("xl", "xh", "c")
RING = ("xl", "xh")
PLANE = ("zh", "zl", "y")
FRAME = ("zh", "zl", "y", "xl")


def normalize(token_sequence, shift, scale):
    values = token_sequence.astype(jnp.float32)
    center = values - jnp.mean(values, axis=-1, keepdims=True)
    spread = jnp.mean(center * center, axis=-1, keepdims=True)
    return (center * lax.rsqrt(spread + EPSILON) * (1.0 + scale) + shift).astype(jnp.bfloat16)


def attend(query_part, key_part, value_part):
    head_size = query_part.shape[-1]
    scores = jnp.einsum(
        "blhd,bmhd->bhlm", query_part, key_part, preferred_element_type=jnp.float32
    ) * head_size ** (-0.5)
    scores = scores - jnp.max(scores, axis=-1, keepdims=True)
    raised = jnp.exp(scores)
    probs = (raised / jnp.sum(raised, axis=-1, keepdims=True)).astype(jnp.bfloat16)
    return jnp.einsum(
        "bhlm,bmhd->blhd", probs, value_part, preferred_element_type=jnp.float32
    ).astype(jnp.bfloat16)


def exchange(blocks, axes):
    return lax.all_to_all(blocks, axes, split_axis=0, concat_axis=0, tiled=True)


def spread_out(block, axes):
    count = lax.axis_size(axes)
    return exchange(jnp.broadcast_to(block[None], (count,) + block.shape), axes)


def times(tokens, weight):
    return jnp.dot(tokens, weight, preferred_element_type=jnp.float32)


def times_transposed(tokens, weight):
    return lax.dot_general(
        tokens, weight, (((1,), (1,)), ((), ())), preferred_element_type=jnp.float32
    )


def shift_ring(block, steps):
    places = [0, 2, 1, 3]
    pairs = [(places[i], places[(i + steps) % 4]) for i in range(4)]
    return lax.ppermute(block, RING, pairs)


def swap_cores(block):
    return lax.ppermute(block, "c", [(0, 1), (1, 0)])


def gather_line(normed):
    before = shift_ring(normed, 1)
    after = shift_ring(normed, -1)
    across = shift_ring(normed, 2)
    near = jnp.concatenate([before, after])
    own_frame = jnp.concatenate([normed, across, swap_cores(normed), swap_cores(across)])
    return own_frame, jnp.concatenate([near, swap_cores(near)])


def join_cores(partial):
    kept, sent = jnp.split(partial, 2)
    return kept + swap_cores(sent.astype(jnp.bfloat16)).astype(jnp.float32)


def scatter_line(own_frame, other_frame):
    before, after = jnp.split(join_cores(other_frame).astype(jnp.bfloat16), 2)
    returned = [shift_ring(before, -1), shift_ring(after, 1)]
    own, across = jnp.split(join_cores(own_frame), 2)
    returned.append(shift_ring(across.astype(jnp.bfloat16), 2))
    return own + sum(part.astype(jnp.float32) for part in returned)


def gather_pair(normed):
    return jnp.concatenate([normed, swap_cores(normed)])


def scatter_pair(partial):
    kept, sent = jnp.split(partial, 2)
    return kept + swap_cores(sent)


def on_device(
    video,
    modulation,
    query_key_value_weight,
    attention_output_weight,
    feed_forward_up_weight,
    feed_forward_down_weight,
):
    stream = video[0]
    own, width = stream.shape
    head_size = width // HEADS
    depth, _, quarter = query_key_value_weight.shape[1:]
    hidden = feed_forward_up_weight.shape[2]
    output_rows = jnp.swapaxes(attention_output_weight, 1, 2)
    down_rows = jnp.swapaxes(feed_forward_down_weight, 1, 2)

    order = np.arange(width).reshape(2, 16, -1).swapaxes(0, 1).reshape(-1)
    inner = jnp.asarray(np.eye(width)[:, order], jnp.bfloat16)
    stream = times(stream, inner).astype(jnp.bfloat16)
    modulation = jnp.swapaxes(modulation.reshape(2, 6, 2, 16, -1), 2, 3).reshape(2, 6, width)

    def halves(rows):
        return jnp.swapaxes(rows.reshape(depth, 2, -1), 0, 1)

    def split_qkv(weight):
        parts = weight.reshape(depth, 3, 2, quarter // 2)
        return jnp.transpose(parts, (2, 0, 1, 3)).reshape(2, depth, -1)

    packs = jnp.concatenate(
        [
            split_qkv(query_key_value_weight[0]),
            halves(output_rows[0]),
            halves(feed_forward_up_weight[0]),
            halves(down_rows[0]),
        ],
        axis=2,
    )
    packs = jnp.broadcast_to(packs[None], (8,) + packs.shape).reshape(16, depth, -1)
    pack = jnp.concatenate(
        [
            halves(feed_forward_up_weight[1]),
            halves(down_rows[1]),
            split_qkv(query_key_value_weight[1]),
            halves(output_rows[1]),
        ],
        axis=2,
    )
    packs, pack = lax.optimization_barrier((packs, pack))
    packs = exchange(packs, ("zh", "zl", "xl")).reshape(16 * depth, -1)

    upper = lax.axis_index("zh") == 1
    kept = jnp.where(upper, pack[1], pack[0])
    met = lax.ppermute(jnp.where(upper, pack[0], pack[1]), "zh", [(0, 1), (1, 0)])
    pack = jnp.where(upper, jnp.stack([met, kept]), jnp.stack([kept, met]))
    ring = jnp.stack([pack] + [shift_ring(pack, -steps) for steps in (1, 2, 3)])
    place = 2 * lax.axis_index("xh") + lax.axis_index("xl")
    ring = lax.dynamic_slice_in_dim(jnp.concatenate([ring, ring]), (4 - place) % 4, 4)
    ring = jnp.transpose(ring.reshape(2, 2, 2, depth, -1), (2, 1, 3, 0, 4))
    ring = ring.reshape(4 * depth, 2, -1)
    parts = []
    start = 0
    for count, size in ((1, hidden // 2), (1, hidden // 2), (3, quarter // 2), (1, quarter // 2)):
        part = ring[:, :, start : start + count * size].reshape(-1, 2, count, size)
        parts.append(jnp.swapaxes(part, 1, 2).reshape(4 * depth, -1))
        start += count * size
    temporal_packs = lax.all_gather(jnp.concatenate(parts, axis=1), PLANE, axis=0)
    temporal_packs = temporal_packs.reshape(2, width, -1)

    def spread_rows(rows):
        columns = rows.shape[-1]
        rows = spread_out(rows, ("y",)).reshape(4, 2, 4, 2 * depth, columns)
        return jnp.transpose(rows, (2, 0, 1, 3, 4)).reshape(width, columns)

    attention_pack = spread_rows(packs[:, : 2 * quarter])
    feed_rows, attention_pack = lax.optimization_barrier((packs[:, 2 * quarter :], attention_pack))
    feed_pack = spread_rows(feed_rows)

    mod = modulation[0]
    local = quarter // 2

    def spatial_attention(normed):
        packed = times(normed, attention_pack[:, : 3 * local]).astype(jnp.bfloat16)
        triple = packed.reshape(1, -1, 3, local // head_size, head_size)
        mixed = attend(triple[:, :, 0], triple[:, :, 1], triple[:, :, 2]).reshape(-1, local)
        return times_transposed(mixed, attention_pack[:, 3 * local :])

    def spatial_feed(normed):
        activated = jax.nn.gelu(times(normed, feed_pack[:, : hidden // 2]), approximate=True)
        return times_transposed(activated.astype(jnp.bfloat16), feed_pack[:, hidden // 2 :])

    own_frame, other_frame = gather_line(normalize(stream, mod[0], mod[1]))
    update = scatter_line(spatial_attention(own_frame), spatial_attention(other_frame))
    stream = (stream.astype(jnp.float32) + mod[2] * update).astype(jnp.bfloat16)
    own_frame, other_frame = gather_line(normalize(stream, mod[3], mod[4]))
    update = scatter_line(spatial_feed(own_frame), spatial_feed(other_frame))
    stream = (stream.astype(jnp.float32) + mod[5] * update).astype(jnp.bfloat16)

    frames = lax.axis_size(FRAME)
    stream = exchange(stream.reshape(frames, own // frames, width), FRAME).reshape(own, width)
    mod = modulation[1]
    local = quarter
    heads = local // head_size
    normed = gather_pair(normalize(stream, mod[0], mod[1]))
    update = 0.0
    for group in range(2):
        weights = temporal_packs[group][:, 2 * hidden :]
        packed = times(normed, weights[:, : 3 * local]).astype(jnp.bfloat16)
        triple = packed.reshape(2, frames, own // frames, 3, heads, head_size)
        triple = jnp.swapaxes(triple, 1, 2).reshape(-1, frames, 3, heads, head_size)
        mixed = attend(triple[:, :, 0], triple[:, :, 1], triple[:, :, 2])
        mixed = jnp.swapaxes(mixed.reshape(2, own // frames, frames, local), 1, 2)
        update += times_transposed(mixed.reshape(-1, local), weights[:, 3 * local :])
    stream = (stream.astype(jnp.float32) + mod[2] * scatter_pair(update)).astype(jnp.bfloat16)
    normed = gather_pair(normalize(stream, mod[3], mod[4]))
    update = 0.0
    for group in range(2):
        weights = temporal_packs[group][:, : 2 * hidden]
        activated = jax.nn.gelu(times(normed, weights[:, :hidden]), approximate=True)
        update += times_transposed(activated.astype(jnp.bfloat16), weights[:, hidden:])
    stream = (stream.astype(jnp.float32) + mod[5] * scatter_pair(update)).astype(jnp.bfloat16)
    stream = times_transposed(stream, inner).astype(jnp.bfloat16)
    stream = exchange(stream.reshape(frames, own // frames, width), FRAME)
    return stream.reshape(1, own, width)


def solution(mesh):
    fine = Mesh(mesh.devices.reshape(2, 4, 4, 2, 2, 2), ("zh", "zl", "y", "xl", "xh", "c"))
    rows = ("xh", "c")
    in_specs = (
        P(FRAME, rows, None),
        P(),
        P(None, FRAME, None, rows),
        P(None, rows, FRAME),
        P(None, FRAME, rows),
        P(None, rows, FRAME),
    )
    out_specs = P(FRAME, rows, None)
    return jax.shard_map(
        on_device, mesh=fine, in_specs=in_specs, out_specs=out_specs, check_vma=False
    )
```

```python
import jax
import jax.numpy as jnp
import numpy as np
from jax import lax
from jax.sharding import Mesh, PartitionSpec as P

HEADS = 16
EPSILON = 1e-06
LINE = ("xl", "xh", "c")
RING = ("xl", "xh")
PLANE = ("zh", "zl", "y")
FRAME = ("zh", "zl", "y", "xl")


def normalize(token_sequence, shift, scale):
    values = token_sequence.astype(jnp.float32)
    center = values - jnp.mean(values, axis=-1, keepdims=True)
    spread = jnp.mean(center * center, axis=-1, keepdims=True)
    return (center * lax.rsqrt(spread + EPSILON) * (1.0 + scale) + shift).astype(jnp.bfloat16)


def attend(query_part, key_part, value_part):
    head_size = query_part.shape[-1]
    scores = jnp.einsum(
        "blhd,bmhd->bhlm", query_part, key_part, preferred_element_type=jnp.float32
    ) * head_size ** (-0.5)
    scores = scores - jnp.max(scores, axis=-1, keepdims=True)
    raised = jnp.exp(scores)
    probs = (raised / jnp.sum(raised, axis=-1, keepdims=True)).astype(jnp.bfloat16)
    return jnp.einsum(
        "bhlm,bmhd->blhd", probs, value_part, preferred_element_type=jnp.float32
    ).astype(jnp.bfloat16)


def exchange(blocks, axes):
    return lax.all_to_all(blocks, axes, split_axis=0, concat_axis=0, tiled=True)


def spread_out(block, axes):
    count = lax.axis_size(axes)
    return exchange(jnp.broadcast_to(block[None], (count,) + block.shape), axes)


def times(tokens, weight):
    return jnp.dot(tokens, weight, preferred_element_type=jnp.float32)


def times_transposed(tokens, weight):
    return lax.dot_general(
        tokens, weight, (((1,), (1,)), ((), ())), preferred_element_type=jnp.float32
    )


def shift_ring(block, steps):
    places = [0, 2, 1, 3]
    pairs = [(places[i], places[(i + steps) % 4]) for i in range(4)]
    return lax.ppermute(block, RING, pairs)


def swap_cores(block):
    return lax.ppermute(block, "c", [(0, 1), (1, 0)])


def gather_line(normed):
    before = shift_ring(normed, 1)
    after = shift_ring(normed, -1)
    across = shift_ring(normed, 2)
    near = jnp.concatenate([before, after])
    own_frame = jnp.concatenate([normed, across, swap_cores(normed), swap_cores(across)])
    return own_frame, jnp.concatenate([near, swap_cores(near)])


def join_cores(partial):
    kept, sent = jnp.split(partial, 2)
    return kept + swap_cores(sent.astype(jnp.bfloat16)).astype(jnp.float32)


def scatter_line(own_frame, other_frame):
    before, after = jnp.split(join_cores(other_frame).astype(jnp.bfloat16), 2)
    returned = [shift_ring(before, -1), shift_ring(after, 1)]
    own, across = jnp.split(join_cores(own_frame), 2)
    returned.append(shift_ring(across.astype(jnp.bfloat16), 2))
    return own + sum(part.astype(jnp.float32) for part in returned)


def gather_pair(normed):
    return jnp.concatenate([normed, swap_cores(normed)])


def scatter_pair(partial):
    kept, sent = jnp.split(partial, 2)
    return kept + swap_cores(sent)


def on_device(
    video,
    modulation,
    query_key_value_weight,
    attention_output_weight,
    feed_forward_up_weight,
    feed_forward_down_weight,
):
    stream = video[0]
    own, width = stream.shape
    head_size = width // HEADS
    depth, _, quarter = query_key_value_weight.shape[1:]
    hidden = feed_forward_up_weight.shape[2]
    output_rows = jnp.swapaxes(attention_output_weight, 1, 2)
    down_rows = jnp.swapaxes(feed_forward_down_weight, 1, 2)

    order = np.arange(width).reshape(2, 16, -1).swapaxes(0, 1).reshape(-1)
    inner = jnp.asarray(np.eye(width)[:, order], jnp.bfloat16)
    stream = times(stream, inner).astype(jnp.bfloat16)
    modulation = jnp.swapaxes(modulation.reshape(2, 6, 2, 16, -1), 2, 3).reshape(2, 6, width)

    def halves(rows):
        return jnp.swapaxes(rows.reshape(depth, 2, -1), 0, 1)

    def split_qkv(weight):
        parts = weight.reshape(depth, 3, 2, quarter // 2)
        return jnp.transpose(parts, (2, 0, 1, 3)).reshape(2, depth, -1)

    packs = jnp.concatenate(
        [
            split_qkv(query_key_value_weight[0]),
            halves(output_rows[0]),
            halves(feed_forward_up_weight[0]),
            halves(down_rows[0]),
        ],
        axis=2,
    )
    packs = jnp.broadcast_to(packs[None], (8,) + packs.shape).reshape(16, depth, -1)
    pack = jnp.concatenate(
        [
            halves(feed_forward_up_weight[1]),
            halves(down_rows[1]),
            split_qkv(query_key_value_weight[1]),
            halves(output_rows[1]),
        ],
        axis=2,
    )
    packs, pack = lax.optimization_barrier((packs, pack))
    packs = exchange(packs, ("zh", "zl", "xl")).reshape(16 * depth, -1)

    upper = lax.axis_index("zh") == 1
    kept = jnp.where(upper, pack[1], pack[0])
    met = lax.ppermute(jnp.where(upper, pack[0], pack[1]), "zh", [(0, 1), (1, 0)])
    pack = jnp.where(upper, jnp.stack([met, kept]), jnp.stack([kept, met]))
    ring = jnp.stack([pack] + [shift_ring(pack, -steps) for steps in (1, 2, 3)])
    place = 2 * lax.axis_index("xh") + lax.axis_index("xl")
    ring = lax.dynamic_slice_in_dim(jnp.concatenate([ring, ring]), (4 - place) % 4, 4)
    ring = jnp.transpose(ring.reshape(2, 2, 2, depth, -1), (2, 1, 3, 0, 4))
    ring = ring.reshape(4 * depth, 2, -1)
    parts = []
    start = 0
    for count, size in ((1, hidden // 2), (1, hidden // 2), (3, quarter // 2), (1, quarter // 2)):
        part = ring[:, :, start : start + count * size].reshape(-1, 2, count, size)
        parts.append(jnp.swapaxes(part, 1, 2).reshape(4 * depth, -1))
        start += count * size
    pack, packs = lax.optimization_barrier((jnp.concatenate(parts, axis=1), packs))
    temporal_packs = lax.all_gather(pack, PLANE, axis=0)
    temporal_packs = temporal_packs.reshape(2, width, -1)

    def inner_rows(spread):
        spread = spread.reshape(4, 2, 4, 2 * depth, -1)
        return jnp.transpose(spread, (2, 0, 1, 3, 4)).reshape(width, -1)

    attention_spread = spread_out(packs[:, : 2 * quarter], ("y",))
    feed_rows, attention_spread = lax.optimization_barrier((packs[:, 2 * quarter :], attention_spread))
    feed_spread = spread_out(feed_rows, ("y",))
    attention_pack = inner_rows(attention_spread)

    mod = modulation[0]
    local = quarter // 2

    def spatial_attention(normed):
        packed = times(normed, attention_pack[:, : 3 * local]).astype(jnp.bfloat16)
        triple = packed.reshape(1, -1, 3, local // head_size, head_size)
        mixed = attend(triple[:, :, 0], triple[:, :, 1], triple[:, :, 2]).reshape(-1, local)
        return times_transposed(mixed, attention_pack[:, 3 * local :])

    def spatial_feed(normed):
        activated = jax.nn.gelu(times(normed, feed_pack[:, : hidden // 2]), approximate=True)
        return times_transposed(activated.astype(jnp.bfloat16), feed_pack[:, hidden // 2 :])

    own_frame, other_frame = gather_line(normalize(stream, mod[0], mod[1]))
    update = scatter_line(spatial_attention(own_frame), spatial_attention(other_frame))
    update, feed_spread = lax.optimization_barrier((update, feed_spread))
    feed_pack = inner_rows(feed_spread)
    stream = (stream.astype(jnp.float32) + mod[2] * update).astype(jnp.bfloat16)
    own_frame, other_frame = gather_line(normalize(stream, mod[3], mod[4]))
    update = scatter_line(spatial_feed(own_frame), spatial_feed(other_frame))
    stream = (stream.astype(jnp.float32) + mod[5] * update).astype(jnp.bfloat16)

    frames = lax.axis_size(FRAME)
    stream = exchange(stream.reshape(frames, own // frames, width), FRAME).reshape(own, width)
    mod = modulation[1]
    local = quarter
    heads = local // head_size
    normed = gather_pair(normalize(stream, mod[0], mod[1]))
    update = 0.0
    for group in range(2):
        weights = temporal_packs[group][:, 2 * hidden :]
        packed = times(normed, weights[:, : 3 * local]).astype(jnp.bfloat16)
        triple = packed.reshape(2, frames, own // frames, 3, heads, head_size)
        triple = jnp.swapaxes(triple, 1, 2).reshape(-1, frames, 3, heads, head_size)
        mixed = attend(triple[:, :, 0], triple[:, :, 1], triple[:, :, 2])
        mixed = jnp.swapaxes(mixed.reshape(2, own // frames, frames, local), 1, 2)
        update += times_transposed(mixed.reshape(-1, local), weights[:, 3 * local :])
    stream = (stream.astype(jnp.float32) + mod[2] * scatter_pair(update)).astype(jnp.bfloat16)
    normed = gather_pair(normalize(stream, mod[3], mod[4]))
    update = 0.0
    for group in range(2):
        weights = temporal_packs[group][:, : 2 * hidden]
        activated = jax.nn.gelu(times(normed, weights[:, :hidden]), approximate=True)
        update += times_transposed(activated.astype(jnp.bfloat16), weights[:, hidden:])
    stream = (stream.astype(jnp.float32) + mod[5] * scatter_pair(update)).astype(jnp.bfloat16)
    stream = times_transposed(stream, inner).astype(jnp.bfloat16)
    stream = exchange(stream.reshape(frames, own // frames, width), FRAME)
    return stream.reshape(1, own, width)


def solution(mesh):
    fine = Mesh(mesh.devices.reshape(2, 4, 4, 2, 2, 2), ("zh", "zl", "y", "xl", "xh", "c"))
    rows = ("xh", "c")
    in_specs = (
        P(FRAME, rows, None),
        P(),
        P(None, FRAME, None, rows),
        P(None, rows, FRAME),
        P(None, FRAME, rows),
        P(None, rows, FRAME),
    )
    out_specs = P(FRAME, rows, None)
    return jax.shard_map(
        on_device, mesh=fine, in_specs=in_specs, out_specs=out_specs, check_vma=False
    )
```

```python
import jax
import jax.numpy as jnp
import numpy as np
from jax import lax
from jax.sharding import Mesh, PartitionSpec as P

HEADS = 16
EPSILON = 1e-06
LINE = ("xl", "xh", "c")
RING = ("xl", "xh")
PLANE = ("zh", "zl", "y")
FRAME = ("zh", "zl", "y", "xl")


def normalize(token_sequence, shift, scale):
    values = token_sequence.astype(jnp.float32)
    center = values - jnp.mean(values, axis=-1, keepdims=True)
    spread = jnp.mean(center * center, axis=-1, keepdims=True)
    return (center * lax.rsqrt(spread + EPSILON) * (1.0 + scale) + shift).astype(jnp.bfloat16)


def attend(query_part, key_part, value_part):
    head_size = query_part.shape[-1]
    scores = jnp.einsum(
        "blhd,bmhd->bhlm", query_part, key_part, preferred_element_type=jnp.float32
    ) * head_size ** (-0.5)
    scores = scores - jnp.max(scores, axis=-1, keepdims=True)
    raised = jnp.exp(scores)
    probs = (raised / jnp.sum(raised, axis=-1, keepdims=True)).astype(jnp.bfloat16)
    return jnp.einsum(
        "bhlm,bmhd->blhd", probs, value_part, preferred_element_type=jnp.float32
    ).astype(jnp.bfloat16)


def exchange(blocks, axes):
    return lax.all_to_all(blocks, axes, split_axis=0, concat_axis=0, tiled=True)


def spread_out(block, axes):
    count = lax.axis_size(axes)
    return exchange(jnp.broadcast_to(block[None], (count,) + block.shape), axes)


def times(tokens, weight):
    return jnp.dot(tokens, weight, preferred_element_type=jnp.float32)


def times_transposed(tokens, weight):
    return lax.dot_general(
        tokens, weight, (((1,), (1,)), ((), ())), preferred_element_type=jnp.float32
    )


def shift_ring(block, steps):
    places = [0, 2, 1, 3]
    pairs = [(places[i], places[(i + steps) % 4]) for i in range(4)]
    return lax.ppermute(block, RING, pairs)


def swap_cores(block):
    return lax.ppermute(block, "c", [(0, 1), (1, 0)])


def gather_line(normed):
    before = shift_ring(normed, 1)
    after = shift_ring(normed, -1)
    across = shift_ring(normed, 2)
    near = jnp.concatenate([before, after])
    own_frame = jnp.concatenate([normed, across, swap_cores(normed), swap_cores(across)])
    return own_frame, jnp.concatenate([near, swap_cores(near)])


def join_cores(partial):
    kept, sent = jnp.split(partial, 2)
    return kept + swap_cores(sent.astype(jnp.bfloat16)).astype(jnp.float32)


def scatter_line(own_frame, other_frame):
    before, after = jnp.split(join_cores(other_frame).astype(jnp.bfloat16), 2)
    returned = [shift_ring(before, -1), shift_ring(after, 1)]
    own, across = jnp.split(join_cores(own_frame), 2)
    returned.append(shift_ring(across.astype(jnp.bfloat16), 2))
    return own + sum(part.astype(jnp.float32) for part in returned)


def gather_pair(normed):
    return jnp.concatenate([normed, swap_cores(normed)])


def scatter_pair(partial):
    kept, sent = jnp.split(partial, 2)
    return kept + swap_cores(sent)


def on_device(
    video,
    modulation,
    query_key_value_weight,
    attention_output_weight,
    feed_forward_up_weight,
    feed_forward_down_weight,
):
    stream = video[0]
    own, width = stream.shape
    head_size = width // HEADS
    depth, _, quarter = query_key_value_weight.shape[1:]
    hidden = feed_forward_up_weight.shape[2]
    output_rows = jnp.swapaxes(attention_output_weight, 1, 2)
    down_rows = jnp.swapaxes(feed_forward_down_weight, 1, 2)

    order = np.arange(width).reshape(2, 16, -1).swapaxes(0, 1).reshape(-1)
    inner = jnp.asarray(np.eye(width)[:, order], jnp.bfloat16)
    stream = times(stream, inner).astype(jnp.bfloat16)
    modulation = jnp.swapaxes(modulation.reshape(2, 6, 2, 16, -1), 2, 3).reshape(2, 6, width)

    def halves(rows):
        return jnp.swapaxes(rows.reshape(depth, 2, -1), 0, 1)

    def split_qkv(weight):
        parts = weight.reshape(depth, 3, 2, quarter // 2)
        return jnp.transpose(parts, (2, 0, 1, 3)).reshape(2, depth, -1)

    first = jnp.concatenate([split_qkv(query_key_value_weight[0]), halves(output_rows[0])], axis=2)
    first = jnp.broadcast_to(first[None], (8,) + first.shape).reshape(16, depth, -1)
    eighth = hidden // 2
    feed = jnp.concatenate(
        [
            rows[0].reshape(depth, 2, 2, eighth // 2)
            for rows in (feed_forward_up_weight, down_rows)
        ],
        axis=3,
    )
    feed = jnp.transpose(feed, (2, 0, 1, 3)).reshape(2, depth, 2 * eighth)
    second = jnp.concatenate(
        [feed, split_qkv(query_key_value_weight[1]), halves(output_rows[1])], axis=2
    )
    third = jnp.concatenate([halves(feed_forward_up_weight[1]), halves(down_rows[1])], axis=2)
    first, second = lax.optimization_barrier((first, second))
    first = exchange(first, ("zh", "zl", "xl")).reshape(16 * depth, -1)

    def meet(kept, met, axis):
        upper = lax.axis_index(axis) == 1
        return jnp.where(upper, jnp.stack([met, kept]), jnp.stack([kept, met]))

    def swap(halved, axis):
        upper = lax.axis_index(axis) == 1
        sent = jnp.where(upper, halved[0], halved[1])
        kept = jnp.where(upper, halved[1], halved[0])
        return meet(kept, lax.ppermute(sent, axis, [(0, 1), (1, 0)]), axis)

    def spread_ring(block, sizes):
        ring = jnp.stack([block] + [shift_ring(block, -steps) for steps in (1, 2, 3)])
        place = 2 * lax.axis_index("xh") + lax.axis_index("xl")
        ring = lax.dynamic_slice_in_dim(jnp.concatenate([ring, ring]), (4 - place) % 4, 4)
        ring = jnp.transpose(ring.reshape(2, 2, 2, depth, -1), (2, 1, 3, 0, 4))
        ring = ring.reshape(4 * depth, 2, -1)
        parts = []
        start = 0
        for count, size in sizes:
            part = ring[:, :, start : start + count * size].reshape(-1, 2, count, size)
            parts.append(jnp.swapaxes(part, 1, 2).reshape(4 * depth, -1))
            start += count * size
        return parts

    half = quarter // 2
    second = swap(second, "zh")
    feed = jnp.moveaxis(second[:, :, : 2 * eighth].reshape(2, depth, 2, -1), 2, 0)
    feed = jnp.swapaxes(swap(feed, "xl"), 0, 1).reshape(4 * depth, -1)
    parts = spread_ring(second[:, :, 2 * eighth :], ((3, half), (1, half)))
    second = jnp.concatenate(parts + [feed], axis=1)
    second, first, third = lax.optimization_barrier((second, first, third))
    second = lax.all_gather(second, PLANE, axis=0).reshape(2, width, -1)

    third = spread_ring(swap(third, "zh"), ((1, eighth), (1, eighth)))
    third = lax.all_gather(jnp.concatenate(third, axis=1), PLANE, axis=0).reshape(2, width, -1)

    first = spread_out(first, ("y",)).reshape(4, 2, 4, 2 * depth, -1)
    attention_pack = jnp.transpose(first, (2, 0, 1, 3, 4)).reshape(width, -1)

    mod = modulation[0]
    local = quarter // 2

    def spatial_attention(normed):
        packed = times(normed, attention_pack[:, : 3 * local]).astype(jnp.bfloat16)
        triple = packed.reshape(1, -1, 3, local // head_size, head_size)
        mixed = attend(triple[:, :, 0], triple[:, :, 1], triple[:, :, 2]).reshape(-1, local)
        return times_transposed(mixed, attention_pack[:, 3 * local :])

    def spatial_feed(normed):
        activated = jax.nn.gelu(times(normed, up), approximate=True)
        return times_transposed(activated.astype(jnp.bfloat16), down)

    own_frame, other_frame = gather_line(normalize(stream, mod[0], mod[1]))
    update = scatter_line(spatial_attention(own_frame), spatial_attention(other_frame))
    stream = (stream.astype(jnp.float32) + mod[2] * update).astype(jnp.bfloat16)
    feed = second[:, :, 4 * quarter :]
    up = jnp.concatenate([feed[0, :, : eighth // 2], feed[1, :, : eighth // 2]], axis=1)
    down = jnp.concatenate([feed[0, :, eighth // 2 :], feed[1, :, eighth // 2 :]], axis=1)
    own_frame, other_frame = gather_line(normalize(stream, mod[3], mod[4]))
    update = scatter_line(spatial_feed(own_frame), spatial_feed(other_frame))
    stream = (stream.astype(jnp.float32) + mod[5] * update).astype(jnp.bfloat16)

    frames = lax.axis_size(FRAME)
    stream = exchange(stream.reshape(frames, own // frames, width), FRAME).reshape(own, width)
    mod = modulation[1]
    local = quarter
    heads = local // head_size
    normed = gather_pair(normalize(stream, mod[0], mod[1]))
    update = 0.0
    for group in range(2):
        weights = second[group][:, : 4 * quarter]
        packed = times(normed, weights[:, : 3 * local]).astype(jnp.bfloat16)
        triple = packed.reshape(2, frames, own // frames, 3, heads, head_size)
        triple = jnp.swapaxes(triple, 1, 2).reshape(-1, frames, 3, heads, head_size)
        mixed = attend(triple[:, :, 0], triple[:, :, 1], triple[:, :, 2])
        mixed = jnp.swapaxes(mixed.reshape(2, own // frames, frames, local), 1, 2)
        update += times_transposed(mixed.reshape(-1, local), weights[:, 3 * local :])
    stream = (stream.astype(jnp.float32) + mod[2] * scatter_pair(update)).astype(jnp.bfloat16)
    normed = gather_pair(normalize(stream, mod[3], mod[4]))
    update = 0.0
    for group in range(2):
        weights = third[group]
        activated = jax.nn.gelu(times(normed, weights[:, :hidden]), approximate=True)
        update += times_transposed(activated.astype(jnp.bfloat16), weights[:, hidden:])
    stream = (stream.astype(jnp.float32) + mod[5] * scatter_pair(update)).astype(jnp.bfloat16)
    stream = times_transposed(stream, inner).astype(jnp.bfloat16)
    stream = exchange(stream.reshape(frames, own // frames, width), FRAME)
    return stream.reshape(1, own, width)


def solution(mesh):
    fine = Mesh(mesh.devices.reshape(2, 4, 4, 2, 2, 2), ("zh", "zl", "y", "xl", "xh", "c"))
    rows = ("xh", "c")
    in_specs = (
        P(FRAME, rows, None),
        P(),
        P(None, FRAME, None, rows),
        P(None, rows, FRAME),
        P(None, FRAME, rows),
        P(None, rows, FRAME),
    )
    out_specs = P(FRAME, rows, None)
    return jax.shard_map(
        on_device, mesh=fine, in_specs=in_specs, out_specs=out_specs, check_vma=False
    )
```

```python
import functools

import jax
import jax.numpy as jnp
import numpy as np
from jax import lax
from jax.experimental import pallas as pl
from jax.experimental.pallas import tpu as pltpu
from jax.sharding import Mesh, PartitionSpec as P

HEADS = 16
EPSILON = 1e-06
LINE = ("xl", "xh", "c")
RING = ("xl", "xh")
PLANE = ("zh", "zl", "y")
FRAME = ("zh", "zl", "y", "xl")


def normalize(token_sequence, shift, scale):
    values = token_sequence.astype(jnp.float32)
    center = values - jnp.mean(values, axis=-1, keepdims=True)
    spread = jnp.mean(center * center, axis=-1, keepdims=True)
    return (center * lax.rsqrt(spread + EPSILON) * (1.0 + scale) + shift).astype(jnp.bfloat16)


VMEM_LIMIT = 48 * 1024 * 1024


def product(left, right):
    return jnp.dot(left, right, preferred_element_type=jnp.float32)


def product_transposed(left, right):
    return lax.dot_general(
        left, right, (((1,), (1,)), ((), ())), preferred_element_type=jnp.float32
    )


def finish(total, kept_ref, sent_ref):
    rows = kept_ref.shape[0]
    kept_ref[...] = total[:rows]
    sent_ref[...] = total[rows:].astype(jnp.bfloat16)


def attention_kernel(heads, size, patches, x_ref, w_ref, kept_ref, sent_ref, packed, mixed, total):
    local = heads * size
    tokens = x_ref.shape[0]
    packed[...] = product(x_ref[...], w_ref[:, : 3 * local]).astype(jnp.bfloat16)
    if patches > 1:
        half = tokens // 2
        row = lax.broadcasted_iota(jnp.int32, (tokens, tokens), 0)
        column = lax.broadcasted_iota(jnp.int32, (tokens, tokens), 1)
        same = (row % patches == column % patches) & ((row < half) == (column < half))
    for head in range(heads):
        at = head * size
        query = packed[:, at : at + size]
        key = packed[:, local + at : local + at + size]
        value = packed[:, 2 * local + at : 2 * local + at + size]
        scores = product_transposed(query, key) * size ** (-0.5)
        if patches > 1:
            scores = jnp.where(same, scores, -1e30)
        raised = jnp.exp(scores - jnp.max(scores, axis=-1, keepdims=True))
        probs = raised * (1.0 / jnp.sum(raised, axis=-1, keepdims=True))
        mixed[:, at : at + size] = product(probs.astype(jnp.bfloat16), value).astype(jnp.bfloat16)
    part = product_transposed(mixed[...], w_ref[:, 3 * local : 4 * local])
    step = pl.program_id(0)
    last = pl.num_programs(0) - 1

    @pl.when(step == 0)
    def _():
        total[...] = part

    @pl.when(step > 0)
    def _():
        total[...] += part

    @pl.when(step == last)
    def _():
        finish(total[...], kept_ref, sent_ref)


def attention_part(normed, weights, heads, size, patches):
    tokens, width = normed.shape
    local = heads * size
    half = (tokens // 2, width)
    return pl.pallas_call(
        functools.partial(attention_kernel, heads, size, patches),
        grid=(weights.shape[0],),
        in_specs=[
            pl.BlockSpec((tokens, width), lambda g: (0, 0)),
            pl.BlockSpec((None, width, 4 * local), lambda g: (g, 0, 0)),
        ],
        out_specs=[pl.BlockSpec(half, lambda g: (0, 0))] * 2,
        out_shape=[
            jax.ShapeDtypeStruct(half, jnp.float32),
            jax.ShapeDtypeStruct(half, jnp.bfloat16),
        ],
        scratch_shapes=[
            pltpu.VMEM((tokens, 3 * local), jnp.bfloat16),
            pltpu.VMEM((tokens, local), jnp.bfloat16),
            pltpu.VMEM((tokens, width), jnp.float32),
        ],
        compiler_params=pltpu.CompilerParams(vmem_limit_bytes=VMEM_LIMIT),
    )(normed, weights)


def feed_kernel(columns, x_ref, *refs):
    *weights, kept_ref, sent_ref, total = refs
    up_ref, down_ref = weights[0], weights[-1]
    start = columns if len(weights) == 1 else 0
    hidden = product(x_ref[...], up_ref[:, :columns])
    activated = jax.nn.gelu(hidden, approximate=True).astype(jnp.bfloat16)
    part = product_transposed(activated, down_ref[:, start : start + columns])
    step = pl.program_id(0)
    last = pl.num_programs(0) - 1

    @pl.when(step == 0)
    def _():
        total[...] = part

    @pl.when(step > 0)
    def _():
        total[...] += part

    @pl.when(step == last)
    def _():
        finish(total[...], kept_ref, sent_ref)


def feed_part(normed, weights, steps, columns, specs):
    tokens, width = normed.shape
    half = (tokens // 2, width)
    return pl.pallas_call(
        functools.partial(feed_kernel, columns),
        grid=(steps,),
        in_specs=[pl.BlockSpec((tokens, width), lambda j: (0, 0))] + specs,
        out_specs=[pl.BlockSpec(half, lambda j: (0, 0))] * 2,
        out_shape=[
            jax.ShapeDtypeStruct(half, jnp.float32),
            jax.ShapeDtypeStruct(half, jnp.bfloat16),
        ],
        scratch_shapes=[pltpu.VMEM((tokens, width), jnp.float32)],
        compiler_params=pltpu.CompilerParams(vmem_limit_bytes=VMEM_LIMIT),
    )(normed, *[weights] * len(specs))


def exchange(blocks, axes):
    return lax.all_to_all(blocks, axes, split_axis=0, concat_axis=0, tiled=True)


def spread_out(block, axes):
    count = lax.axis_size(axes)
    return exchange(jnp.broadcast_to(block[None], (count,) + block.shape), axes)


def shift_ring(block, steps):
    places = [0, 2, 1, 3]
    pairs = [(places[i], places[(i + steps) % 4]) for i in range(4)]
    return lax.ppermute(block, RING, pairs)


def swap_cores(block):
    return lax.ppermute(block, "c", [(0, 1), (1, 0)])


def gather_line(normed):
    before = shift_ring(normed, 1)
    after = shift_ring(normed, -1)
    across = shift_ring(normed, 2)
    near = jnp.concatenate([before, after])
    own_frame = jnp.concatenate([normed, across, swap_cores(normed), swap_cores(across)])
    return own_frame, jnp.concatenate([near, swap_cores(near)])


def join_cores(partial):
    kept, sent = partial
    return kept + swap_cores(sent).astype(jnp.float32)


def scatter_line(own_frame, other_frame):
    before, after = jnp.split(join_cores(other_frame).astype(jnp.bfloat16), 2)
    returned = [shift_ring(before, -1), shift_ring(after, 1)]
    own, across = jnp.split(join_cores(own_frame), 2)
    returned.append(shift_ring(across.astype(jnp.bfloat16), 2))
    return own + sum(part.astype(jnp.float32) for part in returned)


def gather_pair(normed):
    return jnp.concatenate([normed, swap_cores(normed)])


def on_device(
    video,
    modulation,
    query_key_value_weight,
    attention_output_weight,
    feed_forward_up_weight,
    feed_forward_down_weight,
):
    stream = video[0]
    own, width = stream.shape
    head_size = width // HEADS
    depth, _, quarter = query_key_value_weight.shape[1:]
    hidden = feed_forward_up_weight.shape[2]
    output_rows = jnp.swapaxes(attention_output_weight, 1, 2)
    down_rows = jnp.swapaxes(feed_forward_down_weight, 1, 2)

    order = np.arange(width).reshape(2, 16, -1).swapaxes(0, 1).reshape(-1)
    inner = jnp.asarray(np.eye(width)[:, order], jnp.bfloat16)
    stream = product(stream, inner).astype(jnp.bfloat16)
    modulation = jnp.swapaxes(modulation.reshape(2, 6, 2, 16, -1), 2, 3).reshape(2, 6, width)

    def halves(rows):
        return jnp.swapaxes(rows.reshape(depth, 2, -1), 0, 1)

    def split_qkv(weight):
        parts = weight.reshape(depth, 3, 2, quarter // 2)
        return jnp.transpose(parts, (2, 0, 1, 3)).reshape(2, depth, -1)

    first = jnp.concatenate([split_qkv(query_key_value_weight[0]), halves(output_rows[0])], axis=2)
    first = jnp.broadcast_to(first[None], (8,) + first.shape).reshape(16, depth, -1)
    eighth = hidden // 2
    feed = jnp.concatenate(
        [
            rows[0].reshape(depth, 2, 2, eighth // 2)
            for rows in (feed_forward_up_weight, down_rows)
        ],
        axis=3,
    )
    feed = jnp.transpose(feed, (2, 0, 1, 3)).reshape(2, depth, 2 * eighth)
    second = jnp.concatenate(
        [feed, split_qkv(query_key_value_weight[1]), halves(output_rows[1])], axis=2
    )
    third = jnp.concatenate([halves(feed_forward_up_weight[1]), halves(down_rows[1])], axis=2)
    first, second = lax.optimization_barrier((first, second))
    first = exchange(first, ("zh", "zl", "xl")).reshape(16 * depth, -1)

    def meet(kept, met, axis):
        upper = lax.axis_index(axis) == 1
        return jnp.where(upper, jnp.stack([met, kept]), jnp.stack([kept, met]))

    def swap(halved, axis):
        upper = lax.axis_index(axis) == 1
        sent = jnp.where(upper, halved[0], halved[1])
        kept = jnp.where(upper, halved[1], halved[0])
        return meet(kept, lax.ppermute(sent, axis, [(0, 1), (1, 0)]), axis)

    def spread_ring(block, sizes):
        ring = jnp.stack([block] + [shift_ring(block, -steps) for steps in (1, 2, 3)])
        place = 2 * lax.axis_index("xh") + lax.axis_index("xl")
        ring = lax.dynamic_slice_in_dim(jnp.concatenate([ring, ring]), (4 - place) % 4, 4)
        ring = jnp.transpose(ring.reshape(2, 2, 2, depth, -1), (2, 1, 3, 0, 4))
        ring = ring.reshape(4 * depth, 2, -1)
        parts = []
        start = 0
        for count, size in sizes:
            part = ring[:, :, start : start + count * size].reshape(-1, 2, count, size)
            parts.append(jnp.swapaxes(part, 1, 2).reshape(4 * depth, -1))
            start += count * size
        return parts

    half = quarter // 2
    second = swap(second, "zh")
    feed = jnp.moveaxis(second[:, :, : 2 * eighth].reshape(2, depth, 2, -1), 2, 0)
    feed = jnp.swapaxes(swap(feed, "xl"), 0, 1).reshape(4 * depth, -1)
    parts = spread_ring(second[:, :, 2 * eighth :], ((3, half), (1, half)))
    second = jnp.concatenate(parts + [feed], axis=1)
    second, first = lax.optimization_barrier((second, first))
    first = jnp.broadcast_to(first[None], (4,) + first.shape)
    first, third = lax.optimization_barrier((first, third))
    second = lax.all_gather(second, PLANE, axis=0).reshape(2, width, -1)

    third = spread_ring(swap(third, "zh"), ((1, eighth), (1, eighth)))
    third = lax.all_gather(jnp.concatenate(third, axis=1), PLANE, axis=0).reshape(2, width, -1)

    first = exchange(first, ("y",)).reshape(4, 2, 4, 2 * depth, -1)
    first = jnp.transpose(first, (2, 0, 1, 3, 4)).reshape(1, width, -1)

    mod = modulation[0]

    def spatial_attention(normed):
        return attention_part(normed, first, quarter // 2 // head_size, head_size, 1)

    def spatial_feed(normed):
        spec = pl.BlockSpec((None, width, 4 * quarter), lambda j: (j, 0, 1))
        return feed_part(normed, second, 2, eighth // 2, [spec])

    own_frame, other_frame = gather_line(normalize(stream, mod[0], mod[1]))
    other_frame = spatial_attention(other_frame)
    update = scatter_line(spatial_attention(own_frame), other_frame)
    stream = (stream.astype(jnp.float32) + mod[2] * update).astype(jnp.bfloat16)
    own_frame, other_frame = gather_line(normalize(stream, mod[3], mod[4]))
    other_frame = spatial_feed(other_frame)
    update = scatter_line(spatial_feed(own_frame), other_frame)
    stream = (stream.astype(jnp.float32) + mod[5] * update).astype(jnp.bfloat16)

    frames = lax.axis_size(FRAME)
    stream = exchange(stream.reshape(frames, own // frames, width), FRAME).reshape(own, width)
    mod = modulation[1]
    normed = gather_pair(normalize(stream, mod[0], mod[1]))
    update = join_cores(
        attention_part(normed, second, quarter // head_size, head_size, own // frames)
    )
    stream = (stream.astype(jnp.float32) + mod[2] * update).astype(jnp.bfloat16)
    normed = gather_pair(normalize(stream, mod[3], mod[4]))
    columns = hidden // 3
    up_spec = pl.BlockSpec((None, width, columns), lambda j: (j // 3, 0, j % 3))
    down_spec = pl.BlockSpec((None, width, columns), lambda j: (j // 3, 0, 3 + j % 3))
    update = join_cores(feed_part(normed, third, 6, columns, [up_spec, down_spec]))
    stream = (stream.astype(jnp.float32) + mod[5] * update).astype(jnp.bfloat16)
    stream = product_transposed(stream, inner).astype(jnp.bfloat16)
    stream = exchange(stream.reshape(frames, own // frames, width), FRAME)
    return stream.reshape(1, own, width)


def solution(mesh):
    fine = Mesh(mesh.devices.reshape(2, 4, 4, 2, 2, 2), ("zh", "zl", "y", "xl", "xh", "c"))
    rows = ("xh", "c")
    in_specs = (
        P(FRAME, rows, None),
        P(),
        P(None, FRAME, None, rows),
        P(None, rows, FRAME),
        P(None, FRAME, rows),
        P(None, rows, FRAME),
    )
    out_specs = P(FRAME, rows, None)
    return jax.shard_map(
        on_device, mesh=fine, in_specs=in_specs, out_specs=out_specs, check_vma=False
    )
```

```python
import functools

import jax
import jax.numpy as jnp
import numpy as np
from jax import lax
from jax.experimental import pallas as pl
from jax.experimental.pallas import tpu as pltpu
from jax.sharding import Mesh, PartitionSpec as P

HEADS = 16
EPSILON = 1e-06
LINE = ("xl", "xh", "c")
RING = ("xl", "xh")
PLANE = ("zh", "zl", "y")
FRAME = ("zh", "zl", "y", "xl")


def normalize(token_sequence, shift, scale):
    values = token_sequence.astype(jnp.float32)
    center = values - jnp.mean(values, axis=-1, keepdims=True)
    spread = jnp.mean(center * center, axis=-1, keepdims=True)
    return (center * lax.rsqrt(spread + EPSILON) * (1.0 + scale) + shift).astype(jnp.bfloat16)


VMEM_LIMIT = 48 * 1024 * 1024


def product(left, right):
    return jnp.dot(left, right, preferred_element_type=jnp.float32)


def product_transposed(left, right):
    return lax.dot_general(
        left, right, (((1,), (1,)), ((), ())), preferred_element_type=jnp.float32
    )


def finish(total, kept_ref, sent_ref):
    rows = kept_ref.shape[0]
    kept_ref[...] = total[:rows]
    sent_ref[...] = total[rows:].astype(jnp.bfloat16)


def attention_kernel(heads, size, patches, x_ref, w_ref, kept_ref, sent_ref, packed, mixed, total):
    local = heads * size
    tokens = x_ref.shape[0]
    packed[...] = product(x_ref[...], w_ref[:, : 3 * local]).astype(jnp.bfloat16)
    if patches > 1:
        half = tokens // 2
        row = lax.broadcasted_iota(jnp.int32, (tokens, tokens), 0)
        column = lax.broadcasted_iota(jnp.int32, (tokens, tokens), 1)
        same = (row % patches == column % patches) & ((row < half) == (column < half))
    for head in range(heads):
        at = head * size
        query = packed[:, at : at + size]
        key = packed[:, local + at : local + at + size]
        value = packed[:, 2 * local + at : 2 * local + at + size]
        scores = product_transposed(query, key) * size ** (-0.5)
        if patches > 1:
            scores = jnp.where(same, scores, -1e30)
        raised = jnp.exp(scores - jnp.max(scores, axis=-1, keepdims=True))
        probs = raised * (1.0 / jnp.sum(raised, axis=-1, keepdims=True))
        mixed[:, at : at + size] = product(probs.astype(jnp.bfloat16), value).astype(jnp.bfloat16)
    part = product_transposed(mixed[...], w_ref[:, 3 * local : 4 * local])
    step = pl.program_id(0)
    last = pl.num_programs(0) - 1

    @pl.when(step == 0)
    def _():
        total[...] = part

    @pl.when(step > 0)
    def _():
        total[...] += part

    @pl.when(step == last)
    def _():
        finish(total[...], kept_ref, sent_ref)


def attention_part(normed, weights, heads, size, patches):
    tokens, width = normed.shape
    local = heads * size
    half = (tokens // 2, width)
    return pl.pallas_call(
        functools.partial(attention_kernel, heads, size, patches),
        grid=(weights.shape[0],),
        in_specs=[
            pl.BlockSpec((tokens, width), lambda g: (0, 0)),
            pl.BlockSpec((None, width, 4 * local), lambda g: (g, 0, 0)),
        ],
        out_specs=[pl.BlockSpec(half, lambda g: (0, 0))] * 2,
        out_shape=[
            jax.ShapeDtypeStruct(half, jnp.float32),
            jax.ShapeDtypeStruct(half, jnp.bfloat16),
        ],
        scratch_shapes=[
            pltpu.VMEM((tokens, 3 * local), jnp.bfloat16),
            pltpu.VMEM((tokens, local), jnp.bfloat16),
            pltpu.VMEM((tokens, width), jnp.float32),
        ],
        compiler_params=pltpu.CompilerParams(vmem_limit_bytes=VMEM_LIMIT),
    )(normed, weights)


def feed_kernel(x_ref, w_ref, kept_ref, sent_ref, total):
    columns = w_ref.shape[1] // 2
    hidden = product(x_ref[...], w_ref[:, :columns])
    activated = jax.nn.gelu(hidden, approximate=True).astype(jnp.bfloat16)
    part = product_transposed(activated, w_ref[:, columns:])
    step = pl.program_id(0)
    last = pl.num_programs(0) - 1

    @pl.when(step == 0)
    def _():
        total[...] = part

    @pl.when(step > 0)
    def _():
        total[...] += part

    @pl.when(step == last)
    def _():
        finish(total[...], kept_ref, sent_ref)


def feed_part(normed, weights, place):
    tokens, width = normed.shape
    half = (tokens // 2, width)
    return pl.pallas_call(
        feed_kernel,
        grid=(weights.shape[0],),
        in_specs=[
            pl.BlockSpec((tokens, width), lambda g: (0, 0)),
            pl.BlockSpec((None, width, width), lambda g: (g, 0, place)),
        ],
        out_specs=[pl.BlockSpec(half, lambda g: (0, 0))] * 2,
        out_shape=[
            jax.ShapeDtypeStruct(half, jnp.float32),
            jax.ShapeDtypeStruct(half, jnp.bfloat16),
        ],
        scratch_shapes=[pltpu.VMEM((tokens, width), jnp.float32)],
        compiler_params=pltpu.CompilerParams(vmem_limit_bytes=VMEM_LIMIT),
    )(normed, weights)


def exchange(blocks, axes):
    return lax.all_to_all(blocks, axes, split_axis=0, concat_axis=0, tiled=True)


def spread_out(block, axes):
    count = lax.axis_size(axes)
    return exchange(jnp.broadcast_to(block[None], (count,) + block.shape), axes)


def shift_ring(block, steps):
    places = [0, 2, 1, 3]
    pairs = [(places[i], places[(i + steps) % 4]) for i in range(4)]
    return lax.ppermute(block, RING, pairs)


def swap_cores(block):
    return lax.ppermute(block, "c", [(0, 1), (1, 0)])


def gather_row(normed):
    across = shift_ring(normed, 2)
    return jnp.concatenate([normed, across, swap_cores(normed), swap_cores(across)])


def gather_line(normed):
    before = shift_ring(normed, 1)
    after = shift_ring(normed, -1)
    near = jnp.concatenate([before, after])
    return gather_row(normed), jnp.concatenate([near, swap_cores(near)])


def join_cores(partial):
    kept, sent = partial
    return kept + swap_cores(sent).astype(jnp.float32)


def scatter_row(own_frame):
    own, across = jnp.split(join_cores(own_frame), 2)
    return own + shift_ring(across.astype(jnp.bfloat16), 2).astype(jnp.float32)


def scatter_line(own_frame, other_frame):
    before, after = jnp.split(join_cores(other_frame).astype(jnp.bfloat16), 2)
    before, after = shift_ring(before, -1), shift_ring(after, 1)
    return scatter_row(own_frame) + (before.astype(jnp.float32) + after.astype(jnp.float32))


def gather_pair(normed):
    return jnp.concatenate([normed, swap_cores(normed)])


def on_device(
    video,
    modulation,
    query_key_value_weight,
    attention_output_weight,
    feed_forward_up_weight,
    feed_forward_down_weight,
):
    stream = video[0]
    own, width = stream.shape
    head_size = width // HEADS
    depth, _, quarter = query_key_value_weight.shape[1:]
    hidden = feed_forward_up_weight.shape[2]
    output_rows = jnp.swapaxes(attention_output_weight, 1, 2)
    down_rows = jnp.swapaxes(feed_forward_down_weight, 1, 2)

    order = np.arange(width).reshape(2, 16, -1).swapaxes(0, 1).reshape(-1)
    inner = jnp.asarray(np.eye(width)[:, order], jnp.bfloat16)
    stream = product(stream, inner).astype(jnp.bfloat16)
    modulation = jnp.swapaxes(modulation.reshape(2, 6, 2, 16, -1), 2, 3).reshape(2, 6, width)

    def halves(rows):
        return jnp.swapaxes(rows.reshape(depth, 2, -1), 0, 1)

    def split_qkv(weight):
        parts = weight.reshape(depth, 3, 2, quarter // 2)
        return jnp.transpose(parts, (2, 0, 1, 3)).reshape(2, depth, -1)

    first = jnp.concatenate(
        [
            split_qkv(query_key_value_weight[0]),
            halves(output_rows[0]),
            halves(feed_forward_up_weight[0]),
            halves(down_rows[0]),
        ],
        axis=2,
    )
    first = jnp.broadcast_to(first[None], (8,) + first.shape).reshape(16, depth, -1)
    attention = jnp.concatenate(
        [split_qkv(query_key_value_weight[1]), halves(output_rows[1])], axis=2
    )
    feed = jnp.concatenate([halves(feed_forward_up_weight[1]), halves(down_rows[1])], axis=2)
    second = jnp.concatenate([attention, feed], axis=2)
    first, second = lax.optimization_barrier((first, second))
    first = exchange(first, ("zh", "zl", "xl")).reshape(16 * depth, -1)

    def meet(kept, met, axis):
        upper = lax.axis_index(axis) == 1
        return jnp.where(upper, jnp.stack([met, kept]), jnp.stack([kept, met]))

    upper = lax.axis_index("zh") == 1
    kept = jnp.where(upper, second[1], second[0])
    met = lax.ppermute(jnp.where(upper, second[0], second[1]), "zh", [(0, 1), (1, 0)])
    second = meet(kept, met, "zh")
    attention, feed = second[:, :, : 2 * quarter], second[:, :, 2 * quarter :]
    feed = meet(feed, lax.ppermute(feed, "xl", [(0, 1), (1, 0)]), "xl")
    feed = jnp.swapaxes(feed, 0, 1).reshape(4 * depth, -1)
    ring = jnp.stack([attention] + [shift_ring(attention, -steps) for steps in (1, 2, 3)])
    place = 2 * lax.axis_index("xh") + lax.axis_index("xl")
    ring = lax.dynamic_slice_in_dim(jnp.concatenate([ring, ring]), (4 - place) % 4, 4)
    ring = jnp.transpose(ring.reshape(2, 2, 2, depth, -1), (2, 1, 3, 0, 4))
    ring = ring.reshape(4 * depth, 2, 4, quarter // 2)
    ring = jnp.swapaxes(ring, 1, 2).reshape(4 * depth, -1)
    second = jnp.concatenate([ring, feed], axis=1)
    second, first = lax.optimization_barrier((second, first))
    second = lax.all_gather(second, PLANE, axis=0).reshape(2, width, -1)

    def spread_rows(rows):
        rows = spread_out(rows, ("y",)).reshape(4, 2, 4, 2 * depth, -1)
        return jnp.transpose(rows, (2, 0, 1, 3, 4)).reshape(1, width, -1)

    spatial_attention_weight = spread_rows(first[:, : 2 * quarter])
    rest, spatial_attention_weight = lax.optimization_barrier(
        (first[:, 2 * quarter :], spatial_attention_weight)
    )
    spatial_feed_weight = spread_rows(rest)

    mod = modulation[0]

    def spatial_attention(normed):
        return attention_part(
            normed, spatial_attention_weight, quarter // 2 // head_size, head_size, 1
        )

    def spatial_feed(normed):
        return feed_part(normed, spatial_feed_weight, 0)

    own_frame, other_frame = gather_line(normalize(stream, mod[0], mod[1]))
    other_frame = spatial_attention(other_frame)
    update = scatter_line(spatial_attention(own_frame), other_frame)
    stream = (stream.astype(jnp.float32) + mod[2] * update).astype(jnp.bfloat16)
    own_frame, other_frame = gather_line(normalize(stream, mod[3], mod[4]))
    other_frame = spatial_feed(other_frame)
    update = scatter_line(spatial_feed(own_frame), other_frame)
    stream = (stream.astype(jnp.float32) + mod[5] * update).astype(jnp.bfloat16)

    frames = lax.axis_size(FRAME)
    stream = exchange(stream.reshape(frames, own // frames, width), FRAME).reshape(own, width)
    mod = modulation[1]
    normed = gather_pair(normalize(stream, mod[0], mod[1]))
    update = join_cores(
        attention_part(normed, second, quarter // head_size, head_size, own // frames)
    )
    stream = (stream.astype(jnp.float32) + mod[2] * update).astype(jnp.bfloat16)
    own_frame = gather_row(normalize(stream, mod[3], mod[4]))
    update = scatter_row(feed_part(own_frame, second, 1))
    stream = (stream.astype(jnp.float32) + mod[5] * update).astype(jnp.bfloat16)
    stream = product_transposed(stream, inner).astype(jnp.bfloat16)
    stream = exchange(stream.reshape(frames, own // frames, width), FRAME)
    return stream.reshape(1, own, width)


def solution(mesh):
    fine = Mesh(mesh.devices.reshape(2, 4, 4, 2, 2, 2), ("zh", "zl", "y", "xl", "xh", "c"))
    rows = ("xh", "c")
    in_specs = (
        P(FRAME, rows, None),
        P(),
        P(None, FRAME, None, rows),
        P(None, rows, FRAME),
        P(None, FRAME, rows),
        P(None, rows, FRAME),
    )
    out_specs = P(FRAME, rows, None)
    return jax.shard_map(
        on_device, mesh=fine, in_specs=in_specs, out_specs=out_specs, check_vma=False
    )
```

```python
import functools

import jax
import jax.numpy as jnp
import numpy as np
from jax import lax
from jax.experimental import pallas as pl
from jax.experimental.pallas import tpu as pltpu
from jax.sharding import Mesh, PartitionSpec as P

HEADS = 16
EPSILON = 1e-06
LINE = ("xl", "xh", "c")
RING = ("xl", "xh")
PLANE = ("zh", "zl", "y")
FRAME = ("zh", "zl", "y", "xl")


def normalize(token_sequence, shift, scale):
    values = token_sequence.astype(jnp.float32)
    center = values - jnp.mean(values, axis=-1, keepdims=True)
    spread = jnp.mean(center * center, axis=-1, keepdims=True)
    return (center * lax.rsqrt(spread + EPSILON) * (1.0 + scale) + shift).astype(jnp.bfloat16)


VMEM_LIMIT = 48 * 1024 * 1024


def product(left, right):
    return jnp.dot(left, right, preferred_element_type=jnp.float32)


def product_transposed(left, right):
    return lax.dot_general(
        left, right, (((1,), (1,)), ((), ())), preferred_element_type=jnp.float32
    )


def finish(total, kept_ref, sent_ref):
    rows = kept_ref.shape[0]
    kept_ref[...] = total[:rows]
    sent_ref[...] = total[rows:].astype(jnp.bfloat16)


def attention_kernel(heads, size, patches, x_ref, w_ref, kept_ref, sent_ref, packed, mixed, total):
    local = heads * size
    tokens = x_ref.shape[0]
    packed[...] = product(x_ref[...], w_ref[:, : 3 * local]).astype(jnp.bfloat16)
    if patches > 1:
        half = tokens // 2
        row = lax.broadcasted_iota(jnp.int32, (tokens, tokens), 0)
        column = lax.broadcasted_iota(jnp.int32, (tokens, tokens), 1)
        same = (row % patches == column % patches) & ((row < half) == (column < half))
    for head in range(heads):
        at = head * size
        query = packed[:, at : at + size]
        key = packed[:, local + at : local + at + size]
        value = packed[:, 2 * local + at : 2 * local + at + size]
        scores = product_transposed(query, key) * size ** (-0.5)
        if patches > 1:
            scores = jnp.where(same, scores, -1e30)
        raised = jnp.exp(scores - jnp.max(scores, axis=-1, keepdims=True))
        probs = raised * (1.0 / jnp.sum(raised, axis=-1, keepdims=True))
        mixed[:, at : at + size] = product(probs.astype(jnp.bfloat16), value).astype(jnp.bfloat16)
    part = product_transposed(mixed[...], w_ref[:, 3 * local : 4 * local])
    step = pl.program_id(0)
    last = pl.num_programs(0) - 1

    @pl.when(step == 0)
    def _():
        total[...] = part

    @pl.when(step > 0)
    def _():
        total[...] += part

    @pl.when(step == last)
    def _():
        finish(total[...], kept_ref, sent_ref)


def attention_part(normed, weights, heads, size, patches):
    tokens, width = normed.shape
    local = heads * size
    half = (tokens // 2, width)
    return pl.pallas_call(
        functools.partial(attention_kernel, heads, size, patches),
        grid=(weights.shape[0],),
        in_specs=[
            pl.BlockSpec((tokens, width), lambda g: (0, 0)),
            pl.BlockSpec((None, width, 4 * local), lambda g: (g, 0, 0)),
        ],
        out_specs=[pl.BlockSpec(half, lambda g: (0, 0))] * 2,
        out_shape=[
            jax.ShapeDtypeStruct(half, jnp.float32),
            jax.ShapeDtypeStruct(half, jnp.bfloat16),
        ],
        scratch_shapes=[
            pltpu.VMEM((tokens, 3 * local), jnp.bfloat16),
            pltpu.VMEM((tokens, local), jnp.bfloat16),
            pltpu.VMEM((tokens, width), jnp.float32),
        ],
        compiler_params=pltpu.CompilerParams(vmem_limit_bytes=VMEM_LIMIT),
    )(normed, weights)


def feed_kernel(columns, x_ref, *refs):
    *weights, kept_ref, sent_ref, total = refs
    up_ref, down_ref = weights[0], weights[-1]
    start = columns if len(weights) == 1 else 0
    hidden = product(x_ref[...], up_ref[:, :columns])
    activated = jax.nn.gelu(hidden, approximate=True).astype(jnp.bfloat16)
    part = product_transposed(activated, down_ref[:, start : start + columns])
    step = pl.program_id(0)
    last = pl.num_programs(0) - 1

    @pl.when(step == 0)
    def _():
        total[...] = part

    @pl.when(step > 0)
    def _():
        total[...] += part

    @pl.when(step == last)
    def _():
        finish(total[...], kept_ref, sent_ref)


def feed_part(normed, weights, steps, columns, places):
    tokens, width = normed.shape
    half = (tokens // 2, width)
    specs = [
        pl.BlockSpec((None, width, width), lambda j, group=group, block=block: (j + group, 0, block))
        for group, block in places
    ]
    return pl.pallas_call(
        functools.partial(feed_kernel, columns),
        grid=(steps,),
        in_specs=[pl.BlockSpec((tokens, width), lambda j: (0, 0))] + specs,
        out_specs=[pl.BlockSpec(half, lambda j: (0, 0))] * 2,
        out_shape=[
            jax.ShapeDtypeStruct(half, jnp.float32),
            jax.ShapeDtypeStruct(half, jnp.bfloat16),
        ],
        scratch_shapes=[pltpu.VMEM((tokens, width), jnp.float32)],
        compiler_params=pltpu.CompilerParams(vmem_limit_bytes=VMEM_LIMIT),
    )(normed, *[weights] * len(specs))


def exchange(blocks, axes):
    return lax.all_to_all(blocks, axes, split_axis=0, concat_axis=0, tiled=True)


def spread_out(block, axes):
    count = lax.axis_size(axes)
    return exchange(jnp.broadcast_to(block[None], (count,) + block.shape), axes)


def shift_ring(block, steps):
    places = [0, 2, 1, 3]
    pairs = [(places[i], places[(i + steps) % 4]) for i in range(4)]
    return lax.ppermute(block, RING, pairs)


def swap_cores(block):
    return lax.ppermute(block, "c", [(0, 1), (1, 0)])


def gather_row(normed):
    across = shift_ring(normed, 2)
    return jnp.concatenate([normed, across, swap_cores(normed), swap_cores(across)])


def gather_line(normed):
    before = shift_ring(normed, 1)
    after = shift_ring(normed, -1)
    near = jnp.concatenate([before, after])
    return gather_row(normed), jnp.concatenate([near, swap_cores(near)])


def join_cores(partial):
    kept, sent = partial
    return kept + swap_cores(sent).astype(jnp.float32)


def scatter_row(own_frame):
    own, across = jnp.split(join_cores(own_frame), 2)
    return own + shift_ring(across.astype(jnp.bfloat16), 2).astype(jnp.float32)


def scatter_line(own_frame, other_frame):
    before, after = jnp.split(join_cores(other_frame).astype(jnp.bfloat16), 2)
    before, after = shift_ring(before, -1), shift_ring(after, 1)
    return scatter_row(own_frame) + (before.astype(jnp.float32) + after.astype(jnp.float32))


def gather_pair(normed):
    return jnp.concatenate([normed, swap_cores(normed)])


def on_device(
    video,
    modulation,
    query_key_value_weight,
    attention_output_weight,
    feed_forward_up_weight,
    feed_forward_down_weight,
):
    stream = video[0]
    own, width = stream.shape
    head_size = width // HEADS
    depth, _, quarter = query_key_value_weight.shape[1:]
    hidden = feed_forward_up_weight.shape[2]
    output_rows = jnp.swapaxes(attention_output_weight, 1, 2)
    down_rows = jnp.swapaxes(feed_forward_down_weight, 1, 2)

    order = np.arange(width).reshape(2, 16, -1).swapaxes(0, 1).reshape(-1)
    inner = jnp.asarray(np.eye(width)[:, order], jnp.bfloat16)
    stream = product(stream, inner).astype(jnp.bfloat16)
    modulation = jnp.swapaxes(modulation.reshape(2, 6, 2, 16, -1), 2, 3).reshape(2, 6, width)

    def halves(rows):
        return jnp.swapaxes(rows.reshape(depth, 2, -1), 0, 1)

    def split_qkv(weight):
        parts = weight.reshape(depth, 3, 2, quarter // 2)
        return jnp.transpose(parts, (2, 0, 1, 3)).reshape(2, depth, -1)

    first = jnp.concatenate([split_qkv(query_key_value_weight[0]), halves(output_rows[0])], axis=2)
    first = jnp.broadcast_to(first[None], (8,) + first.shape).reshape(16, depth, -1)
    feed = jnp.stack([feed_forward_up_weight[0], down_rows[0]])
    second = jnp.concatenate(
        [feed, split_qkv(query_key_value_weight[1]), halves(output_rows[1])], axis=2
    )
    third = jnp.concatenate([halves(feed_forward_up_weight[1]), halves(down_rows[1])], axis=2)
    first, second = lax.optimization_barrier((first, second))
    first = exchange(first, ("zh", "zl", "xl")).reshape(16 * depth, -1)

    def meet(kept, met, axis):
        upper = lax.axis_index(axis) == 1
        return jnp.where(upper, jnp.stack([met, kept]), jnp.stack([kept, met]))

    def swap(halved, axis):
        upper = lax.axis_index(axis) == 1
        sent = jnp.where(upper, halved[0], halved[1])
        kept = jnp.where(upper, halved[1], halved[0])
        return meet(kept, lax.ppermute(sent, axis, [(0, 1), (1, 0)]), axis)

    def gather_groups(rows):
        return lax.all_gather(rows, PLANE, axis=0).reshape(2, width, -1)

    second = swap(second, "zh")
    feed = jnp.moveaxis(second[:, :, :hidden].reshape(2, depth, 2, -1), 2, 0)
    feed = jnp.swapaxes(swap(feed, "xl"), 0, 1).reshape(4 * depth, -1)
    block = second[:, :, hidden:]
    ring = jnp.stack([block] + [shift_ring(block, -steps) for steps in (1, 2, 3)])
    place = 2 * lax.axis_index("xh") + lax.axis_index("xl")
    ring = lax.dynamic_slice_in_dim(jnp.concatenate([ring, ring]), (4 - place) % 4, 4)
    ring = jnp.transpose(ring.reshape(2, 2, 2, depth, -1), (2, 1, 3, 0, 4))
    ring = ring.reshape(4 * depth, 2, 4, quarter // 2)
    ring = jnp.swapaxes(ring, 1, 2).reshape(4 * depth, -1)
    second = jnp.concatenate([ring, feed], axis=1)
    second, first = lax.optimization_barrier((second, first))
    second = gather_groups(second)

    first = spread_out(first, ("y",)).reshape(4, 2, 4, 2 * depth, -1)
    first = jnp.transpose(first, (2, 0, 1, 3, 4)).reshape(1, width, -1)

    mod = modulation[0]

    def spatial_attention(normed):
        return attention_part(normed, first, quarter // 2 // head_size, head_size, 1)

    def spatial_feed(normed):
        return feed_part(normed, second, 1, hidden // 2, ((0, 1), (1, 1)))

    own_frame, other_frame = gather_line(normalize(stream, mod[0], mod[1]))
    other_frame = spatial_attention(other_frame)
    own_frame = spatial_attention(own_frame)
    third, own_frame = lax.optimization_barrier((third, own_frame))
    third = swap(third, "zh")
    third = meet(third, lax.ppermute(third, "xl", [(0, 1), (1, 0)]), "xl")
    third = gather_groups(jnp.swapaxes(third, 0, 1).reshape(4 * depth, -1))
    update = scatter_line(own_frame, other_frame)
    stream = (stream.astype(jnp.float32) + mod[2] * update).astype(jnp.bfloat16)
    own_frame, other_frame = gather_line(normalize(stream, mod[3], mod[4]))
    other_frame = spatial_feed(other_frame)
    update = scatter_line(spatial_feed(own_frame), other_frame)
    stream = (stream.astype(jnp.float32) + mod[5] * update).astype(jnp.bfloat16)

    frames = lax.axis_size(FRAME)
    stream = exchange(stream.reshape(frames, own // frames, width), FRAME).reshape(own, width)
    mod = modulation[1]
    normed = gather_pair(normalize(stream, mod[0], mod[1]))
    update = join_cores(
        attention_part(normed, second, quarter // head_size, head_size, own // frames)
    )
    stream = (stream.astype(jnp.float32) + mod[2] * update).astype(jnp.bfloat16)
    own_frame = gather_row(normalize(stream, mod[3], mod[4]))
    update = scatter_row(feed_part(own_frame, third, 2, hidden // 2, ((0, 0),)))
    stream = (stream.astype(jnp.float32) + mod[5] * update).astype(jnp.bfloat16)
    stream = product_transposed(stream, inner).astype(jnp.bfloat16)
    stream = exchange(stream.reshape(frames, own // frames, width), FRAME)
    return stream.reshape(1, own, width)


def solution(mesh):
    fine = Mesh(mesh.devices.reshape(2, 4, 4, 2, 2, 2), ("zh", "zl", "y", "xl", "xh", "c"))
    rows = ("xh", "c")
    in_specs = (
        P(FRAME, rows, None),
        P(),
        P(None, FRAME, None, rows),
        P(None, rows, FRAME),
        P(None, FRAME, rows),
        P(None, rows, FRAME),
    )
    out_specs = P(FRAME, rows, None)
    return jax.shard_map(
        on_device, mesh=fine, in_specs=in_specs, out_specs=out_specs, check_vma=False
    )
```

```python
import functools

import jax
import jax.numpy as jnp
from jax import lax
from jax.experimental import pallas as pl
from jax.experimental.pallas import tpu as pltpu
from jax.sharding import Mesh, PartitionSpec as P

HEADS = 16
EPSILON = 1e-06
LINE = ("xl", "xh", "c")
RING = ("xl", "xh")
PLANE = ("z", "y")
FRAME = ("z", "y", "xl")


def normalize(token_sequence, shift, scale):
    values = token_sequence.astype(jnp.float32)
    center = values - jnp.mean(values, axis=-1, keepdims=True)
    spread = jnp.mean(center * center, axis=-1, keepdims=True)
    return (center * lax.rsqrt(spread + EPSILON) * (1.0 + scale) + shift).astype(jnp.bfloat16)


VMEM_LIMIT = 48 * 1024 * 1024


def product(left, right):
    return jnp.dot(left, right, preferred_element_type=jnp.float32)


def product_transposed(left, right):
    return lax.dot_general(
        left, right, (((1,), (1,)), ((), ())), preferred_element_type=jnp.float32
    )


def columns_of(ref, start, stop):
    block = ref[:, :, start:stop]
    return block.reshape(block.shape[0] * block.shape[1], stop - start)


def finish(total, kept_ref, sent_ref):
    rows = kept_ref.shape[0]
    kept_ref[...] = total[:rows]
    sent_ref[...] = total[rows:].astype(jnp.bfloat16)


def attention_kernel(heads, size, patches, start, x_ref, w_ref, kept_ref, sent_ref, packed, mixed, total):
    local = heads * size
    tokens = x_ref.shape[0]
    packed[...] = product(x_ref[...], columns_of(w_ref, start, start + 3 * local)).astype(jnp.bfloat16)
    if patches > 1:
        half = tokens // 2
        row = lax.broadcasted_iota(jnp.int32, (tokens, tokens), 0)
        column = lax.broadcasted_iota(jnp.int32, (tokens, tokens), 1)
        same = (row % patches == column % patches) & ((row < half) == (column < half))
    for head in range(heads):
        at = head * size
        query = packed[:, at : at + size]
        key = packed[:, local + at : local + at + size]
        value = packed[:, 2 * local + at : 2 * local + at + size]
        scores = product_transposed(query, key) * size ** (-0.5)
        if patches > 1:
            scores = jnp.where(same, scores, -1e30)
        raised = jnp.exp(scores - jnp.max(scores, axis=-1, keepdims=True))
        probs = raised * (1.0 / jnp.sum(raised, axis=-1, keepdims=True))
        mixed[:, at : at + size] = product(probs.astype(jnp.bfloat16), value).astype(jnp.bfloat16)
    part = product_transposed(mixed[...], columns_of(w_ref, start + 3 * local, start + 4 * local))
    step = pl.program_id(0)
    last = pl.num_programs(0) - 1

    @pl.when(step == 0)
    def _():
        total[...] = part

    @pl.when(step > 0)
    def _():
        total[...] += part

    @pl.when(step == last)
    def _():
        finish(total[...], kept_ref, sent_ref)


def weight_spec(weights, columns, group):
    chunks, _, rows, _ = weights.shape
    return pl.BlockSpec((chunks, None, rows, columns), lambda j: (0, j + group, 0, 0))


def attention_part(normed, weights, heads, size, patches, start):
    tokens, width = normed.shape
    local = heads * size
    half = (tokens // 2, width)
    return pl.pallas_call(
        functools.partial(attention_kernel, heads, size, patches, start),
        grid=(weights.shape[1],),
        in_specs=[
            pl.BlockSpec((tokens, width), lambda j: (0, 0)),
            weight_spec(weights, weights.shape[3], 0),
        ],
        out_specs=[pl.BlockSpec(half, lambda j: (0, 0))] * 2,
        out_shape=[
            jax.ShapeDtypeStruct(half, jnp.float32),
            jax.ShapeDtypeStruct(half, jnp.bfloat16),
        ],
        scratch_shapes=[
            pltpu.VMEM((tokens, 3 * local), jnp.bfloat16),
            pltpu.VMEM((tokens, local), jnp.bfloat16),
            pltpu.VMEM((tokens, width), jnp.float32),
        ],
        compiler_params=pltpu.CompilerParams(vmem_limit_bytes=VMEM_LIMIT),
    )(normed, weights)


def feed_kernel(columns, x_ref, *refs):
    *weights, kept_ref, sent_ref, total = refs
    up_ref, down_ref = weights[0], weights[-1]
    start = columns if len(weights) == 1 else 0
    hidden = product(x_ref[...], columns_of(up_ref, 0, columns))
    activated = jax.nn.gelu(hidden, approximate=True).astype(jnp.bfloat16)
    part = product_transposed(activated, columns_of(down_ref, start, start + columns))
    step = pl.program_id(0)
    last = pl.num_programs(0) - 1

    @pl.when(step == 0)
    def _():
        total[...] = part

    @pl.when(step > 0)
    def _():
        total[...] += part

    @pl.when(step == last)
    def _():
        finish(total[...], kept_ref, sent_ref)


def feed_part(normed, weights, steps, columns, block, groups):
    tokens, width = normed.shape
    half = (tokens // 2, width)
    return pl.pallas_call(
        functools.partial(feed_kernel, columns),
        grid=(steps,),
        in_specs=[pl.BlockSpec((tokens, width), lambda j: (0, 0))]
        + [weight_spec(weights, block, group) for group in groups],
        out_specs=[pl.BlockSpec(half, lambda j: (0, 0))] * 2,
        out_shape=[
            jax.ShapeDtypeStruct(half, jnp.float32),
            jax.ShapeDtypeStruct(half, jnp.bfloat16),
        ],
        scratch_shapes=[pltpu.VMEM((tokens, width), jnp.float32)],
        compiler_params=pltpu.CompilerParams(vmem_limit_bytes=VMEM_LIMIT),
    )(normed, *[weights] * len(groups))


def exchange(blocks, axes):
    return lax.all_to_all(blocks, axes, split_axis=0, concat_axis=0, tiled=True)


def spread_out(block, axes):
    count = lax.axis_size(axes)
    return exchange(jnp.broadcast_to(block[None], (count,) + block.shape), axes)


def shift_ring(block, steps):
    places = [0, 2, 1, 3]
    pairs = [(places[i], places[(i + steps) % 4]) for i in range(4)]
    return lax.ppermute(block, RING, pairs)


def swap_cores(block):
    return lax.ppermute(block, "c", [(0, 1), (1, 0)])


def gather_row(normed):
    across = shift_ring(normed, 2)
    return jnp.concatenate([normed, across, swap_cores(normed), swap_cores(across)])


def gather_line(normed):
    before = shift_ring(normed, 1)
    after = shift_ring(normed, -1)
    near = jnp.concatenate([before, after])
    return gather_row(normed), jnp.concatenate([near, swap_cores(near)])


def join_cores(partial):
    kept, sent = partial
    return kept + swap_cores(sent).astype(jnp.float32)


def scatter_row(own_frame):
    own, across = jnp.split(join_cores(own_frame), 2)
    return own + shift_ring(across.astype(jnp.bfloat16), 2).astype(jnp.float32)


def scatter_line(own_frame, other_frame):
    before, after = jnp.split(join_cores(other_frame).astype(jnp.bfloat16), 2)
    before, after = shift_ring(before, -1), shift_ring(after, 1)
    return scatter_row(own_frame) + (before.astype(jnp.float32) + after.astype(jnp.float32))


def gather_pair(normed):
    return jnp.concatenate([normed, swap_cores(normed)])


def on_device(
    video,
    modulation,
    query_key_value_weight,
    attention_output_weight,
    feed_forward_up_weight,
    feed_forward_down_weight,
):
    stream = video[0]
    own, width = stream.shape
    head_size = width // HEADS
    depth, _, quarter = query_key_value_weight.shape[1:]
    hidden = feed_forward_up_weight.shape[2]
    output_rows = jnp.swapaxes(attention_output_weight, 1, 2)
    down_rows = jnp.swapaxes(feed_forward_down_weight, 1, 2)

    layers, lines = lax.axis_size("z"), lax.axis_size("y")
    eighth, local = hidden // 2, quarter // 2

    def halves(rows):
        return jnp.swapaxes(rows.reshape(depth, 2, -1), 0, 1)

    feed = jnp.concatenate([halves(feed_forward_up_weight[0]), halves(down_rows[0])], axis=2)
    feed = jnp.broadcast_to(feed[None], (lines,) + feed.shape)
    heads = jnp.concatenate(
        [
            query_key_value_weight[1].reshape(depth, 3, lines, head_size),
            output_rows[1].reshape(depth, 1, lines, head_size),
        ],
        axis=1,
    )
    heads = jnp.transpose(heads, (2, 0, 1, 3)).reshape(lines, 1, depth, -1)
    heads = jnp.broadcast_to(heads, (lines, 2) + heads.shape[2:])
    late = jnp.stack([feed_forward_up_weight[1], down_rows[1]])
    late = jnp.transpose(late.reshape(2, depth, 2, 2, eighth // 2), (0, 3, 2, 1, 4))
    late = late.reshape(lines, 2, depth, -1)
    packs = jnp.concatenate([feed, late, heads], axis=3).reshape(2 * lines, depth, -1)
    packs = exchange(packs, ("y", "xl")).reshape(2 * lines * depth, -1)
    spatial_feed_weight = lax.all_gather(packs[:, :hidden], "z", axis=0, tiled=True)
    spatial_feed_weight = spatial_feed_weight.reshape(1, 1, width, -1)

    first = query_key_value_weight[0].reshape(depth, 3, 2, local)
    first = jnp.transpose(first, (2, 0, 1, 3)).reshape(2, depth, -1)
    first = jnp.concatenate([first, halves(output_rows[0])], axis=2)
    first, packs = lax.optimization_barrier((first, packs))
    first = jnp.broadcast_to(first[None], (layers,) + first.shape)
    first = exchange(first.reshape(2 * layers, depth, -1), ("z", "xl")).reshape(
        2 * layers * depth, -1
    )

    late, heads = packs[:, hidden : hidden + eighth // 2], packs[:, hidden + eighth // 2 :]
    heads = jnp.stack([heads, lax.ppermute(heads, "xh", [(0, 1), (1, 0)])], axis=1)
    heads = jnp.swapaxes(heads.reshape(-1, 2, 4, head_size), 1, 2)
    temporal = jnp.concatenate([late, heads.reshape(late.shape[0], -1)], axis=1)
    temporal, first = lax.optimization_barrier((temporal, first))
    temporal = lax.all_gather(temporal, PLANE, axis=0)
    temporal = temporal.reshape((layers, lines) + temporal.shape[1:])

    first = spread_out(first, ("y",)).reshape(lines, layers, 2 * depth, -1)
    first = jnp.swapaxes(first, 0, 1).reshape(1, 1, width, -1)

    mod = modulation[0]

    def spatial_attention(normed):
        return attention_part(normed, first, local // head_size, head_size, 1, 0)

    def spatial_feed(normed):
        return feed_part(normed, spatial_feed_weight, 1, eighth, hidden, (0,))

    own_frame, other_frame = gather_line(normalize(stream, mod[0], mod[1]))
    other_frame = spatial_attention(other_frame)
    update = scatter_line(spatial_attention(own_frame), other_frame)
    stream = (stream.astype(jnp.float32) + mod[2] * update).astype(jnp.bfloat16)
    own_frame, other_frame = gather_line(normalize(stream, mod[3], mod[4]))
    other_frame = spatial_feed(other_frame)
    update = scatter_line(spatial_feed(own_frame), other_frame)
    stream = (stream.astype(jnp.float32) + mod[5] * update).astype(jnp.bfloat16)

    frames = lax.axis_size(FRAME)
    stream = exchange(stream.reshape(frames, own // frames, width), FRAME).reshape(own, width)
    mod = modulation[1]
    normed = gather_pair(normalize(stream, mod[0], mod[1]))
    start, block = eighth // 2, 3 * 128
    update = join_cores(
        attention_part(normed, temporal, local // head_size, head_size, own // frames, start)
    )
    stream = (stream.astype(jnp.float32) + mod[2] * update).astype(jnp.bfloat16)

    def temporal_feed(normed):
        return feed_part(normed, temporal, 2, start, block, (0, 2))

    own_frame, other_frame = gather_line(normalize(stream, mod[3], mod[4]))
    other_frame = temporal_feed(other_frame)
    update = scatter_line(temporal_feed(own_frame), other_frame)
    stream = (stream.astype(jnp.float32) + mod[5] * update).astype(jnp.bfloat16)
    stream = exchange(stream.reshape(frames, own // frames, width), FRAME)
    return stream.reshape(1, own, width)


def solution(mesh):
    fine = Mesh(mesh.devices.reshape(8, 4, 2, 2, 2), ("z", "y", "xl", "xh", "c"))
    rows = ("xh", "c")
    in_specs = (
        P(FRAME, rows, None),
        P(),
        P(None, FRAME, None, rows),
        P(None, rows, FRAME),
        P(None, FRAME, rows),
        P(None, rows, FRAME),
    )
    out_specs = P(FRAME, rows, None)
    return jax.shard_map(
        on_device, mesh=fine, in_specs=in_specs, out_specs=out_specs, check_vma=False
    )
```

```python
import functools

import jax
import jax.numpy as jnp
from jax import lax
from jax.experimental import pallas as pl
from jax.experimental.pallas import tpu as pltpu
from jax.sharding import Mesh, PartitionSpec as P

HEADS = 16
EPSILON = 1e-06
LINE = ("xl", "xh", "c")
RING = ("xl", "xh")
FRAME = ("z", "y", "xl")


def normalize(token_sequence, shift, scale):
    values = token_sequence.astype(jnp.float32)
    center = values - jnp.mean(values, axis=-1, keepdims=True)
    spread = jnp.mean(center * center, axis=-1, keepdims=True)
    return (center * lax.rsqrt(spread + EPSILON) * (1.0 + scale) + shift).astype(jnp.bfloat16)


VMEM_LIMIT = 48 * 1024 * 1024


def product(left, right):
    return jnp.dot(left, right, preferred_element_type=jnp.float32)


def product_transposed(left, right):
    return lax.dot_general(
        left, right, (((1,), (1,)), ((), ())), preferred_element_type=jnp.float32
    )


def finish(total, kept_ref, sent_ref):
    rows = kept_ref.shape[0]
    kept_ref[...] = total[:rows]
    sent_ref[...] = total[rows:].astype(jnp.bfloat16)


def attention_kernel(heads, size, patches, x_ref, *refs):
    *weights, kept_ref, sent_ref, packed, mixed = refs
    local = heads * size
    tokens = x_ref.shape[0]
    last = weights[-1].shape[1] - local
    start = 0
    for w_ref in weights:
        stop = w_ref.shape[1] if w_ref is not weights[-1] else last
        part = product(x_ref[...], w_ref[:, :stop])
        packed[:, start : start + stop] = part.astype(jnp.bfloat16)
        start += stop
    if patches > 1:
        half = tokens // 2
        row = lax.broadcasted_iota(jnp.int32, (tokens, tokens), 0)
        column = lax.broadcasted_iota(jnp.int32, (tokens, tokens), 1)
        same = (row % patches == column % patches) & ((row < half) == (column < half))
    for head in range(heads):
        at = head * size
        query = packed[:, at : at + size]
        key = packed[:, local + at : local + at + size]
        value = packed[:, 2 * local + at : 2 * local + at + size]
        scores = product_transposed(query, key) * size ** (-0.5)
        if patches > 1:
            scores = jnp.where(same, scores, -1e30)
        raised = jnp.exp(scores - jnp.max(scores, axis=-1, keepdims=True))
        probs = raised * (1.0 / jnp.sum(raised, axis=-1, keepdims=True))
        mixed[:, at : at + size] = product(probs.astype(jnp.bfloat16), value).astype(jnp.bfloat16)
    total = product_transposed(mixed[...], weights[-1][:, last:])
    finish(total, kept_ref, sent_ref)


def feed_kernel(x_ref, w_ref, kept_ref, sent_ref):
    columns = w_ref.shape[1] // 2
    hidden = product(x_ref[...], w_ref[:, :columns])
    activated = jax.nn.gelu(hidden, approximate=True).astype(jnp.bfloat16)
    finish(product_transposed(activated, w_ref[:, columns:]), kept_ref, sent_ref)


def call(kernel, normed, weights, columns, blocks, scratch):
    tokens, width = normed.shape
    half = (tokens // 2, width)
    specs = [
        pl.BlockSpec((width, columns), lambda j, block=block: (0, block)) for block in blocks
    ]
    return pl.pallas_call(
        kernel,
        grid=(1,),
        in_specs=[pl.BlockSpec((tokens, width), lambda j: (0, 0))] + specs,
        out_specs=[pl.BlockSpec(half, lambda j: (0, 0))] * 2,
        out_shape=[
            jax.ShapeDtypeStruct(half, jnp.float32),
            jax.ShapeDtypeStruct(half, jnp.bfloat16),
        ],
        scratch_shapes=scratch,
        compiler_params=pltpu.CompilerParams(vmem_limit_bytes=VMEM_LIMIT),
    )(normed, *[weights] * len(blocks))


def attention_part(normed, weights, heads, size, patches, columns, blocks):
    tokens = normed.shape[0]
    scratch = [
        pltpu.VMEM((tokens, 3 * heads * size), jnp.bfloat16),
        pltpu.VMEM((tokens, heads * size), jnp.bfloat16),
    ]
    kernel = functools.partial(attention_kernel, heads, size, patches)
    return call(kernel, normed, weights, columns, blocks, scratch)


def feed_part(normed, weights):
    return call(feed_kernel, normed, weights, normed.shape[1], (0,), [])


def exchange(blocks, axes):
    return lax.all_to_all(blocks, axes, split_axis=0, concat_axis=0, tiled=True)


def spread_out(block, axes):
    count = lax.axis_size(axes)
    return exchange(jnp.broadcast_to(block[None], (count,) + block.shape), axes)


def shift_ring(block, steps):
    places = [0, 2, 1, 3]
    pairs = [(places[i], places[(i + steps) % 4]) for i in range(4)]
    return lax.ppermute(block, RING, pairs)


def swap_cores(block):
    return lax.ppermute(block, "c", [(0, 1), (1, 0)])


def gather_line(normed):
    before = shift_ring(normed, 1)
    after = shift_ring(normed, -1)
    across = shift_ring(normed, 2)
    before, after, across = lax.optimization_barrier((before, after, across))
    near = jnp.concatenate([before, after])
    own_frame = jnp.concatenate([normed, across, swap_cores(normed), swap_cores(across)])
    return own_frame, jnp.concatenate([near, swap_cores(near)])


def join_cores(partial):
    kept, sent = partial
    return kept + swap_cores(sent).astype(jnp.float32)


def scatter_row(own_frame):
    own, across = jnp.split(join_cores(own_frame), 2)
    return own + shift_ring(across.astype(jnp.bfloat16), 2).astype(jnp.float32)


def scatter_line(own_frame, other_frame):
    before, after = jnp.split(join_cores(other_frame).astype(jnp.bfloat16), 2)
    before, after = shift_ring(before, -1), shift_ring(after, 1)
    return scatter_row(own_frame) + (before.astype(jnp.float32) + after.astype(jnp.float32))


def gather_pair(normed):
    return jnp.concatenate([normed, swap_cores(normed)])


def on_device(
    video,
    modulation,
    query_key_value_weight,
    attention_output_weight,
    feed_forward_up_weight,
    feed_forward_down_weight,
):
    stream = video[0]
    own, width = stream.shape
    head_size = width // HEADS
    depth, _, quarter = query_key_value_weight.shape[1:]
    hidden = feed_forward_up_weight.shape[2]
    output_rows = jnp.swapaxes(attention_output_weight, 1, 2)
    down_rows = jnp.swapaxes(feed_forward_down_weight, 1, 2)

    layers, lines = lax.axis_size("z"), lax.axis_size("y")
    local = quarter // 2

    def halves(rows):
        return jnp.swapaxes(rows.reshape(depth, 2, -1), 0, 1)

    feeds = [
        jnp.concatenate([halves(feed_forward_up_weight[b]), halves(down_rows[b])], axis=2)
        for b in range(2)
    ]
    heads = jnp.concatenate(
        [query_key_value_weight[1].reshape(depth, -1), output_rows[1]], axis=1
    )
    packs = jnp.concatenate(feeds + [jnp.broadcast_to(heads, (2,) + heads.shape)], axis=2)
    packs = jnp.broadcast_to(packs, (lines,) + packs.shape).reshape(2 * lines, depth, -1)
    packs = exchange(packs, ("y", "xl")).reshape(2 * lines * depth, -1)
    spatial_feed_weight = lax.all_gather(packs[:, :hidden], "z", axis=0, tiled=True)

    first = query_key_value_weight[0].reshape(depth, 3, 2, local)
    first = jnp.transpose(first, (2, 0, 1, 3)).reshape(2, depth, -1)
    first = jnp.concatenate([first, halves(output_rows[0])], axis=2)
    first, packs = lax.optimization_barrier((first, packs))
    first = jnp.broadcast_to(first[None], (layers,) + first.shape)
    first = exchange(first.reshape(2 * layers, depth, -1), ("z", "xl")).reshape(
        2 * layers * depth, -1
    )

    heads = packs[:, 2 * hidden :]
    heads = jnp.stack([heads, lax.ppermute(heads, "xh", [(0, 1), (1, 0)])], axis=1)
    heads = jnp.swapaxes(heads.reshape(-1, 2, 4, quarter), 1, 2).reshape(-1, 8 * quarter)
    temporal = jnp.concatenate([packs[:, hidden : 2 * hidden], heads], axis=1)
    temporal, first = lax.optimization_barrier((temporal, first))
    temporal = lax.all_gather(temporal, "z", axis=0, tiled=True)

    first = spread_out(first, ("y",)).reshape(lines, layers, 2 * depth, -1)
    first = jnp.swapaxes(first, 0, 1).reshape(width, -1)

    mod = modulation[0]

    def spatial_attention(normed):
        return attention_part(normed, first, local // head_size, head_size, 1, 4 * local, (0,))

    own_frame, other_frame = gather_line(normalize(stream, mod[0], mod[1]))
    other_frame = spatial_attention(other_frame)
    update = scatter_line(spatial_attention(own_frame), other_frame)
    stream = (stream.astype(jnp.float32) + mod[2] * update).astype(jnp.bfloat16)
    own_frame, other_frame = gather_line(normalize(stream, mod[3], mod[4]))
    other_frame = feed_part(other_frame, spatial_feed_weight)
    update = scatter_line(feed_part(own_frame, spatial_feed_weight), other_frame)
    stream = (stream.astype(jnp.float32) + mod[5] * update).astype(jnp.bfloat16)

    frames = lax.axis_size(FRAME)
    stream = exchange(stream.reshape(frames, own // frames, width), FRAME).reshape(own, width)
    mod = modulation[1]
    normed = gather_pair(normalize(stream, mod[0], mod[1]))
    heads = 2 * quarter // head_size
    update = join_cores(
        attention_part(normed, temporal, heads, head_size, own // frames, 4 * quarter, (1, 2))
    )
    stream = (stream.astype(jnp.float32) + mod[2] * update).astype(jnp.bfloat16)
    own_frame, other_frame = gather_line(normalize(stream, mod[3], mod[4]))
    other_frame = feed_part(other_frame, temporal)
    update = scatter_line(feed_part(own_frame, temporal), other_frame)
    stream = (stream.astype(jnp.float32) + mod[5] * update).astype(jnp.bfloat16)
    stream = exchange(stream.reshape(frames, own // frames, width), FRAME)
    return stream.reshape(1, own, width)


def solution(mesh):
    fine = Mesh(mesh.devices.reshape(8, 4, 2, 2, 2), ("z", "y", "xl", "xh", "c"))
    rows = ("xh", "c")
    in_specs = (
        P(FRAME, rows, None),
        P(),
        P(None, FRAME, None, rows),
        P(None, rows, FRAME),
        P(None, FRAME, rows),
        P(None, rows, FRAME),
    )
    out_specs = P(FRAME, rows, None)
    return jax.shard_map(
        on_device, mesh=fine, in_specs=in_specs, out_specs=out_specs, check_vma=False
    )
```

```python
import functools

import jax
import jax.numpy as jnp
from jax import lax
from jax.experimental import pallas as pl
from jax.experimental.pallas import tpu as pltpu
from jax.sharding import Mesh, PartitionSpec as P

HEADS = 16
EPSILON = 1e-06
LINE = ("xl", "xh", "c")
RING = ("xl", "xh")
FRAME = ("z", "y", "xl")


def normalize(token_sequence, shift, scale):
    values = token_sequence.astype(jnp.float32)
    center = values - jnp.mean(values, axis=-1, keepdims=True)
    spread = jnp.mean(center * center, axis=-1, keepdims=True)
    return (center * lax.rsqrt(spread + EPSILON) * (1.0 + scale) + shift).astype(jnp.bfloat16)


VMEM_LIMIT = 48 * 1024 * 1024


def product(left, right):
    return jnp.dot(left, right, preferred_element_type=jnp.float32)


def product_transposed(left, right):
    return lax.dot_general(
        left, right, (((1,), (1,)), ((), ())), preferred_element_type=jnp.float32
    )


def finish(total, kept_ref, sent_ref):
    rows = kept_ref.shape[0]
    kept_ref[...] = total[:rows]
    sent_ref[...] = total[rows:].astype(jnp.bfloat16)


def attention_kernel(heads, size, patches, x_ref, *refs):
    *weights, kept_ref, sent_ref, packed, mixed = refs
    local = heads * size
    tokens = x_ref.shape[0]
    last = weights[-1].shape[1] - local
    start = 0
    for w_ref in weights:
        stop = w_ref.shape[1] if w_ref is not weights[-1] else last
        part = product(x_ref[...], w_ref[:, :stop])
        packed[:, start : start + stop] = part.astype(jnp.bfloat16)
        start += stop
    if patches > 1:
        half = tokens // 2
        row = lax.broadcasted_iota(jnp.int32, (tokens, tokens), 0)
        column = lax.broadcasted_iota(jnp.int32, (tokens, tokens), 1)
        same = (row % patches == column % patches) & ((row < half) == (column < half))
    for head in range(heads):
        at = head * size
        query = packed[:, at : at + size]
        key = packed[:, local + at : local + at + size]
        value = packed[:, 2 * local + at : 2 * local + at + size]
        scores = product_transposed(query, key) * size ** (-0.5)
        if patches > 1:
            scores = jnp.where(same, scores, -1e30)
        raised = jnp.exp(scores - jnp.max(scores, axis=-1, keepdims=True))
        probs = raised * (1.0 / jnp.sum(raised, axis=-1, keepdims=True))
        mixed[:, at : at + size] = product(probs.astype(jnp.bfloat16), value).astype(jnp.bfloat16)
    total = product_transposed(mixed[...], weights[-1][:, last:])
    finish(total, kept_ref, sent_ref)


def feed_kernel(x_ref, w_ref, kept_ref, sent_ref):
    columns = w_ref.shape[1] // 2
    hidden = product(x_ref[...], w_ref[:, :columns])
    activated = jax.nn.gelu(hidden, approximate=True).astype(jnp.bfloat16)
    finish(product_transposed(activated, w_ref[:, columns:]), kept_ref, sent_ref)


def call(kernel, normed, weights, columns, blocks, scratch):
    tokens, width = normed.shape
    half = (tokens // 2, width)
    specs = [
        pl.BlockSpec((width, columns), lambda j, block=block: (0, block)) for block in blocks
    ]
    return pl.pallas_call(
        kernel,
        grid=(1,),
        in_specs=[pl.BlockSpec((tokens, width), lambda j: (0, 0))] + specs,
        out_specs=[pl.BlockSpec(half, lambda j: (0, 0))] * 2,
        out_shape=[
            jax.ShapeDtypeStruct(half, jnp.float32),
            jax.ShapeDtypeStruct(half, jnp.bfloat16),
        ],
        scratch_shapes=scratch,
        compiler_params=pltpu.CompilerParams(vmem_limit_bytes=VMEM_LIMIT),
    )(normed, *[weights] * len(blocks))


def attention_part(normed, weights, heads, size, patches, columns, blocks):
    tokens = normed.shape[0]
    scratch = [
        pltpu.VMEM((tokens, 3 * heads * size), jnp.bfloat16),
        pltpu.VMEM((tokens, heads * size), jnp.bfloat16),
    ]
    kernel = functools.partial(attention_kernel, heads, size, patches)
    return call(kernel, normed, weights, columns, blocks, scratch)


def feed_part(normed, weights):
    return call(feed_kernel, normed, weights, normed.shape[1], (0,), [])


def exchange(blocks, axes):
    return lax.all_to_all(blocks, axes, split_axis=0, concat_axis=0, tiled=True)


def spread_out(block, axes):
    count = lax.axis_size(axes)
    return exchange(jnp.broadcast_to(block[None], (count,) + block.shape), axes)


def shift_ring(block, steps):
    places = [0, 2, 1, 3]
    pairs = [(places[i], places[(i + steps) % 4]) for i in range(4)]
    return lax.ppermute(block, RING, pairs)


def swap_cores(block):
    return lax.ppermute(block, "c", [(0, 1), (1, 0)])


def gather_line(normed):
    before = shift_ring(normed, 1)
    after = shift_ring(normed, -1)
    across = shift_ring(normed, 2)
    near = jnp.concatenate([before, after])
    own_frame = jnp.concatenate([normed, across, swap_cores(normed), swap_cores(across)])
    return own_frame, jnp.concatenate([near, swap_cores(near)])


def join_cores(partial):
    kept, sent = partial
    return kept + swap_cores(sent).astype(jnp.float32)


def scatter_row(own_frame):
    own, across = jnp.split(join_cores(own_frame), 2)
    return own + shift_ring(across.astype(jnp.bfloat16), 2).astype(jnp.float32)


def scatter_line(own_frame, other_frame):
    before, after = jnp.split(join_cores(other_frame).astype(jnp.bfloat16), 2)
    before, after = shift_ring(before, -1), shift_ring(after, 1)
    return scatter_row(own_frame) + (before.astype(jnp.float32) + after.astype(jnp.float32))


def gather_pair(normed):
    return jnp.concatenate([normed, swap_cores(normed)])


def on_device(
    video,
    modulation,
    query_key_value_weight,
    attention_output_weight,
    feed_forward_up_weight,
    feed_forward_down_weight,
):
    stream = video[0]
    own, width = stream.shape
    head_size = width // HEADS
    depth, _, quarter = query_key_value_weight.shape[1:]
    hidden = feed_forward_up_weight.shape[2]
    output_rows = jnp.swapaxes(attention_output_weight, 1, 2)
    down_rows = jnp.swapaxes(feed_forward_down_weight, 1, 2)

    layers, lines = lax.axis_size("z"), lax.axis_size("y")
    local = quarter // 2

    def halves(rows):
        return jnp.swapaxes(rows.reshape(depth, 2, -1), 0, 1)

    feeds = [
        jnp.concatenate([halves(feed_forward_up_weight[b]), halves(down_rows[b])], axis=2)
        for b in range(2)
    ]
    packs = jnp.broadcast_to(feeds[0][None], (lines,) + feeds[0].shape)
    packs = exchange(packs.reshape(2 * lines, depth, -1), ("y", "xl")).reshape(-1, hidden)
    spatial_feed_weight = lax.all_gather(packs, "z", axis=0, tiled=True)

    first = query_key_value_weight[0].reshape(depth, 3, 2, local)
    first = jnp.transpose(first, (2, 0, 1, 3)).reshape(2, depth, -1)
    first = jnp.concatenate([first, halves(output_rows[0])], axis=2)
    first, packs = lax.optimization_barrier((first, packs))
    first = jnp.broadcast_to(first[None], (layers,) + first.shape)
    first = exchange(first.reshape(2 * layers, depth, -1), ("z", "xl")).reshape(
        2 * layers * depth, -1
    )

    heads = jnp.concatenate(
        [query_key_value_weight[1].reshape(depth, -1), output_rows[1]], axis=1
    )
    upper = lax.axis_index("xl") == 1
    kept = jnp.concatenate([jnp.where(upper, feeds[1][1], feeds[1][0]), heads], axis=1)
    sent = jnp.concatenate([jnp.where(upper, feeds[1][0], feeds[1][1]), heads], axis=1)
    met = lax.ppermute(sent, "xl", [(0, 1), (1, 0)])
    block = jnp.where(upper, jnp.stack([met, kept]), jnp.stack([kept, met]))
    turns = [block]
    for steps in range(1, lines):
        pairs = [((place + steps) % lines, place) for place in range(lines)]
        turns.append(lax.ppermute(block, "y", pairs))
    turns = jnp.stack(turns + turns)
    turns = lax.dynamic_slice_in_dim(turns, (lines - lax.axis_index("y")) % lines, lines)
    turns = turns.reshape(2 * lines * depth, -1)
    heads = turns[:, hidden:]
    heads = jnp.stack([heads, lax.ppermute(heads, "xh", [(0, 1), (1, 0)])], axis=1)
    heads = jnp.swapaxes(heads.reshape(-1, 2, 4, quarter), 1, 2).reshape(-1, 8 * quarter)
    temporal = jnp.concatenate([turns[:, :hidden], heads], axis=1)
    temporal, _ = lax.optimization_barrier((temporal, first))
    temporal = lax.all_gather(temporal, "z", axis=0, tiled=True)

    first = spread_out(first, ("y",)).reshape(lines, layers, 2 * depth, -1)
    first = jnp.swapaxes(first, 0, 1).reshape(width, -1)

    mod = modulation[0]

    def spatial_attention(normed):
        return attention_part(normed, first, local // head_size, head_size, 1, 4 * local, (0,))

    own_frame, other_frame = gather_line(normalize(stream, mod[0], mod[1]))
    other_frame = spatial_attention(other_frame)
    update = scatter_line(spatial_attention(own_frame), other_frame)
    stream = (stream.astype(jnp.float32) + mod[2] * update).astype(jnp.bfloat16)
    own_frame, other_frame = gather_line(normalize(stream, mod[3], mod[4]))
    other_frame = feed_part(other_frame, spatial_feed_weight)
    update = scatter_line(feed_part(own_frame, spatial_feed_weight), other_frame)
    stream = (stream.astype(jnp.float32) + mod[5] * update).astype(jnp.bfloat16)

    frames = lax.axis_size(FRAME)
    stream = exchange(stream.reshape(frames, own // frames, width), FRAME).reshape(own, width)
    mod = modulation[1]
    normed = gather_pair(normalize(stream, mod[0], mod[1]))
    heads = 2 * quarter // head_size
    update = join_cores(
        attention_part(normed, temporal, heads, head_size, own // frames, 4 * quarter, (1, 2))
    )
    stream = (stream.astype(jnp.float32) + mod[2] * update).astype(jnp.bfloat16)
    own_frame, other_frame = gather_line(normalize(stream, mod[3], mod[4]))
    other_frame = feed_part(other_frame, temporal)
    update = scatter_line(feed_part(own_frame, temporal), other_frame)
    stream = (stream.astype(jnp.float32) + mod[5] * update).astype(jnp.bfloat16)
    stream = exchange(stream.reshape(frames, own // frames, width), FRAME)
    return stream.reshape(1, own, width)


def solution(mesh):
    fine = Mesh(mesh.devices.reshape(8, 4, 2, 2, 2), ("z", "y", "xl", "xh", "c"))
    rows = ("xh", "c")
    in_specs = (
        P(FRAME, rows, None),
        P(),
        P(None, FRAME, None, rows),
        P(None, rows, FRAME),
        P(None, FRAME, rows),
        P(None, rows, FRAME),
    )
    out_specs = P(FRAME, rows, None)
    return jax.shard_map(
        on_device, mesh=fine, in_specs=in_specs, out_specs=out_specs, check_vma=False
    )
```

```python
import functools

import jax
import jax.numpy as jnp
from jax import lax
from jax.experimental import pallas as pl
from jax.experimental.pallas import tpu as pltpu
from jax.sharding import Mesh, PartitionSpec as P

HEADS = 16
EPSILON = 1e-06
LINE = ("xl", "xh", "c")
RING = ("xl", "xh")
FRAME = ("z", "y", "xl")


def normalize(token_sequence, shift, scale):
    values = token_sequence.astype(jnp.float32)
    center = values - jnp.mean(values, axis=-1, keepdims=True)
    spread = jnp.mean(center * center, axis=-1, keepdims=True)
    return (center * lax.rsqrt(spread + EPSILON) * (1.0 + scale) + shift).astype(jnp.bfloat16)


VMEM_LIMIT = 48 * 1024 * 1024


def product(left, right):
    return jnp.dot(left, right, preferred_element_type=jnp.float32)


def product_transposed(left, right):
    return lax.dot_general(
        left, right, (((1,), (1,)), ((), ())), preferred_element_type=jnp.float32
    )


def finish(total, kept_ref, sent_ref):
    rows = kept_ref.shape[0]
    kept_ref[...] = total[:rows]
    sent_ref[...] = total[rows:].astype(jnp.bfloat16)


def attention_kernel(heads, size, patches, x_ref, *refs):
    *weights, kept_ref, sent_ref, packed, mixed = refs
    local = heads * size
    tokens = x_ref.shape[0]
    last = weights[-1].shape[1] - local
    start = 0
    for w_ref in weights:
        stop = w_ref.shape[1] if w_ref is not weights[-1] else last
        part = product(x_ref[...], w_ref[:, :stop])
        packed[:, start : start + stop] = part.astype(jnp.bfloat16)
        start += stop
    if patches > 1:
        half = tokens // 2
        row = lax.broadcasted_iota(jnp.int32, (tokens, tokens), 0)
        column = lax.broadcasted_iota(jnp.int32, (tokens, tokens), 1)
        same = (row % patches == column % patches) & ((row < half) == (column < half))
    for head in range(heads):
        at = head * size
        query = packed[:, at : at + size]
        key = packed[:, local + at : local + at + size]
        value = packed[:, 2 * local + at : 2 * local + at + size]
        scores = product_transposed(query, key) * size ** (-0.5)
        if patches > 1:
            scores = jnp.where(same, scores, -1e30)
        raised = jnp.exp(scores - jnp.max(scores, axis=-1, keepdims=True))
        probs = raised * (1.0 / jnp.sum(raised, axis=-1, keepdims=True))
        mixed[:, at : at + size] = product(probs.astype(jnp.bfloat16), value).astype(jnp.bfloat16)
    total = product_transposed(mixed[...], weights[-1][:, last:])
    finish(total, kept_ref, sent_ref)


def feed_kernel(x_ref, up_ref, down_ref, kept_ref, sent_ref):
    hidden = product(x_ref[...], up_ref[...])
    activated = jax.nn.gelu(hidden, approximate=True).astype(jnp.bfloat16)
    finish(product_transposed(activated, down_ref[...]), kept_ref, sent_ref)


def call(kernel, normed, weights, columns, scratch):
    tokens, width = normed.shape
    half = (tokens // 2, width)
    specs = [
        pl.BlockSpec((width, columns), lambda j, block=block: (0, block)) for _, block in weights
    ]
    return pl.pallas_call(
        kernel,
        grid=(1,),
        in_specs=[pl.BlockSpec((tokens, width), lambda j: (0, 0))] + specs,
        out_specs=[pl.BlockSpec(half, lambda j: (0, 0))] * 2,
        out_shape=[
            jax.ShapeDtypeStruct(half, jnp.float32),
            jax.ShapeDtypeStruct(half, jnp.bfloat16),
        ],
        scratch_shapes=scratch,
        compiler_params=pltpu.CompilerParams(vmem_limit_bytes=VMEM_LIMIT),
    )(normed, *[array for array, _ in weights])


def attention_part(normed, weights, heads, size, patches, columns):
    tokens = normed.shape[0]
    scratch = [
        pltpu.VMEM((tokens, 3 * heads * size), jnp.bfloat16),
        pltpu.VMEM((tokens, heads * size), jnp.bfloat16),
    ]
    kernel = functools.partial(attention_kernel, heads, size, patches)
    return call(kernel, normed, weights, columns, scratch)


def feed_part(normed, up, down, columns):
    return call(feed_kernel, normed, [up, down], columns, [])


def exchange(blocks, axes):
    return lax.all_to_all(blocks, axes, split_axis=0, concat_axis=0, tiled=True)


def spread_out(block, axes):
    count = lax.axis_size(axes)
    return exchange(jnp.broadcast_to(block[None], (count,) + block.shape), axes)


def shift_ring(block, steps):
    places = [0, 2, 1, 3]
    pairs = [(places[i], places[(i + steps) % 4]) for i in range(4)]
    return lax.ppermute(block, RING, pairs)


def swap_cores(block):
    return lax.ppermute(block, "c", [(0, 1), (1, 0)])


def gather_row(normed):
    across = shift_ring(normed, 2)
    return jnp.concatenate([normed, across, swap_cores(normed), swap_cores(across)])


def gather_line(normed):
    before = shift_ring(normed, 1)
    after = shift_ring(normed, -1)
    near = jnp.concatenate([before, after])
    return gather_row(normed), jnp.concatenate([near, swap_cores(near)])


def join_cores(partial):
    kept, sent = partial
    return kept + swap_cores(sent).astype(jnp.float32)


def scatter_row(own_frame):
    own, across = jnp.split(join_cores(own_frame), 2)
    return own + shift_ring(across.astype(jnp.bfloat16), 2).astype(jnp.float32)


def scatter_line(own_frame, other_frame):
    before, after = jnp.split(join_cores(other_frame).astype(jnp.bfloat16), 2)
    before, after = shift_ring(before, -1), shift_ring(after, 1)
    return scatter_row(own_frame) + (before.astype(jnp.float32) + after.astype(jnp.float32))


def gather_pair(normed):
    return jnp.concatenate([normed, swap_cores(normed)])


def on_device(
    video,
    modulation,
    query_key_value_weight,
    attention_output_weight,
    feed_forward_up_weight,
    feed_forward_down_weight,
):
    stream = video[0]
    own, width = stream.shape
    head_size = width // HEADS
    depth, _, quarter = query_key_value_weight.shape[1:]
    hidden = feed_forward_up_weight.shape[2]
    output_rows = jnp.swapaxes(attention_output_weight, 1, 2)
    down_rows = jnp.swapaxes(feed_forward_down_weight, 1, 2)

    layers, lines = lax.axis_size("z"), lax.axis_size("y")
    local = quarter // 2

    def halves(rows):
        return jnp.swapaxes(rows.reshape(depth, 2, -1), 0, 1)

    rows = query_key_value_weight[0].reshape(depth, 3, 2, local)
    rows = jnp.transpose(rows, (2, 0, 1, 3)).reshape(2, depth, -1)
    rows = jnp.concatenate(
        [rows, halves(output_rows[0]), halves(feed_forward_up_weight[0]), halves(down_rows[0])],
        axis=2,
    )
    rows = jnp.broadcast_to(rows[None], (layers,) + rows.shape).reshape(2 * layers, depth, -1)
    pack = jnp.concatenate(
        [
            feed_forward_up_weight[1],
            down_rows[1],
            query_key_value_weight[1].reshape(depth, -1),
            output_rows[1],
        ],
        axis=1,
    )
    rows, pack = lax.optimization_barrier((rows, pack))
    rows = exchange(rows, ("z", "xl")).reshape(2 * layers * depth, -1)

    def in_order(part):
        part = part.reshape(lines, layers, 2 * depth, -1)
        return jnp.swapaxes(part, 0, 1).reshape(width, -1)

    first = spread_out(rows[:, : 2 * quarter], ("y",))
    up_rows, down_rows = jnp.split(rows[:, 2 * quarter :], 2, axis=1)
    up_rows, first = lax.optimization_barrier((up_rows, first))
    up = spread_out(up_rows, ("y",))
    down_rows, up = lax.optimization_barrier((down_rows, up))
    down = spread_out(down_rows, ("y",))
    first = in_order(first)

    upper = lax.axis_index("xl") == 1
    met = lax.ppermute(pack, "xl", [(0, 1), (1, 0)])
    block = jnp.where(upper, jnp.stack([met, pack]), jnp.stack([pack, met]))
    turns = [block]
    for steps in range(1, lines):
        pairs = [((place + steps) % lines, place) for place in range(lines)]
        turns.append(lax.ppermute(block, "y", pairs))
    turns = jnp.stack(turns + turns)
    turns = lax.dynamic_slice_in_dim(turns, (lines - lax.axis_index("y")) % lines, lines)
    turns = turns.reshape(2 * lines * depth, -1)
    heads = turns[:, 2 * hidden :]
    heads = jnp.stack([heads, lax.ppermute(heads, "xh", [(0, 1), (1, 0)])], axis=1)
    heads = jnp.swapaxes(heads.reshape(-1, 2, 4, quarter), 1, 2).reshape(-1, 8 * quarter)
    temporal = jnp.concatenate([turns[:, : 2 * hidden], heads], axis=1)
    temporal = lax.all_gather(temporal, "z", axis=0, tiled=True)

    mod = modulation[0]

    def spatial_attention(normed):
        weights = [(first, 0)]
        return attention_part(normed, weights, local // head_size, head_size, 1, 4 * local)

    def spatial_feed(normed):
        return feed_part(normed, (up, 0), (down, 0), hidden // 2)

    own_frame, other_frame = gather_line(normalize(stream, mod[0], mod[1]))
    other_frame = spatial_attention(other_frame)
    update = scatter_line(spatial_attention(own_frame), other_frame)
    update, up = lax.optimization_barrier((update, up))
    up, down = in_order(up), in_order(down)
    stream = (stream.astype(jnp.float32) + mod[2] * update).astype(jnp.bfloat16)
    own_frame, other_frame = gather_line(normalize(stream, mod[3], mod[4]))
    other_frame = spatial_feed(other_frame)
    update = scatter_line(spatial_feed(own_frame), other_frame)
    stream = (stream.astype(jnp.float32) + mod[5] * update).astype(jnp.bfloat16)

    frames = lax.axis_size(FRAME)
    stream = exchange(stream.reshape(frames, own // frames, width), FRAME).reshape(own, width)
    mod = modulation[1]
    normed = gather_pair(normalize(stream, mod[0], mod[1]))
    heads = 2 * quarter // head_size
    weights = [(temporal, 2), (temporal, 3)]
    update = join_cores(
        attention_part(normed, weights, heads, head_size, own // frames, 4 * quarter)
    )
    stream = (stream.astype(jnp.float32) + mod[2] * update).astype(jnp.bfloat16)
    own_frame = gather_row(normalize(stream, mod[3], mod[4]))
    update = scatter_row(feed_part(own_frame, (temporal, 0), (temporal, 1), hidden))
    stream = (stream.astype(jnp.float32) + mod[5] * update).astype(jnp.bfloat16)
    stream = exchange(stream.reshape(frames, own // frames, width), FRAME)
    return stream.reshape(1, own, width)


def solution(mesh):
    fine = Mesh(mesh.devices.reshape(8, 4, 2, 2, 2), ("z", "y", "xl", "xh", "c"))
    rows = ("xh", "c")
    in_specs = (
        P(FRAME, rows, None),
        P(),
        P(None, FRAME, None, rows),
        P(None, rows, FRAME),
        P(None, FRAME, rows),
        P(None, rows, FRAME),
    )
    out_specs = P(FRAME, rows, None)
    return jax.shard_map(
        on_device, mesh=fine, in_specs=in_specs, out_specs=out_specs, check_vma=False
    )
```

```python
import functools

import jax
import jax.numpy as jnp
from jax import lax
from jax.experimental import pallas as pl
from jax.experimental.pallas import tpu as pltpu
from jax.sharding import Mesh, PartitionSpec as P

HEADS = 16
EPSILON = 1e-06
LINE = ("xl", "xh", "c")
RING = ("xl", "xh")
FRAME = ("z", "y", "xl")


def normalize(token_sequence, shift, scale):
    values = token_sequence.astype(jnp.float32)
    center = values - jnp.mean(values, axis=-1, keepdims=True)
    spread = jnp.mean(center * center, axis=-1, keepdims=True)
    return (center * lax.rsqrt(spread + EPSILON) * (1.0 + scale) + shift).astype(jnp.bfloat16)


VMEM_LIMIT = 48 * 1024 * 1024


def product(left, right):
    return jnp.dot(left, right, preferred_element_type=jnp.float32)


def product_transposed(left, right):
    return lax.dot_general(
        left, right, (((1,), (1,)), ((), ())), preferred_element_type=jnp.float32
    )


def finish(total, kept_ref, sent_ref):
    rows = kept_ref.shape[0]
    kept_ref[...] = total[:rows]
    sent_ref[...] = total[rows:].astype(jnp.bfloat16)


def attention_kernel(heads, size, patches, x_ref, *refs):
    *weights, kept_ref, sent_ref, packed, mixed = refs
    local = heads * size
    tokens = x_ref.shape[0]
    last = weights[-1].shape[1] - local
    start = 0
    for w_ref in weights:
        stop = w_ref.shape[1] if w_ref is not weights[-1] else last
        part = product(x_ref[...], w_ref[:, :stop])
        packed[:, start : start + stop] = part.astype(jnp.bfloat16)
        start += stop
    if patches > 1:
        half = tokens // 2
        row = lax.broadcasted_iota(jnp.int32, (tokens, tokens), 0)
        column = lax.broadcasted_iota(jnp.int32, (tokens, tokens), 1)
        same = (row % patches == column % patches) & ((row < half) == (column < half))
    for head in range(heads):
        at = head * size
        query = packed[:, at : at + size]
        key = packed[:, local + at : local + at + size]
        value = packed[:, 2 * local + at : 2 * local + at + size]
        scores = product_transposed(query, key) * size ** (-0.5)
        if patches > 1:
            scores = jnp.where(same, scores, -1e30)
        raised = jnp.exp(scores - jnp.max(scores, axis=-1, keepdims=True))
        probs = raised * (1.0 / jnp.sum(raised, axis=-1, keepdims=True))
        mixed[:, at : at + size] = product(probs.astype(jnp.bfloat16), value).astype(jnp.bfloat16)
    total = product_transposed(mixed[...], weights[-1][:, last:])
    finish(total, kept_ref, sent_ref)


def feed_kernel(x_ref, up_ref, down_ref, kept_ref, sent_ref):
    hidden = product(x_ref[...], up_ref[...])
    activated = jax.nn.gelu(hidden, approximate=True).astype(jnp.bfloat16)
    finish(product_transposed(activated, down_ref[...]), kept_ref, sent_ref)


def call(kernel, normed, weights, columns, scratch):
    tokens, width = normed.shape
    half = (tokens // 2, width)
    specs = [
        pl.BlockSpec((width, columns), lambda j, block=block: (0, block)) for _, block in weights
    ]
    return pl.pallas_call(
        kernel,
        grid=(1,),
        in_specs=[pl.BlockSpec((tokens, width), lambda j: (0, 0))] + specs,
        out_specs=[pl.BlockSpec(half, lambda j: (0, 0))] * 2,
        out_shape=[
            jax.ShapeDtypeStruct(half, jnp.float32),
            jax.ShapeDtypeStruct(half, jnp.bfloat16),
        ],
        scratch_shapes=scratch,
        compiler_params=pltpu.CompilerParams(vmem_limit_bytes=VMEM_LIMIT),
    )(normed, *[array for array, _ in weights])


def attention_part(normed, weights, heads, size, patches, columns):
    tokens = normed.shape[0]
    scratch = [
        pltpu.VMEM((tokens, 3 * heads * size), jnp.bfloat16),
        pltpu.VMEM((tokens, heads * size), jnp.bfloat16),
    ]
    kernel = functools.partial(attention_kernel, heads, size, patches)
    return call(kernel, normed, weights, columns, scratch)


def feed_part(normed, up, down, columns):
    return call(feed_kernel, normed, [up, down], columns, [])


def exchange(blocks, axes):
    return lax.all_to_all(blocks, axes, split_axis=0, concat_axis=0, tiled=True)


def spread_out(block, axes):
    count = lax.axis_size(axes)
    return exchange(jnp.broadcast_to(block[None], (count,) + block.shape), axes)


def shift_ring(block, steps):
    places = [0, 2, 1, 3]
    pairs = [(places[i], places[(i + steps) % 4]) for i in range(4)]
    return lax.ppermute(block, RING, pairs)


def swap_cores(block):
    return lax.ppermute(block, "c", [(0, 1), (1, 0)])


def gather_row(normed):
    across = shift_ring(normed, 2)
    return jnp.concatenate([normed, across, swap_cores(normed), swap_cores(across)])


def gather_line(normed, beside):
    before = shift_ring(normed, 1)
    after = shift_ring(normed, -1)
    near, beside = lax.optimization_barrier((jnp.concatenate([before, after]), beside))
    return gather_row(normed), jnp.concatenate([near, swap_cores(near)]), beside


def join_cores(partial):
    kept, sent = partial
    return kept + swap_cores(sent).astype(jnp.float32)


def scatter_row(own_frame):
    own, across = jnp.split(join_cores(own_frame), 2)
    return own + shift_ring(across.astype(jnp.bfloat16), 2).astype(jnp.float32)


def scatter_line(own_frame, other_frame):
    before, after = jnp.split(join_cores(other_frame).astype(jnp.bfloat16), 2)
    before, after = shift_ring(before, -1), shift_ring(after, 1)
    return scatter_row(own_frame) + (before.astype(jnp.float32) + after.astype(jnp.float32))


def gather_pair(normed):
    return jnp.concatenate([normed, swap_cores(normed)])


def on_device(
    video,
    modulation,
    query_key_value_weight,
    attention_output_weight,
    feed_forward_up_weight,
    feed_forward_down_weight,
):
    stream = video[0]
    own, width = stream.shape
    head_size = width // HEADS
    depth, _, quarter = query_key_value_weight.shape[1:]
    hidden = feed_forward_up_weight.shape[2]
    output_rows = jnp.swapaxes(attention_output_weight, 1, 2)
    down_rows = jnp.swapaxes(feed_forward_down_weight, 1, 2)

    layers, lines = lax.axis_size("z"), lax.axis_size("y")
    local = quarter // 2

    def halves(rows):
        return jnp.swapaxes(rows.reshape(depth, 2, -1), 0, 1)

    rows = query_key_value_weight[0].reshape(depth, 3, 2, local)
    rows = jnp.transpose(rows, (2, 0, 1, 3)).reshape(2, depth, -1)
    rows = jnp.concatenate(
        [rows, halves(output_rows[0]), halves(feed_forward_up_weight[0]), halves(down_rows[0])],
        axis=2,
    )
    rows = jnp.broadcast_to(rows[None], (layers,) + rows.shape).reshape(2 * layers, depth, -1)
    pack = jnp.concatenate(
        [
            feed_forward_up_weight[1],
            down_rows[1],
            query_key_value_weight[1].reshape(depth, -1),
            output_rows[1],
        ],
        axis=1,
    )
    rows, pack = lax.optimization_barrier((rows, pack))
    rows = exchange(rows, ("z", "xl")).reshape(2 * layers * depth, -1)

    def in_order(part):
        part = part.reshape(lines, layers, 2 * depth, -1)
        return jnp.swapaxes(part, 0, 1).reshape(width, -1)

    first = spread_out(rows[:, : 2 * quarter], ("y",))

    upper = lax.axis_index("xl") == 1
    met = lax.ppermute(pack, "xl", [(0, 1), (1, 0)])
    block = jnp.where(upper, jnp.stack([met, pack]), jnp.stack([pack, met]))
    turns = [block]
    for steps in range(1, lines):
        pairs = [((place + steps) % lines, place) for place in range(lines)]
        turns.append(lax.ppermute(block, "y", pairs))
    turns = jnp.stack(turns + turns)
    turns = lax.dynamic_slice_in_dim(turns, (lines - lax.axis_index("y")) % lines, lines)
    turns = turns.reshape(2 * lines * depth, -1)
    heads = turns[:, 2 * hidden :]
    heads = jnp.stack([heads, lax.ppermute(heads, "xh", [(0, 1), (1, 0)])], axis=1)
    heads = jnp.swapaxes(heads.reshape(-1, 2, 4, quarter), 1, 2).reshape(-1, 8 * quarter)
    temporal = jnp.concatenate([turns[:, : 2 * hidden], heads], axis=1)
    temporal, rows = lax.optimization_barrier((temporal, rows))
    temporal = lax.all_gather(temporal, "z", axis=0, tiled=True)

    up_rows, down_rows = jnp.split(rows[:, 2 * quarter :], 2, axis=1)
    up_rows, first = lax.optimization_barrier((up_rows, first))
    up = spread_out(up_rows, ("y",))
    down_rows, up = lax.optimization_barrier((down_rows, up))
    down = spread_out(down_rows, ("y",))
    first = in_order(first)

    mod = modulation[0]

    def spatial_attention(normed):
        weights = [(first, 0)]
        return attention_part(normed, weights, local // head_size, head_size, 1, 4 * local)

    def spatial_feed(normed):
        return feed_part(normed, (up, 0), (down, 0), hidden // 2)

    own_frame, other_frame, _ = gather_line(normalize(stream, mod[0], mod[1]), ())
    other_frame = spatial_attention(other_frame)
    update = scatter_line(spatial_attention(own_frame), other_frame)
    update, up = lax.optimization_barrier((update, up))
    up = in_order(up)
    stream = (stream.astype(jnp.float32) + mod[2] * update).astype(jnp.bfloat16)
    own_frame, other_frame, down = gather_line(normalize(stream, mod[3], mod[4]), down)
    down = in_order(down)
    other_frame = spatial_feed(other_frame)
    update = scatter_line(spatial_feed(own_frame), other_frame)
    stream = (stream.astype(jnp.float32) + mod[5] * update).astype(jnp.bfloat16)

    frames = lax.axis_size(FRAME)
    stream = exchange(stream.reshape(frames, own // frames, width), FRAME).reshape(own, width)
    mod = modulation[1]
    normed = gather_pair(normalize(stream, mod[0], mod[1]))
    heads = 2 * quarter // head_size
    weights = [(temporal, 2), (temporal, 3)]
    update = join_cores(
        attention_part(normed, weights, heads, head_size, own // frames, 4 * quarter)
    )
    stream = (stream.astype(jnp.float32) + mod[2] * update).astype(jnp.bfloat16)
    own_frame = gather_row(normalize(stream, mod[3], mod[4]))
    update = scatter_row(feed_part(own_frame, (temporal, 0), (temporal, 1), hidden))
    stream = (stream.astype(jnp.float32) + mod[5] * update).astype(jnp.bfloat16)
    stream = exchange(stream.reshape(frames, own // frames, width), FRAME)
    return stream.reshape(1, own, width)


def solution(mesh):
    fine = Mesh(mesh.devices.reshape(8, 4, 2, 2, 2), ("z", "y", "xl", "xh", "c"))
    rows = ("xh", "c")
    in_specs = (
        P(FRAME, rows, None),
        P(),
        P(None, FRAME, None, rows),
        P(None, rows, FRAME),
        P(None, FRAME, rows),
        P(None, rows, FRAME),
    )
    out_specs = P(FRAME, rows, None)
    return jax.shard_map(
        on_device, mesh=fine, in_specs=in_specs, out_specs=out_specs, check_vma=False
    )
```

```python
import functools

import jax
import jax.numpy as jnp
from jax import lax
from jax.experimental import pallas as pl
from jax.experimental.pallas import tpu as pltpu
from jax.sharding import Mesh, PartitionSpec as P

HEADS = 16
EPSILON = 1e-06
LINE = ("xl", "xh", "c")
RING = ("xl", "xh")
FRAME = ("z", "y", "xl")


def normalize(token_sequence, shift, scale):
    values = token_sequence.astype(jnp.float32)
    center = values - jnp.mean(values, axis=-1, keepdims=True)
    spread = jnp.mean(center * center, axis=-1, keepdims=True)
    return (center * lax.rsqrt(spread + EPSILON) * (1.0 + scale) + shift).astype(jnp.bfloat16)


VMEM_LIMIT = 48 * 1024 * 1024


def product(left, right):
    return jnp.dot(left, right, preferred_element_type=jnp.float32)


def product_transposed(left, right):
    return lax.dot_general(
        left, right, (((1,), (1,)), ((), ())), preferred_element_type=jnp.float32
    )


def finish(total, kept_ref, sent_ref):
    rows = kept_ref.shape[0]
    kept_ref[...] = total[:rows]
    sent_ref[...] = total[rows:].astype(jnp.bfloat16)


def attention_kernel(heads, size, patches, x_ref, *refs):
    *weights, kept_ref, sent_ref, packed, mixed = refs
    local = heads * size
    tokens = x_ref.shape[0]
    last = weights[-1].shape[1] - local
    start = 0
    for w_ref in weights:
        stop = w_ref.shape[1] if w_ref is not weights[-1] else last
        part = product(x_ref[...], w_ref[:, :stop])
        packed[:, start : start + stop] = part.astype(jnp.bfloat16)
        start += stop
    if patches > 1:
        half = tokens // 2
        row = lax.broadcasted_iota(jnp.int32, (tokens, tokens), 0)
        column = lax.broadcasted_iota(jnp.int32, (tokens, tokens), 1)
        same = (row % patches == column % patches) & ((row < half) == (column < half))
    for head in range(heads):
        at = head * size
        query = packed[:, at : at + size]
        key = packed[:, local + at : local + at + size]
        value = packed[:, 2 * local + at : 2 * local + at + size]
        scores = product_transposed(query, key) * size ** (-0.5)
        if patches > 1:
            scores = jnp.where(same, scores, -1e30)
        raised = jnp.exp(scores - jnp.max(scores, axis=-1, keepdims=True))
        probs = raised * (1.0 / jnp.sum(raised, axis=-1, keepdims=True))
        mixed[:, at : at + size] = product(probs.astype(jnp.bfloat16), value).astype(jnp.bfloat16)
    total = product_transposed(mixed[...], weights[-1][:, last:])
    finish(total, kept_ref, sent_ref)


def feed_kernel(x_ref, w_ref, kept_ref, sent_ref):
    columns = w_ref.shape[1] // 2
    hidden = product(x_ref[...], w_ref[:, :columns])
    activated = jax.nn.gelu(hidden, approximate=True).astype(jnp.bfloat16)
    finish(product_transposed(activated, w_ref[:, columns:]), kept_ref, sent_ref)


def call(kernel, normed, weights, columns, blocks, scratch):
    tokens, width = normed.shape
    half = (tokens // 2, width)
    specs = [
        pl.BlockSpec((width, columns), lambda j, block=block: (0, block)) for block in blocks
    ]
    return pl.pallas_call(
        kernel,
        grid=(1,),
        in_specs=[pl.BlockSpec((tokens, width), lambda j: (0, 0))] + specs,
        out_specs=[pl.BlockSpec(half, lambda j: (0, 0))] * 2,
        out_shape=[
            jax.ShapeDtypeStruct(half, jnp.float32),
            jax.ShapeDtypeStruct(half, jnp.bfloat16),
        ],
        scratch_shapes=scratch,
        compiler_params=pltpu.CompilerParams(vmem_limit_bytes=VMEM_LIMIT),
    )(normed, *[weights] * len(blocks))


def attention_part(normed, weights, heads, size, patches, columns, blocks):
    tokens = normed.shape[0]
    scratch = [
        pltpu.VMEM((tokens, 3 * heads * size), jnp.bfloat16),
        pltpu.VMEM((tokens, heads * size), jnp.bfloat16),
    ]
    kernel = functools.partial(attention_kernel, heads, size, patches)
    return call(kernel, normed, weights, columns, blocks, scratch)


def feed_part(normed, weights):
    return call(feed_kernel, normed, weights, normed.shape[1], (0,), [])


def exchange(blocks, axes):
    return lax.all_to_all(blocks, axes, split_axis=0, concat_axis=0, tiled=True)


def spread_out(block, axes):
    count = lax.axis_size(axes)
    return exchange(jnp.broadcast_to(block[None], (count,) + block.shape), axes)


def shift_ring(block, steps):
    places = [0, 2, 1, 3]
    pairs = [(places[i], places[(i + steps) % 4]) for i in range(4)]
    return lax.ppermute(block, RING, pairs)


def swap_cores(block):
    return lax.ppermute(block, "c", [(0, 1), (1, 0)])


def gather_line(normed):
    before = shift_ring(normed, 1)
    after = shift_ring(normed, -1)
    across = shift_ring(normed, 2)
    near = jnp.concatenate([before, after])
    own_frame = jnp.concatenate([normed, across, swap_cores(normed), swap_cores(across)])
    return own_frame, jnp.concatenate([near, swap_cores(near)])


def join_cores(partial):
    kept, sent = partial
    return kept + swap_cores(sent).astype(jnp.float32)


def scatter_row(own_frame):
    own, across = jnp.split(join_cores(own_frame), 2)
    return own + shift_ring(across.astype(jnp.bfloat16), 2).astype(jnp.float32)


def scatter_line(own_frame, other_frame):
    before, after = jnp.split(join_cores(other_frame).astype(jnp.bfloat16), 2)
    before, after = shift_ring(before, -1), shift_ring(after, 1)
    return scatter_row(own_frame) + (before.astype(jnp.float32) + after.astype(jnp.float32))


def gather_pair(normed):
    return jnp.concatenate([normed, swap_cores(normed)])


def on_device(
    video,
    modulation,
    query_key_value_weight,
    attention_output_weight,
    feed_forward_up_weight,
    feed_forward_down_weight,
):
    stream = video[0]
    own, width = stream.shape
    head_size = width // HEADS
    depth, _, quarter = query_key_value_weight.shape[1:]
    hidden = feed_forward_up_weight.shape[2]
    output_rows = jnp.swapaxes(attention_output_weight, 1, 2)
    down_rows = jnp.swapaxes(feed_forward_down_weight, 1, 2)

    layers, lines = lax.axis_size("z"), lax.axis_size("y")
    local = quarter // 2

    def halves(rows):
        return jnp.swapaxes(rows.reshape(depth, 2, -1), 0, 1)

    feeds = [
        jnp.concatenate([halves(feed_forward_up_weight[b]), halves(down_rows[b])], axis=2)
        for b in range(2)
    ]
    packs = jnp.broadcast_to(feeds[0][None], (lines,) + feeds[0].shape)
    packs = exchange(packs.reshape(2 * lines, depth, -1), ("y", "xl")).reshape(-1, hidden)
    spatial_feed_weight = lax.all_gather(packs, "z", axis=0, tiled=True)

    first = query_key_value_weight[0].reshape(depth, 3, 2, local)
    first = jnp.transpose(first, (2, 0, 1, 3)).reshape(2, depth, -1)
    first = jnp.concatenate([first, halves(output_rows[0])], axis=2)
    first, packs = lax.optimization_barrier((first, packs))
    first = jnp.broadcast_to(first[None], (layers,) + first.shape)
    first = exchange(first.reshape(2 * layers, depth, -1), ("z", "xl")).reshape(
        2 * layers * depth, -1
    )

    heads = jnp.concatenate(
        [query_key_value_weight[1].reshape(depth, -1), output_rows[1]], axis=1
    )
    upper = lax.axis_index("xl") == 1
    kept = jnp.concatenate([jnp.where(upper, feeds[1][1], feeds[1][0]), heads], axis=1)
    sent = jnp.concatenate([jnp.where(upper, feeds[1][0], feeds[1][1]), heads], axis=1)
    sent, first = lax.optimization_barrier((sent, first))
    first = spread_out(first, ("y",))
    met = lax.ppermute(sent, "xl", [(0, 1), (1, 0)])
    block = jnp.where(upper, jnp.stack([met, kept]), jnp.stack([kept, met]))
    turns = [block]
    for steps in range(1, lines):
        pairs = [((place + steps) % lines, place) for place in range(lines)]
        turns.append(lax.ppermute(block, "y", pairs))
    turns = jnp.stack(turns + turns)
    turns = lax.dynamic_slice_in_dim(turns, (lines - lax.axis_index("y")) % lines, lines)
    turns = turns.reshape(2 * lines * depth, -1)
    turns, first = lax.optimization_barrier((turns, first))
    heads = turns[:, hidden:]
    heads = jnp.stack([heads, lax.ppermute(heads, "xh", [(0, 1), (1, 0)])], axis=1)
    heads = jnp.swapaxes(heads.reshape(-1, 2, 4, quarter), 1, 2).reshape(-1, 8 * quarter)
    temporal = jnp.concatenate([turns[:, :hidden], heads], axis=1)
    temporal = lax.all_gather(temporal, "z", axis=0, tiled=True)

    first = first.reshape(lines, layers, 2 * depth, -1)
    first = jnp.swapaxes(first, 0, 1).reshape(width, -1)

    mod = modulation[0]

    def spatial_attention(normed):
        return attention_part(normed, first, local // head_size, head_size, 1, 4 * local, (0,))

    own_frame, other_frame = gather_line(normalize(stream, mod[0], mod[1]))
    other_frame = spatial_attention(other_frame)
    update = scatter_line(spatial_attention(own_frame), other_frame)
    stream = (stream.astype(jnp.float32) + mod[2] * update).astype(jnp.bfloat16)
    own_frame, other_frame = gather_line(normalize(stream, mod[3], mod[4]))
    other_frame = feed_part(other_frame, spatial_feed_weight)
    update = scatter_line(feed_part(own_frame, spatial_feed_weight), other_frame)
    stream = (stream.astype(jnp.float32) + mod[5] * update).astype(jnp.bfloat16)

    frames = lax.axis_size(FRAME)
    stream = exchange(stream.reshape(frames, own // frames, width), FRAME).reshape(own, width)
    mod = modulation[1]
    normed = gather_pair(normalize(stream, mod[0], mod[1]))
    heads = 2 * quarter // head_size
    update = join_cores(
        attention_part(normed, temporal, heads, head_size, own // frames, 4 * quarter, (1, 2))
    )
    stream = (stream.astype(jnp.float32) + mod[2] * update).astype(jnp.bfloat16)
    own_frame, other_frame = gather_line(normalize(stream, mod[3], mod[4]))
    other_frame = feed_part(other_frame, temporal)
    update = scatter_line(feed_part(own_frame, temporal), other_frame)
    stream = (stream.astype(jnp.float32) + mod[5] * update).astype(jnp.bfloat16)
    stream = exchange(stream.reshape(frames, own // frames, width), FRAME)
    return stream.reshape(1, own, width)


def solution(mesh):
    fine = Mesh(mesh.devices.reshape(8, 4, 2, 2, 2), ("z", "y", "xl", "xh", "c"))
    rows = ("xh", "c")
    in_specs = (
        P(FRAME, rows, None),
        P(),
        P(None, FRAME, None, rows),
        P(None, rows, FRAME),
        P(None, FRAME, rows),
        P(None, rows, FRAME),
    )
    out_specs = P(FRAME, rows, None)
    return jax.shard_map(
        on_device, mesh=fine, in_specs=in_specs, out_specs=out_specs, check_vma=False
    )
```

```python
import functools

import jax
import jax.numpy as jnp
from jax import lax
from jax.experimental import pallas as pl
from jax.experimental.pallas import tpu as pltpu
from jax.sharding import Mesh, PartitionSpec as P

HEADS = 16
EPSILON = 1e-06
LINE = ("xl", "xh", "c")
RING = ("xl", "xh")
FRAME = ("z", "y", "xl")


def normalize(token_sequence, shift, scale):
    values = token_sequence.astype(jnp.float32)
    center = values - jnp.mean(values, axis=-1, keepdims=True)
    spread = jnp.mean(center * center, axis=-1, keepdims=True)
    return (center * lax.rsqrt(spread + EPSILON) * (1.0 + scale) + shift).astype(jnp.bfloat16)


VMEM_LIMIT = 48 * 1024 * 1024


def product(left, right):
    return jnp.dot(left, right, preferred_element_type=jnp.float32)


def product_transposed(left, right):
    return lax.dot_general(
        left, right, (((1,), (1,)), ((), ())), preferred_element_type=jnp.float32
    )


def finish(total, kept_ref, sent_ref):
    rows = kept_ref.shape[0]
    kept_ref[...] = total[:rows]
    sent_ref[...] = total[rows:].astype(jnp.bfloat16)


def attention_kernel(heads, size, patches, x_ref, *refs):
    *weights, kept_ref, sent_ref, packed, mixed = refs
    local = heads * size
    tokens = x_ref.shape[0]
    last = weights[-1].shape[1] - local
    start = 0
    for w_ref in weights:
        stop = w_ref.shape[1] if w_ref is not weights[-1] else last
        part = product(x_ref[...], w_ref[:, :stop])
        packed[:, start : start + stop] = part.astype(jnp.bfloat16)
        start += stop
    if patches > 1:
        half = tokens // 2
        row = lax.broadcasted_iota(jnp.int32, (tokens, tokens), 0)
        column = lax.broadcasted_iota(jnp.int32, (tokens, tokens), 1)
        same = (row % patches == column % patches) & ((row < half) == (column < half))
    for head in range(heads):
        at = head * size
        query = packed[:, at : at + size]
        key = packed[:, local + at : local + at + size]
        value = packed[:, 2 * local + at : 2 * local + at + size]
        scores = product_transposed(query, key) * size ** (-0.5)
        if patches > 1:
            scores = jnp.where(same, scores, -1e30)
        raised = jnp.exp(scores - jnp.max(scores, axis=-1, keepdims=True))
        probs = raised * (1.0 / jnp.sum(raised, axis=-1, keepdims=True))
        mixed[:, at : at + size] = product(probs.astype(jnp.bfloat16), value).astype(jnp.bfloat16)
    total = product_transposed(mixed[...], weights[-1][:, last:])
    finish(total, kept_ref, sent_ref)


def feed_kernel(x_ref, w_ref, kept_ref, sent_ref):
    columns = w_ref.shape[1] // 2
    hidden = product(x_ref[...], w_ref[:, :columns])
    activated = jax.nn.gelu(hidden, approximate=True).astype(jnp.bfloat16)
    finish(product_transposed(activated, w_ref[:, columns:]), kept_ref, sent_ref)


def call(kernel, normed, weights, columns, blocks, scratch):
    tokens, width = normed.shape
    half = (tokens // 2, width)
    specs = [
        pl.BlockSpec((width, columns), lambda j, block=block: (0, block)) for block in blocks
    ]
    return pl.pallas_call(
        kernel,
        grid=(1,),
        in_specs=[pl.BlockSpec((tokens, width), lambda j: (0, 0))] + specs,
        out_specs=[pl.BlockSpec(half, lambda j: (0, 0))] * 2,
        out_shape=[
            jax.ShapeDtypeStruct(half, jnp.float32),
            jax.ShapeDtypeStruct(half, jnp.bfloat16),
        ],
        scratch_shapes=scratch,
        compiler_params=pltpu.CompilerParams(vmem_limit_bytes=VMEM_LIMIT),
    )(normed, *[weights] * len(blocks))


def attention_part(normed, weights, heads, size, patches, columns, blocks):
    tokens = normed.shape[0]
    scratch = [
        pltpu.VMEM((tokens, 3 * heads * size), jnp.bfloat16),
        pltpu.VMEM((tokens, heads * size), jnp.bfloat16),
    ]
    kernel = functools.partial(attention_kernel, heads, size, patches)
    return call(kernel, normed, weights, columns, blocks, scratch)


def feed_part(normed, weights):
    return call(feed_kernel, normed, weights, normed.shape[1], (0,), [])


def exchange(blocks, axes):
    return lax.all_to_all(blocks, axes, split_axis=0, concat_axis=0, tiled=True)


def spread_out(block, axes):
    count = lax.axis_size(axes)
    return exchange(jnp.broadcast_to(block[None], (count,) + block.shape), axes)


def shift_ring(block, steps):
    places = [0, 2, 1, 3]
    pairs = [(places[i], places[(i + steps) % 4]) for i in range(4)]
    return lax.ppermute(block, RING, pairs)


def swap_cores(block):
    return lax.ppermute(block, "c", [(0, 1), (1, 0)])


def gather_line(normed):
    before = shift_ring(normed, 1)
    after = shift_ring(normed, -1)
    across = shift_ring(normed, 2)
    near = jnp.concatenate([before, after])
    own_frame = jnp.concatenate([normed, across, swap_cores(normed), swap_cores(across)])
    return own_frame, jnp.concatenate([near, swap_cores(near)])


def join_cores(partial):
    kept, sent = partial
    return kept + swap_cores(sent).astype(jnp.float32)


def scatter_row(own_frame):
    own, across = jnp.split(join_cores(own_frame), 2)
    return own + shift_ring(across.astype(jnp.bfloat16), 2).astype(jnp.float32)


def scatter_line(own_frame, other_frame):
    before, after = jnp.split(join_cores(other_frame).astype(jnp.bfloat16), 2)
    before, after = shift_ring(before, -1), shift_ring(after, 1)
    return scatter_row(own_frame) + (before.astype(jnp.float32) + after.astype(jnp.float32))


def gather_pair(normed):
    return jnp.concatenate([normed, swap_cores(normed)])


def on_device(
    video,
    modulation,
    query_key_value_weight,
    attention_output_weight,
    feed_forward_up_weight,
    feed_forward_down_weight,
):
    stream = video[0]
    own, width = stream.shape
    head_size = width // HEADS
    depth, _, quarter = query_key_value_weight.shape[1:]
    hidden = feed_forward_up_weight.shape[2]
    output_rows = jnp.swapaxes(attention_output_weight, 1, 2)
    down_rows = jnp.swapaxes(feed_forward_down_weight, 1, 2)

    layers, lines = lax.axis_size("z"), lax.axis_size("y")
    local = quarter // 2

    def halves(rows):
        return jnp.swapaxes(rows.reshape(depth, 2, -1), 0, 1)

    feeds = [
        jnp.concatenate([halves(feed_forward_up_weight[b]), halves(down_rows[b])], axis=2)
        for b in range(2)
    ]
    packs = jnp.broadcast_to(feeds[0][None], (lines,) + feeds[0].shape)
    packs = exchange(packs.reshape(2 * lines, depth, -1), ("y", "xl")).reshape(-1, hidden)
    spatial_feed_weight = lax.all_gather(packs, "z", axis=0, tiled=True)

    first = query_key_value_weight[0].reshape(depth, 3, 2, local)
    first = jnp.transpose(first, (2, 0, 1, 3)).reshape(2, depth, -1)
    first = jnp.concatenate([first, halves(output_rows[0])], axis=2)
    first, packs = lax.optimization_barrier((first, packs))
    first = jnp.broadcast_to(first[None], (layers,) + first.shape)
    first = exchange(first.reshape(2 * layers, depth, -1), ("z", "xl")).reshape(
        2 * layers * depth, -1
    )

    heads = jnp.concatenate(
        [query_key_value_weight[1].reshape(depth, -1), output_rows[1]], axis=1
    )
    upper = lax.axis_index("xl") == 1
    kept = jnp.concatenate([jnp.where(upper, feeds[1][1], feeds[1][0]), heads], axis=1)
    sent = jnp.concatenate([jnp.where(upper, feeds[1][0], feeds[1][1]), heads], axis=1)
    first = spread_out(first, ("y",))
    met = lax.ppermute(sent, "xl", [(0, 1), (1, 0)])
    block = jnp.where(upper, jnp.stack([met, kept]), jnp.stack([kept, met]))
    turns = [block]
    for steps in range(1, lines):
        pairs = [((place + steps) % lines, place) for place in range(lines)]
        turns.append(lax.ppermute(block, "y", pairs))
    turns = jnp.stack(turns + turns)
    turns = lax.dynamic_slice_in_dim(turns, (lines - lax.axis_index("y")) % lines, lines)
    turns = turns.reshape(2 * lines * depth, -1)
    heads = turns[:, hidden:]
    heads = jnp.stack([heads, lax.ppermute(heads, "xh", [(0, 1), (1, 0)])], axis=1)
    heads = jnp.swapaxes(heads.reshape(-1, 2, 4, quarter), 1, 2).reshape(-1, 8 * quarter)
    temporal = jnp.concatenate([turns[:, :hidden], heads], axis=1)
    mod = modulation[0]
    own_frame, other_frame = gather_line(normalize(stream, mod[0], mod[1]))
    temporal, first, own_frame, other_frame = lax.optimization_barrier(
        (temporal, first, own_frame, other_frame)
    )
    temporal = lax.all_gather(temporal, "z", axis=0, tiled=True)

    first = first.reshape(lines, layers, 2 * depth, -1)
    first = jnp.swapaxes(first, 0, 1).reshape(width, -1)


    def spatial_attention(normed):
        return attention_part(normed, first, local // head_size, head_size, 1, 4 * local, (0,))

    other_frame = spatial_attention(other_frame)
    update = scatter_line(spatial_attention(own_frame), other_frame)
    stream = (stream.astype(jnp.float32) + mod[2] * update).astype(jnp.bfloat16)
    own_frame, other_frame = gather_line(normalize(stream, mod[3], mod[4]))
    other_frame = feed_part(other_frame, spatial_feed_weight)
    update = scatter_line(feed_part(own_frame, spatial_feed_weight), other_frame)
    stream = (stream.astype(jnp.float32) + mod[5] * update).astype(jnp.bfloat16)

    frames = lax.axis_size(FRAME)
    stream = exchange(stream.reshape(frames, own // frames, width), FRAME).reshape(own, width)
    mod = modulation[1]
    normed = gather_pair(normalize(stream, mod[0], mod[1]))
    heads = 2 * quarter // head_size
    update = join_cores(
        attention_part(normed, temporal, heads, head_size, own // frames, 4 * quarter, (1, 2))
    )
    stream = (stream.astype(jnp.float32) + mod[2] * update).astype(jnp.bfloat16)
    own_frame, other_frame = gather_line(normalize(stream, mod[3], mod[4]))
    other_frame = feed_part(other_frame, temporal)
    update = scatter_line(feed_part(own_frame, temporal), other_frame)
    stream = (stream.astype(jnp.float32) + mod[5] * update).astype(jnp.bfloat16)
    stream = exchange(stream.reshape(frames, own // frames, width), FRAME)
    return stream.reshape(1, own, width)


def solution(mesh):
    fine = Mesh(mesh.devices.reshape(8, 4, 2, 2, 2), ("z", "y", "xl", "xh", "c"))
    rows = ("xh", "c")
    in_specs = (
        P(FRAME, rows, None),
        P(),
        P(None, FRAME, None, rows),
        P(None, rows, FRAME),
        P(None, FRAME, rows),
        P(None, rows, FRAME),
    )
    out_specs = P(FRAME, rows, None)
    return jax.shard_map(
        on_device, mesh=fine, in_specs=in_specs, out_specs=out_specs, check_vma=False
    )
```

```python
import functools

import jax
import jax.numpy as jnp
from jax import lax
from jax.experimental import pallas as pl
from jax.experimental.pallas import tpu as pltpu
from jax.sharding import Mesh, PartitionSpec as P

HEADS = 16
EPSILON = 1e-06
LINE = ("xl", "xh", "c")
RING = ("xl", "xh")
PLANE = ("z", "y")
FRAME = ("z", "y", "xl")


def normalize(token_sequence, shift, scale):
    values = token_sequence.astype(jnp.float32)
    center = values - jnp.mean(values, axis=-1, keepdims=True)
    spread = jnp.mean(center * center, axis=-1, keepdims=True)
    return (center * lax.rsqrt(spread + EPSILON) * (1.0 + scale) + shift).astype(jnp.bfloat16)


VMEM_LIMIT = 48 * 1024 * 1024


def product(left, right):
    return jnp.dot(left, right, preferred_element_type=jnp.float32)


def product_transposed(left, right):
    return lax.dot_general(
        left, right, (((1,), (1,)), ((), ())), preferred_element_type=jnp.float32
    )


def columns_of(ref, start, stop):
    block = ref[:, :, start:stop]
    return block.reshape(block.shape[0] * block.shape[1], stop - start)


def finish(total, kept_ref, sent_ref):
    rows = kept_ref.shape[0]
    kept_ref[...] = total[:rows]
    sent_ref[...] = total[rows:].astype(jnp.bfloat16)


def attention_kernel(heads, size, patches, start, x_ref, w_ref, kept_ref, sent_ref, packed, mixed, total):
    local = heads * size
    tokens = x_ref.shape[0]
    packed[...] = product(x_ref[...], columns_of(w_ref, start, start + 3 * local)).astype(jnp.bfloat16)
    if patches > 1:
        half = tokens // 2
        row = lax.broadcasted_iota(jnp.int32, (tokens, tokens), 0)
        column = lax.broadcasted_iota(jnp.int32, (tokens, tokens), 1)
        same = (row % patches == column % patches) & ((row < half) == (column < half))
    for head in range(heads):
        at = head * size
        query = packed[:, at : at + size]
        key = packed[:, local + at : local + at + size]
        value = packed[:, 2 * local + at : 2 * local + at + size]
        scores = product_transposed(query, key) * size ** (-0.5)
        if patches > 1:
            scores = jnp.where(same, scores, -1e30)
        raised = jnp.exp(scores - jnp.max(scores, axis=-1, keepdims=True))
        probs = raised * (1.0 / jnp.sum(raised, axis=-1, keepdims=True))
        mixed[:, at : at + size] = product(probs.astype(jnp.bfloat16), value).astype(jnp.bfloat16)
    part = product_transposed(mixed[...], columns_of(w_ref, start + 3 * local, start + 4 * local))
    step = pl.program_id(0)
    last = pl.num_programs(0) - 1

    @pl.when(step == 0)
    def _():
        total[...] = part

    @pl.when(step > 0)
    def _():
        total[...] += part

    @pl.when(step == last)
    def _():
        finish(total[...], kept_ref, sent_ref)


def weight_spec(weights, columns, group):
    chunks, _, rows, _ = weights.shape
    return pl.BlockSpec((chunks, None, rows, columns), lambda j: (0, j + group, 0, 0))


def attention_part(normed, weights, heads, size, patches, start):
    tokens, width = normed.shape
    local = heads * size
    half = (tokens // 2, width)
    return pl.pallas_call(
        functools.partial(attention_kernel, heads, size, patches, start),
        grid=(weights.shape[1],),
        in_specs=[
            pl.BlockSpec((tokens, width), lambda j: (0, 0)),
            weight_spec(weights, weights.shape[3], 0),
        ],
        out_specs=[pl.BlockSpec(half, lambda j: (0, 0))] * 2,
        out_shape=[
            jax.ShapeDtypeStruct(half, jnp.float32),
            jax.ShapeDtypeStruct(half, jnp.bfloat16),
        ],
        scratch_shapes=[
            pltpu.VMEM((tokens, 3 * local), jnp.bfloat16),
            pltpu.VMEM((tokens, local), jnp.bfloat16),
            pltpu.VMEM((tokens, width), jnp.float32),
        ],
        compiler_params=pltpu.CompilerParams(vmem_limit_bytes=VMEM_LIMIT),
    )(normed, weights)


def feed_kernel(columns, x_ref, *refs):
    *weights, kept_ref, sent_ref, total = refs
    up_ref, down_ref = weights[0], weights[-1]
    start = columns if len(weights) == 1 else 0
    hidden = product(x_ref[...], columns_of(up_ref, 0, columns))
    activated = jax.nn.gelu(hidden, approximate=True).astype(jnp.bfloat16)
    part = product_transposed(activated, columns_of(down_ref, start, start + columns))
    step = pl.program_id(0)
    last = pl.num_programs(0) - 1

    @pl.when(step == 0)
    def _():
        total[...] = part

    @pl.when(step > 0)
    def _():
        total[...] += part

    @pl.when(step == last)
    def _():
        finish(total[...], kept_ref, sent_ref)


def feed_part(normed, weights, steps, columns, block, groups):
    tokens, width = normed.shape
    half = (tokens // 2, width)
    return pl.pallas_call(
        functools.partial(feed_kernel, columns),
        grid=(steps,),
        in_specs=[pl.BlockSpec((tokens, width), lambda j: (0, 0))]
        + [weight_spec(weights, block, group) for group in groups],
        out_specs=[pl.BlockSpec(half, lambda j: (0, 0))] * 2,
        out_shape=[
            jax.ShapeDtypeStruct(half, jnp.float32),
            jax.ShapeDtypeStruct(half, jnp.bfloat16),
        ],
        scratch_shapes=[pltpu.VMEM((tokens, width), jnp.float32)],
        compiler_params=pltpu.CompilerParams(vmem_limit_bytes=VMEM_LIMIT),
    )(normed, *[weights] * len(groups))


def line_up_kernel(in_ref, out_ref):
    groups, columns = in_ref.shape[0], out_ref.shape[1] // in_ref.shape[0]
    for group in range(groups):
        at = group * columns
        out_ref[:, at : at + columns] = in_ref[group, :, :columns]


def line_up(weights, width, columns, block):
    chunks, groups, rows, _ = weights.shape
    return pl.pallas_call(
        line_up_kernel,
        grid=(chunks,),
        in_specs=[pl.BlockSpec((None, groups, rows, block), lambda j: (j, 0, 0, 0))],
        out_specs=pl.BlockSpec((rows, groups * columns), lambda j: (j, 0)),
        out_shape=jax.ShapeDtypeStruct((width, groups * columns), weights.dtype),
    )(weights)


def exchange(blocks, axes):
    return lax.all_to_all(blocks, axes, split_axis=0, concat_axis=0, tiled=True)


def spread_out(block, axes):
    count = lax.axis_size(axes)
    return exchange(jnp.broadcast_to(block[None], (count,) + block.shape), axes)


def shift_ring(block, steps):
    places = [0, 2, 1, 3]
    pairs = [(places[i], places[(i + steps) % 4]) for i in range(4)]
    return lax.ppermute(block, RING, pairs)


def swap_cores(block):
    return lax.ppermute(block, "c", [(0, 1), (1, 0)])


def gather_row(normed):
    across = shift_ring(normed, 2)
    return jnp.concatenate([normed, across, swap_cores(normed), swap_cores(across)])


def gather_line(normed):
    before = shift_ring(normed, 1)
    after = shift_ring(normed, -1)
    near = jnp.concatenate([before, after])
    return gather_row(normed), jnp.concatenate([near, swap_cores(near)])


def join_cores(partial):
    kept, sent = partial
    return kept + swap_cores(sent).astype(jnp.float32)


def scatter_row(own_frame):
    own, across = jnp.split(join_cores(own_frame), 2)
    return own + shift_ring(across.astype(jnp.bfloat16), 2).astype(jnp.float32)


def scatter_line(own_frame, other_frame):
    before, after = jnp.split(join_cores(other_frame).astype(jnp.bfloat16), 2)
    before, after = shift_ring(before, -1), shift_ring(after, 1)
    return scatter_row(own_frame) + (before.astype(jnp.float32) + after.astype(jnp.float32))


def gather_pair(normed):
    return jnp.concatenate([normed, swap_cores(normed)])


def on_device(
    video,
    modulation,
    query_key_value_weight,
    attention_output_weight,
    feed_forward_up_weight,
    feed_forward_down_weight,
):
    stream = video[0]
    own, width = stream.shape
    head_size = width // HEADS
    depth, _, quarter = query_key_value_weight.shape[1:]
    hidden = feed_forward_up_weight.shape[2]
    output_rows = jnp.swapaxes(attention_output_weight, 1, 2)
    down_rows = jnp.swapaxes(feed_forward_down_weight, 1, 2)

    layers, lines = lax.axis_size("z"), lax.axis_size("y")
    eighth, local = hidden // 2, quarter // 2

    def halves(rows):
        return jnp.swapaxes(rows.reshape(depth, 2, -1), 0, 1)

    feed = jnp.concatenate([halves(feed_forward_up_weight[0]), halves(down_rows[0])], axis=2)
    feed = jnp.broadcast_to(feed[None], (lines,) + feed.shape)
    heads = jnp.concatenate(
        [
            query_key_value_weight[1].reshape(depth, 3, lines, head_size),
            output_rows[1].reshape(depth, 1, lines, head_size),
        ],
        axis=1,
    )
    heads = jnp.transpose(heads, (2, 0, 1, 3)).reshape(lines, 1, depth, -1)
    heads = jnp.broadcast_to(heads, (lines, 2) + heads.shape[2:])
    late = jnp.stack([feed_forward_up_weight[1], down_rows[1]])
    late = jnp.transpose(late.reshape(2, depth, 2, 2, eighth // 2), (0, 3, 2, 1, 4))
    late = late.reshape(lines, 2, depth, -1)
    packs = jnp.concatenate([feed, late, heads], axis=3).reshape(2 * lines, depth, -1)
    packs = exchange(packs, ("y", "xl")).reshape(2 * lines * depth, -1)
    spatial_feed_weight = lax.all_gather(packs[:, :hidden], "z", axis=0, tiled=True)
    spatial_feed_weight = spatial_feed_weight.reshape(1, 1, width, -1)

    first = query_key_value_weight[0].reshape(depth, 3, 2, local)
    first = jnp.transpose(first, (2, 0, 1, 3)).reshape(2, depth, -1)
    first = jnp.concatenate([first, halves(output_rows[0])], axis=2)
    first, packs = lax.optimization_barrier((first, packs))
    first = jnp.broadcast_to(first[None], (layers,) + first.shape)
    first = exchange(first.reshape(2 * layers, depth, -1), ("z", "xl")).reshape(
        2 * layers * depth, -1
    )

    late, heads = packs[:, hidden : hidden + eighth // 2], packs[:, hidden + eighth // 2 :]
    heads = jnp.stack([heads, lax.ppermute(heads, "xh", [(0, 1), (1, 0)])], axis=1)
    heads = jnp.swapaxes(heads.reshape(-1, 2, 4, head_size), 1, 2)
    temporal = jnp.concatenate([late, heads.reshape(late.shape[0], -1)], axis=1)
    temporal, first = lax.optimization_barrier((temporal, first))
    temporal = lax.all_gather(temporal, PLANE, axis=0)
    temporal = temporal.reshape((layers, lines) + temporal.shape[1:])

    first = spread_out(first, ("y",)).reshape(lines, layers, 2 * depth, -1)
    first = jnp.swapaxes(first, 0, 1).reshape(1, 1, width, -1)

    mod = modulation[0]

    def spatial_attention(normed):
        return attention_part(normed, first, local // head_size, head_size, 1, 0)

    def spatial_feed(normed):
        return feed_part(normed, spatial_feed_weight, 1, eighth, hidden, (0,))

    own_frame, other_frame = gather_line(normalize(stream, mod[0], mod[1]))
    other_frame = spatial_attention(other_frame)
    update = scatter_line(spatial_attention(own_frame), other_frame)
    stream = (stream.astype(jnp.float32) + mod[2] * update).astype(jnp.bfloat16)
    own_frame, other_frame = gather_line(normalize(stream, mod[3], mod[4]))
    other_frame = spatial_feed(other_frame)
    update = scatter_line(spatial_feed(own_frame), other_frame)
    stream = (stream.astype(jnp.float32) + mod[5] * update).astype(jnp.bfloat16)

    frames = lax.axis_size(FRAME)
    stream = exchange(stream.reshape(frames, own // frames, width), FRAME).reshape(own, width)
    mod = modulation[1]
    normed = gather_pair(normalize(stream, mod[0], mod[1]))
    start, block = eighth // 2, 3 * 128
    update = join_cores(
        attention_part(normed, temporal, local // head_size, head_size, own // frames, start)
    )
    stream = (stream.astype(jnp.float32) + mod[2] * update).astype(jnp.bfloat16)

    temporal_feed_weight = line_up(temporal, width, start, block).reshape(1, 1, width, -1)

    def temporal_feed(normed):
        return feed_part(normed, temporal_feed_weight, 1, eighth, hidden, (0,))

    own_frame, other_frame = gather_line(normalize(stream, mod[3], mod[4]))
    other_frame = temporal_feed(other_frame)
    update = scatter_line(temporal_feed(own_frame), other_frame)
    stream = (stream.astype(jnp.float32) + mod[5] * update).astype(jnp.bfloat16)
    stream = exchange(stream.reshape(frames, own // frames, width), FRAME)
    return stream.reshape(1, own, width)


def solution(mesh):
    fine = Mesh(mesh.devices.reshape(8, 4, 2, 2, 2), ("z", "y", "xl", "xh", "c"))
    rows = ("xh", "c")
    in_specs = (
        P(FRAME, rows, None),
        P(),
        P(None, FRAME, None, rows),
        P(None, rows, FRAME),
        P(None, FRAME, rows),
        P(None, rows, FRAME),
    )
    out_specs = P(FRAME, rows, None)
    return jax.shard_map(
        on_device, mesh=fine, in_specs=in_specs, out_specs=out_specs, check_vma=False
    )
```

```python
import functools

import jax
import jax.numpy as jnp
from jax import lax
from jax.experimental import pallas as pl
from jax.experimental.pallas import tpu as pltpu
from jax.sharding import Mesh, PartitionSpec as P

HEADS = 16
EPSILON = 1e-06
LINE = ("xl", "xh", "c")
RING = ("xl", "xh")
PLANE = ("z", "y")
FRAME = ("z", "y", "xl")


def normalize(token_sequence, shift, scale):
    values = token_sequence.astype(jnp.float32)
    center = values - jnp.mean(values, axis=-1, keepdims=True)
    spread = jnp.mean(center * center, axis=-1, keepdims=True)
    return (center * lax.rsqrt(spread + EPSILON) * (1.0 + scale) + shift).astype(jnp.bfloat16)


VMEM_LIMIT = 48 * 1024 * 1024


def product(left, right):
    return jnp.dot(left, right, preferred_element_type=jnp.float32)


def product_transposed(left, right):
    return lax.dot_general(
        left, right, (((1,), (1,)), ((), ())), preferred_element_type=jnp.float32
    )


def columns_of(ref, start, stop):
    block = ref[:, :, start:stop]
    return block.reshape(block.shape[0] * block.shape[1], stop - start)


def finish(total, kept_ref, sent_ref):
    rows = kept_ref.shape[0]
    kept_ref[...] = total[:rows]
    sent_ref[...] = total[rows:].astype(jnp.bfloat16)


def attention_kernel(heads, size, patches, start, x_ref, w_ref, kept_ref, sent_ref, packed, mixed, total):
    local = heads * size
    tokens = x_ref.shape[0]
    packed[...] = product(x_ref[...], columns_of(w_ref, start, start + 3 * local)).astype(jnp.bfloat16)
    if patches > 1:
        half = tokens // 2
        row = lax.broadcasted_iota(jnp.int32, (tokens, tokens), 0)
        column = lax.broadcasted_iota(jnp.int32, (tokens, tokens), 1)
        same = (row % patches == column % patches) & ((row < half) == (column < half))
    for head in range(heads):
        at = head * size
        query = packed[:, at : at + size]
        key = packed[:, local + at : local + at + size]
        value = packed[:, 2 * local + at : 2 * local + at + size]
        scores = product_transposed(query, key) * size ** (-0.5)
        if patches > 1:
            scores = jnp.where(same, scores, -1e30)
        raised = jnp.exp(scores - jnp.max(scores, axis=-1, keepdims=True))
        probs = raised * (1.0 / jnp.sum(raised, axis=-1, keepdims=True))
        mixed[:, at : at + size] = product(probs.astype(jnp.bfloat16), value).astype(jnp.bfloat16)
    part = product_transposed(mixed[...], columns_of(w_ref, start + 3 * local, start + 4 * local))
    step = pl.program_id(0)
    last = pl.num_programs(0) - 1

    @pl.when(step == 0)
    def _():
        total[...] = part

    @pl.when(step > 0)
    def _():
        total[...] += part

    @pl.when(step == last)
    def _():
        finish(total[...], kept_ref, sent_ref)


def weight_spec(weights, columns, group):
    chunks, _, rows, _ = weights.shape
    return pl.BlockSpec((chunks, None, rows, columns), lambda j: (0, j + group, 0, 0))


def attention_part(normed, weights, heads, size, patches, start):
    tokens, width = normed.shape
    local = heads * size
    half = (tokens // 2, width)
    return pl.pallas_call(
        functools.partial(attention_kernel, heads, size, patches, start),
        grid=(weights.shape[1],),
        in_specs=[
            pl.BlockSpec((tokens, width), lambda j: (0, 0)),
            weight_spec(weights, weights.shape[3], 0),
        ],
        out_specs=[pl.BlockSpec(half, lambda j: (0, 0))] * 2,
        out_shape=[
            jax.ShapeDtypeStruct(half, jnp.float32),
            jax.ShapeDtypeStruct(half, jnp.bfloat16),
        ],
        scratch_shapes=[
            pltpu.VMEM((tokens, 3 * local), jnp.bfloat16),
            pltpu.VMEM((tokens, local), jnp.bfloat16),
            pltpu.VMEM((tokens, width), jnp.float32),
        ],
        compiler_params=pltpu.CompilerParams(vmem_limit_bytes=VMEM_LIMIT),
    )(normed, weights)


def feed_kernel(columns, x_ref, *refs):
    *weights, kept_ref, sent_ref, total = refs
    up_ref, down_ref = weights[0], weights[-1]
    start = columns if len(weights) == 1 else 0
    hidden = product(x_ref[...], columns_of(up_ref, 0, columns))
    activated = jax.nn.gelu(hidden, approximate=True).astype(jnp.bfloat16)
    part = product_transposed(activated, columns_of(down_ref, start, start + columns))
    step = pl.program_id(0)
    last = pl.num_programs(0) - 1

    @pl.when(step == 0)
    def _():
        total[...] = part

    @pl.when(step > 0)
    def _():
        total[...] += part

    @pl.when(step == last)
    def _():
        finish(total[...], kept_ref, sent_ref)


def feed_part(normed, weights, steps, columns, block, groups):
    tokens, width = normed.shape
    half = (tokens // 2, width)
    return pl.pallas_call(
        functools.partial(feed_kernel, columns),
        grid=(steps,),
        in_specs=[pl.BlockSpec((tokens, width), lambda j: (0, 0))]
        + [weight_spec(weights, block, group) for group in groups],
        out_specs=[pl.BlockSpec(half, lambda j: (0, 0))] * 2,
        out_shape=[
            jax.ShapeDtypeStruct(half, jnp.float32),
            jax.ShapeDtypeStruct(half, jnp.bfloat16),
        ],
        scratch_shapes=[pltpu.VMEM((tokens, width), jnp.float32)],
        compiler_params=pltpu.CompilerParams(vmem_limit_bytes=VMEM_LIMIT),
    )(normed, *[weights] * len(groups))


def line_up_kernel(in_ref, out_ref):
    groups, columns = in_ref.shape[0], out_ref.shape[1] // in_ref.shape[0]
    for group in range(groups):
        at = group * columns
        out_ref[:, at : at + columns] = in_ref[group, :, :columns]


def line_up(weights, width, columns, block):
    chunks, groups, rows, _ = weights.shape
    return pl.pallas_call(
        line_up_kernel,
        grid=(chunks,),
        in_specs=[pl.BlockSpec((None, groups, rows, block), lambda j: (j, 0, 0, 0))],
        out_specs=pl.BlockSpec((rows, groups * columns), lambda j: (j, 0)),
        out_shape=jax.ShapeDtypeStruct((width, groups * columns), weights.dtype),
    )(weights)


def exchange(blocks, axes):
    return lax.all_to_all(blocks, axes, split_axis=0, concat_axis=0, tiled=True)


def spread_out(block, axes):
    count = lax.axis_size(axes)
    return exchange(jnp.broadcast_to(block[None], (count,) + block.shape), axes)


def shift_ring(block, steps):
    places = [0, 2, 1, 3]
    pairs = [(places[i], places[(i + steps) % 4]) for i in range(4)]
    return lax.ppermute(block, RING, pairs)


def swap_cores(block):
    return lax.ppermute(block, "c", [(0, 1), (1, 0)])


def gather_row(normed):
    across = shift_ring(normed, 2)
    return jnp.concatenate([normed, across, swap_cores(normed), swap_cores(across)])


def gather_line(normed, beside=()):
    before = shift_ring(normed, 1)
    after = shift_ring(normed, -1)
    near, beside = lax.optimization_barrier((jnp.concatenate([before, after]), beside))
    return gather_row(normed), jnp.concatenate([near, swap_cores(near)]), beside


def join_cores(partial):
    kept, sent = partial
    return kept + swap_cores(sent).astype(jnp.float32)


def scatter_row(own_frame):
    own, across = jnp.split(join_cores(own_frame), 2)
    return own + shift_ring(across.astype(jnp.bfloat16), 2).astype(jnp.float32)


def scatter_line(own_frame, other_frame):
    before, after = jnp.split(join_cores(other_frame).astype(jnp.bfloat16), 2)
    before, after = shift_ring(before, -1), shift_ring(after, 1)
    return scatter_row(own_frame) + (before.astype(jnp.float32) + after.astype(jnp.float32))


def gather_pair(normed):
    return jnp.concatenate([normed, swap_cores(normed)])


def on_device(
    video,
    modulation,
    query_key_value_weight,
    attention_output_weight,
    feed_forward_up_weight,
    feed_forward_down_weight,
):
    stream = video[0]
    own, width = stream.shape
    head_size = width // HEADS
    depth, _, quarter = query_key_value_weight.shape[1:]
    hidden = feed_forward_up_weight.shape[2]
    output_rows = jnp.swapaxes(attention_output_weight, 1, 2)
    down_rows = jnp.swapaxes(feed_forward_down_weight, 1, 2)

    layers, lines = lax.axis_size("z"), lax.axis_size("y")
    eighth, local = hidden // 2, quarter // 2

    def halves(rows):
        return jnp.swapaxes(rows.reshape(depth, 2, -1), 0, 1)

    feed = jnp.concatenate([halves(feed_forward_up_weight[0]), halves(down_rows[0])], axis=2)
    feed = jnp.broadcast_to(feed[None], (lines,) + feed.shape)
    heads = jnp.concatenate(
        [
            query_key_value_weight[1].reshape(depth, 3, lines, head_size),
            output_rows[1].reshape(depth, 1, lines, head_size),
        ],
        axis=1,
    )
    heads = jnp.transpose(heads, (2, 0, 1, 3)).reshape(lines, 1, depth, -1)
    heads = jnp.broadcast_to(heads, (lines, 2) + heads.shape[2:])
    late = jnp.stack([feed_forward_up_weight[1], down_rows[1]])
    late = jnp.transpose(late.reshape(2, depth, 2, 2, eighth // 2), (0, 3, 2, 1, 4))
    late = late.reshape(lines, 2, depth, -1)
    packs = jnp.concatenate([feed, late, heads], axis=3).reshape(2 * lines, depth, -1)
    packs = exchange(packs, ("y", "xl")).reshape(2 * lines * depth, -1)
    spatial_feed_weight = lax.all_gather(packs[:, :hidden], "z", axis=0, tiled=True)
    spatial_feed_weight = spatial_feed_weight.reshape(1, 1, width, -1)

    first = query_key_value_weight[0].reshape(depth, 3, 2, local)
    first = jnp.transpose(first, (2, 0, 1, 3)).reshape(2, depth, -1)
    first = jnp.concatenate([first, halves(output_rows[0])], axis=2)
    first, packs = lax.optimization_barrier((first, packs))
    first = jnp.broadcast_to(first[None], (layers,) + first.shape)
    first = exchange(first.reshape(2 * layers, depth, -1), ("z", "xl")).reshape(
        2 * layers * depth, -1
    )

    late, heads = packs[:, hidden : hidden + eighth // 2], packs[:, hidden + eighth // 2 :]
    heads = jnp.stack([heads, lax.ppermute(heads, "xh", [(0, 1), (1, 0)])], axis=1)
    heads = jnp.swapaxes(heads.reshape(-1, 2, 4, head_size), 1, 2)
    temporal = jnp.concatenate([late, heads.reshape(late.shape[0], -1)], axis=1)
    temporal, first = lax.optimization_barrier((temporal, first))
    temporal = lax.all_gather(temporal, PLANE, axis=0)
    temporal = temporal.reshape((layers, lines) + temporal.shape[1:])

    first = spread_out(first, ("y",)).reshape(lines, layers, 2 * depth, -1)
    first = jnp.swapaxes(first, 0, 1).reshape(1, 1, width, -1)

    mod = modulation[0]

    def spatial_attention(normed):
        return attention_part(normed, first, local // head_size, head_size, 1, 0)

    def spatial_feed(normed):
        return feed_part(normed, spatial_feed_weight, 1, eighth, hidden, (0,))

    own_frame, other_frame, _ = gather_line(normalize(stream, mod[0], mod[1]))
    other_frame = spatial_attention(other_frame)
    update = scatter_line(spatial_attention(own_frame), other_frame)
    stream = (stream.astype(jnp.float32) + mod[2] * update).astype(jnp.bfloat16)
    own_frame, other_frame, _ = gather_line(normalize(stream, mod[3], mod[4]))
    other_frame = spatial_feed(other_frame)
    update = scatter_line(spatial_feed(own_frame), other_frame)
    stream = (stream.astype(jnp.float32) + mod[5] * update).astype(jnp.bfloat16)

    frames = lax.axis_size(FRAME)
    stream = exchange(stream.reshape(frames, own // frames, width), FRAME).reshape(own, width)
    mod = modulation[1]
    normed = gather_pair(normalize(stream, mod[0], mod[1]))
    start, block = eighth // 2, 3 * 128
    update = join_cores(
        attention_part(normed, temporal, local // head_size, head_size, own // frames, start)
    )
    stream = (stream.astype(jnp.float32) + mod[2] * update).astype(jnp.bfloat16)

    temporal_feed_weight = line_up(temporal, width, start, block).reshape(1, 1, width, -1)

    def temporal_feed(normed):
        return feed_part(normed, temporal_feed_weight, 1, eighth, hidden, (0,))

    own_frame, other_frame, temporal_feed_weight = gather_line(
        normalize(stream, mod[3], mod[4]), temporal_feed_weight
    )
    other_frame = temporal_feed(other_frame)
    update = scatter_line(temporal_feed(own_frame), other_frame)
    stream = (stream.astype(jnp.float32) + mod[5] * update).astype(jnp.bfloat16)
    stream = exchange(stream.reshape(frames, own // frames, width), FRAME)
    return stream.reshape(1, own, width)


def solution(mesh):
    fine = Mesh(mesh.devices.reshape(8, 4, 2, 2, 2), ("z", "y", "xl", "xh", "c"))
    rows = ("xh", "c")
    in_specs = (
        P(FRAME, rows, None),
        P(),
        P(None, FRAME, None, rows),
        P(None, rows, FRAME),
        P(None, FRAME, rows),
        P(None, rows, FRAME),
    )
    out_specs = P(FRAME, rows, None)
    return jax.shard_map(
        on_device, mesh=fine, in_specs=in_specs, out_specs=out_specs, check_vma=False
    )
```
